512 devices in a mesh: region: 16 (over z, core), block: 32 (over x, y).
Axes of the slice: x: 4, y: 8, z: 8, core: 2. Of those that a mesh axis runs over, the one named last changes fastest.
Arguments:
- features: bfloat16 [2048, 64, 512], P(('region', 'block')), may hold values from -6 to 6
- counts: int32 [2048], P(('region', 'block')), may hold values from 0 to 512, as said below
- rebalance: int32 [2048], P(('region', 'block')), may hold values from -1 to 1023, as said below
- neighbors: int32 [2048, 26], P(('region', 'block')), may hold values from -1 to 2047, as said below
- coarse_owner: int32 [2048], P(('region', 'block')), may hold values from -1 to 15, as said below
- conv_weight: bfloat16 [27, 64, 128], replicated, may hold values from -0.15625 to 0.15625
- convolution_bias_vector: float32 [128], replicated, may hold values from -3 to 3
- merged_adjoint: bfloat16 [1024, 8192], P(('region', 'block')), may hold values from -0.119628906 to 0.119628906
Outputs:
- pooled: bfloat16 [1024, 8192], P(('region', 'block'))
- weight_grad: float32 [27, 64, 128], replicated
- bias_grad: float32 [128], replicated
The draws below stay inside these ranges and needn't reach their ends.
Inputs may be any that keep to these rules, and one draw needn't show every extreme that they name: `counts`: 0 marks an empty block; exactly half of each region group's blocks are occupied. `rebalance`: -1 for an empty block; else a row of the block's own region group, each row of a group taken by exactly one block; of the blocks of one device at most 1 have rows on one same device. `neighbors`: -1 where an offset has no occupied neighbour and at every offset of an empty block; neighbours at offsets with ea = 0 lie on the same device, the others on the same device or one of the two beside it along block in the same region group. `coarse_owner`: -1 for an empty block; of the blocks on one device of the working layout at most 1 have the same coarse owner.
All inputs are finite; a program needn't handle non-finite values.
Results may differ from the reference program's by a relative error of at most 0.0029.
Values may be sent and summed in bfloat16 or wider, within the bound.
No kernel may reach another device: no remote copies, remote signals or barrier semaphores. Data moves between devices by JAX's collectives and lax.ppermute only.
A program may use at most 128 MiB of HBM per device.

```python
import math
import jax
import jax.numpy as jnp
from jax import lax

C_IN = 64
C_OUT = 128
TAPS = 27
HOME = 4
WORK = 2
BLOCKS = 2048
ROWS = 1024
N_REGION = 16
N_BLOCK = 32


def layout(key):
    region_count = N_REGION
    device_count = N_BLOCK
    home_slots = HOME
    work_slots = HOME // 2
    group_slots = device_count * home_slots
    subkeys = jax.random.split(key, 7)
    crowded_device = jax.random.randint(subkeys[0], (region_count, 1), 0, device_count)
    device_weight = jax.random.randint(subkeys[1], (region_count, device_count), 1, 5)
    random_noise = jax.random.randint(subkeys[2], (region_count, device_count, home_slots), 0, 1024)
    scores = random_noise * device_weight[:, :, None]
    device_ids = jnp.arange(device_count, dtype=jnp.int32)[None, :, None]
    scores = jnp.where(device_ids == crowded_device[:, :, None], 5000, scores)
    scores = scores.reshape(region_count, group_slots) * group_slots + jnp.arange(group_slots, dtype=jnp.int32)[None, :]
    chosen = jax.lax.top_k(scores, device_count * work_slots)[1]
    group_ids = jnp.arange(region_count, dtype=jnp.int32)[:, None]
    occupied = jnp.zeros((region_count, group_slots), jnp.int32).at[group_ids, chosen].set(1)
    ranking = jnp.maximum(jnp.cumsum(occupied, axis=1) - 1, 0)
    shuffles = jax.vmap(lambda subkey: jax.random.permutation(subkey, device_count))(jax.random.split(subkeys[3], region_count))
    dest_device = jnp.take_along_axis(shuffles, ranking % device_count, axis=1)
    dest_slot = ranking // device_count
    rebalance = jnp.where(occupied == 1, (group_ids * device_count + dest_device) * work_slots + dest_slot, -1)
    raw_counts = jnp.minimum(jax.random.randint(subkeys[4], (region_count, group_slots), 1, 700), 512)
    counts = jnp.where(occupied == 1, raw_counts, 0)
    position_of = jax.vmap(lambda subkey: jax.random.permutation(subkey, home_slots))(jax.random.split(subkeys[5], region_count * device_count)).reshape(region_count, device_count, home_slots)
    slot_of = jnp.argsort(position_of, axis=2)
    x_layers = home_slots // 4
    x_local = position_of // 4
    y_coord = position_of // 2 % 2
    z_coord = position_of % 2
    x_global = device_ids * x_layers + x_local
    occupied_cube = occupied.reshape(region_count, device_count, home_slots)
    group_cube = jnp.arange(region_count, dtype=jnp.int32)[:, None, None]
    entries = []
    for delta_x in (-1, 0, 1):
        for delta_y in (-1, 0, 1):
            for delta_z in (-1, 0, 1):
                if delta_x == 0 and delta_y == 0 and (delta_z == 0):
                    continue
                next_x = x_global + delta_x
                next_y = y_coord + delta_y
                next_z = z_coord + delta_z
                within = (next_x >= 0) & (next_x < device_count * x_layers) & (next_y >= 0) & (next_y < 2) & (next_z >= 0) & (next_z < 2)
                clipped_x = jnp.clip(next_x, 0, device_count * x_layers - 1)
                next_device = clipped_x // x_layers
                next_position = clipped_x % x_layers * 4 + jnp.clip(next_y, 0, 1) * 2 + jnp.clip(next_z, 0, 1)
                next_slot = slot_of[group_cube, next_device, next_position]
                usable = within & (occupied_cube == 1) & (occupied_cube[group_cube, next_device, next_slot] == 1)
                global_index = (group_cube * device_count + next_device) * home_slots + next_slot
                entries.append(jnp.where(usable, global_index, -1))
    neighbors = jnp.stack(entries, axis=-1).reshape(region_count * group_slots, 26)
    twisting = jax.vmap(lambda subkey: jax.random.permutation(subkey, region_count))(jax.random.split(subkeys[6], device_count))
    coarse = jnp.where(occupied == 1, (group_ids + twisting[dest_device, dest_slot % region_count]) % region_count, -1)
    return (counts.reshape(-1).astype(jnp.int32), rebalance.reshape(-1).astype(jnp.int32), neighbors.astype(jnp.int32), coarse.reshape(-1).astype(jnp.int32))


def draw_counts(key, part):
    return layout(key)[0]


def draw_rebalance(key, part):
    return layout(key)[1]


def draw_neighbors(key, part):
    return layout(key)[2]


def draw_coarse_owner(key, part):
    return layout(key)[3]


def level_of(stream_key, shape, shards, low, high):
    def one(axis_at, shards_of):
        draws = jax.random.uniform(jax.random.fold_in(jax.random.fold_in(stream_key, 6), axis_at), (shards_of,), jnp.float32, low / len(shards), high / len(shards))
        return jnp.repeat(jnp.exp(draws), shape[axis_at] // shards_of).reshape((-1,) + (1,) * (len(shape) - axis_at - 1))

    gain = one(*shards[0])
    for cut in shards[1:]:
        gain = gain * one(*cut)
    return gain


def gaussian(key, shape, width, bound, shards=(), kind=jnp.bfloat16):
    loudness = level_of(key, shape, shards, -0.22, 0.18) if shards else 1.0
    result = jax.random.normal(key, shape, jnp.float32) * width * loudness
    return jnp.minimum(jnp.maximum(result, -bound), bound).astype(kind)


def setup_inputs(seed: int = 0) -> dict:
    seeds = jax.random.split(jax.random.key(seed), 9)
    return {
        "features": gaussian(seeds[0], (BLOCKS, C_IN, 512), 1.0, 6.0, ((0, 512),)),
        "counts": draw_counts(jax.random.fold_in(seeds[8], 71), 0),
        "rebalance": draw_rebalance(jax.random.fold_in(seeds[8], 71), 0),
        "neighbors": draw_neighbors(jax.random.fold_in(seeds[8], 71), 0),
        "coarse_owner": draw_coarse_owner(jax.random.fold_in(seeds[8], 71), 0),
        "conv_weight": gaussian(seeds[5], (TAPS, C_IN, C_OUT), (TAPS * C_IN) ** -0.5, 0.15625),
        "convolution_bias_vector": gaussian(seeds[6], (C_OUT,), 0.5, 3.0, (), jnp.float32),
        "merged_adjoint": gaussian(seeds[7], (ROWS, C_OUT * 64), 0.02, 0.119628906, ((0, 512),)),
    }


def filled_fraction(block_counts):
    hashed = (jnp.arange(512, dtype=jnp.int32) * 167) % 512
    return hashed[None, :] < block_counts[:, None]


def offset_list():
    return [(ea, eb, ec) for ea in (-1, 0, 1) for eb in (-1, 0, 1) for ec in (-1, 0, 1) if (ea, eb, ec) != (0, 0, 0)]


def source_range(step):
    return (7, 8) if step < 0 else ((0, 1) if step > 0 else (0, 8))


def target_range(step):
    return (0, 1) if step < 0 else ((9, 10) if step > 0 else (1, 9))


def source_piece(cube_view, offset):
    rows_now, channels = cube_view.shape[0], cube_view.shape[1]
    a_low, a_high = source_range(offset[0])
    b_low, b_high = source_range(offset[1])
    c_low, c_high = source_range(offset[2])
    piece = cube_view[:, :, a_low:a_high, b_low:b_high, c_low:c_high]
    return piece.reshape(rows_now, channels, -1)


def padded_cube(blocks_in, shell_in):
    rows_now, channels = blocks_in.shape[0], blocks_in.shape[1]
    cube = jnp.zeros((rows_now, channels, 10, 10, 10), blocks_in.dtype)
    cube = cube.at[:, :, 1:9, 1:9, 1:9].set(blocks_in.reshape(rows_now, channels, 8, 8, 8))
    pointer = 0
    for offset in offset_list():
        a_low, a_high = target_range(offset[0])
        b_low, b_high = target_range(offset[1])
        c_low, c_high = target_range(offset[2])
        extent = (a_high - a_low) * (b_high - b_low) * (c_high - c_low)
        piece = shell_in[:, :, pointer:pointer + extent].reshape(rows_now, channels, a_high - a_low, b_high - b_low, c_high - c_low)
        cube = cube.at[:, :, a_low:a_high, b_low:b_high, c_low:c_high].set(piece)
        pointer = pointer + extent
    return cube


def taps(blocks_in, shell_in):
    rows_now, channels = blocks_in.shape[0], blocks_in.shape[1]
    cube = padded_cube(blocks_in, shell_in)
    pieces = []
    for ea in (-1, 0, 1):
        for eb in (-1, 0, 1):
            for ec in (-1, 0, 1):
                window = cube[:, :, 1 + ea:9 + ea, 1 + eb:9 + eb, 1 + ec:9 + ec]
                pieces.append(window.reshape(rows_now, channels, 512))
    return jnp.concatenate(pieces, axis=1)


def pool_table():
    voxels = jnp.arange(512, dtype=jnp.int32)
    cell_index = ((voxels // 128) * 4 + (voxels // 16) % 4) * 4 + (voxels % 8) // 2
    return jnp.where(cell_index[:, None] == jnp.arange(64, dtype=jnp.int32)[None, :], 0.125, 0.0).astype(jnp.float32)


def reference(features, counts, rebalance, neighbors, coarse_owner, conv_weight, convolution_bias_vector, merged_adjoint):
    block_total = features.shape[0]
    channels = features.shape[1]
    result_feature_count = convolution_bias_vector.shape[0]
    tap_count = conv_weight.shape[0]
    row_total = block_total // 2
    occupied_mask = filled_fraction(counts)
    masked = jnp.where(occupied_mask[:, None, :], features, jnp.zeros_like(features))
    masked_cube = masked.reshape(block_total, channels, 8, 8, 8)
    present = neighbors >= 0
    safe_index = jnp.where(present, neighbors, 0)
    shell_parts = []
    for column, offset in enumerate(offset_list()):
        piece = jnp.take(source_piece(masked_cube, offset), safe_index[:, column], axis=0)
        shell_parts.append(jnp.where(present[:, column][:, None, None], piece, jnp.zeros_like(piece)))
    shells = jnp.concatenate(shell_parts, axis=2)
    source = jnp.zeros((row_total,), jnp.int32).at[jnp.where(rebalance >= 0, rebalance, row_total)].set(
        jnp.arange(block_total, dtype=jnp.int32), mode="drop")
    row_ids = jnp.arange(row_total, dtype=jnp.int32)
    owner_device = (row_ids // WORK) % N_BLOCK
    owner_slot = row_ids % WORK
    receiving_line = (jnp.take(coarse_owner, source) * N_BLOCK + owner_device) * WORK + owner_slot
    flattened_weight = conv_weight.reshape(tap_count * channels, result_feature_count).astype(jnp.float32)
    table = pool_table()
    sample_number = math.gcd(row_total, 32)

    def forward(lookup):
        stacked_layers = taps(masked[lookup], shells[lookup])
        before_activation = jnp.einsum("esh,sb->ebh", stacked_layers.astype(jnp.float32), flattened_weight) + convolution_bias_vector[None, :, None]
        activation = jnp.where(filled_fraction(counts[lookup])[:, None, :], jax.nn.silu(before_activation), 0.0)
        pooled_part = jnp.einsum("ncv,vp->ncp", activation, table, precision=lax.Precision.HIGHEST)
        return pooled_part.reshape(sample_number, result_feature_count * 64).astype(jnp.bfloat16)

    pooled_work = lax.map(forward, source.reshape(-1, sample_number)).reshape(row_total, result_feature_count * 64)
    pooled = jnp.zeros_like(pooled_work).at[receiving_line].set(pooled_work)
    derivative_of_evened_tiles = jnp.take(merged_adjoint, receiving_line, axis=0)

    def backward(running, component):
        lookup, part_grad = component
        stacked_layers = taps(masked[lookup], shells[lookup])
        before_activation = jnp.einsum("esh,sb->ebh", stacked_layers.astype(jnp.float32), flattened_weight) + convolution_bias_vector[None, :, None]
        mask_view = filled_fraction(counts[lookup])[:, None, :]
        spread_grad = jnp.einsum("ncp,vp->ncv", part_grad.reshape(sample_number, result_feature_count, 64).astype(jnp.float32),
                                 table, precision=lax.Precision.HIGHEST)
        sigmoid_value = jax.nn.sigmoid(before_activation)
        grad_pre = jnp.where(mask_view, spread_grad * sigmoid_value * (1.0 + before_activation * (1.0 - sigmoid_value)), 0.0)
        gradient_lower_bits = grad_pre.astype(jnp.bfloat16)
        partial_weight = jnp.einsum("sez,stz->et", stacked_layers.astype(jnp.float32), gradient_lower_bits.astype(jnp.float32))
        return (running[0] + partial_weight, running[1] + jnp.sum(grad_pre, axis=(0, 2))), None

    start_state = (jnp.zeros((tap_count * channels, result_feature_count), jnp.float32), jnp.zeros((result_feature_count,), jnp.float32))
    totals, _ = lax.scan(backward, start_state, (source.reshape(-1, sample_number),
                                                 derivative_of_evened_tiles.reshape(-1, sample_number, result_feature_count * 64)))
    return pooled, totals[0].reshape(tap_count, channels, result_feature_count), totals[1]
```

```python
import functools

import jax
import jax.numpy as jnp
from jax import lax
from jax.experimental import pallas as pl
from jax.experimental.pallas import tpu as pltpu
from jax.sharding import PartitionSpec as P

SLOTS = 4
CH = 64
OUT = 128
VOX = 512
FRAME = 768
EDGES = ((-1, -1), (-1, 0), (-1, 1), (0, -1), (0, 0), (0, 1), (1, -1), (1, 0), (1, 1))


def voxel_mask(count):
    lanes = lax.broadcasted_iota(jnp.int32, (1, VOX), 1)
    return ((lanes * 167) & 511) < count


def layer_pair(block):
    lanes = lax.broadcasted_iota(jnp.int32, (CH, 128), 1)
    return jnp.where(lanes < 64, block[:, :128], block[:, VOX - 128 :])


def layers_kernel(counts_ref, features_ref, layers_ref):
    for slot in range(SLOTS):
        block = features_ref[slot].astype(jnp.float32)
        block = jnp.where(voxel_mask(counts_ref[slot]), block, 0.0)
        layers_ref[slot] = layer_pair(block).astype(jnp.bfloat16)


def column_of(ea, eb, ec):
    tap = 9 * (ea + 1) + 3 * (eb + 1) + (ec + 1)
    return tap if tap < 13 else tap - 1


def pool_table(rows_are_voxels):
    shape = (VOX, 64) if rows_are_voxels else (64, VOX)
    voxel = lax.broadcasted_iota(jnp.int32, shape, 0 if rows_are_voxels else 1)
    cell = lax.broadcasted_iota(jnp.int32, shape, 1 if rows_are_voxels else 0)
    index = ((voxel >> 7) << 4) | (((voxel >> 4) & 3) << 2) | ((voxel & 7) >> 1)
    return jnp.where(index == cell, 0.125, 0.0).astype(jnp.bfloat16)


def pick_rows(odd, transposed):
    shape = (OUT, 64) if transposed else (64, OUT)
    channel = lax.broadcasted_iota(jnp.int32, shape, 0 if transposed else 1)
    row = lax.broadcasted_iota(jnp.int32, shape, 1 if transposed else 0)
    return jnp.where(channel == 2 * row + odd, 1.0, 0.0).astype(jnp.bfloat16)


def dot(a, b):
    return jnp.dot(a, b, preferred_element_type=jnp.float32)


def forward_kernel(
    counts_ref,
    neighbors_ref,
    features_ref,
    layers_ref,
    before_ref,
    after_ref,
    weight_ref,
    bias_ref,
    pooled_ref,
    stacked_ref,
    slope_ref,
    blocks_ref,
    rims_ref,
):
    slot = pl.program_id(0)
    first = (lax.axis_index("region") * lax.axis_size("block") + lax.axis_index("block")) * SLOTS

    @pl.when(slot == 0)
    def _():
        for index in range(SLOTS):
            block = features_ref[index].astype(jnp.float32)
            blocks_ref[index] = jnp.where(voxel_mask(counts_ref[index]), block, 0.0)
            rims_ref[index] = before_ref[index].astype(jnp.float32)
            rims_ref[SLOTS + index] = layers_ref[index].astype(jnp.float32)
            rims_ref[2 * SLOTS + index] = after_ref[index].astype(jnp.float32)
        blocks_ref[SLOTS] = jnp.zeros((CH, VOX), jnp.float32)
        rims_ref[3 * SLOTS] = jnp.zeros((CH, 128), jnp.float32)

    def rim(ea, eb, ec):
        target = neighbors_ref[slot, column_of(ea, eb, ec)]
        place = jnp.clip(target - (first - SLOTS), 0, 3 * SLOTS - 1)
        return rims_ref[jnp.where(target >= 0, place, 3 * SLOTS)]

    def inner(eb, ec):
        if eb == 0 and ec == 0:
            return blocks_ref[slot]
        target = neighbors_ref[slot, column_of(0, eb, ec)]
        place = jnp.clip(target - first, 0, SLOTS - 1)
        return blocks_ref[jnp.where(target >= 0, place, SLOTS)]

    def frame(eb, ec):
        return jnp.concatenate([rim(-1, eb, ec), inner(eb, ec), rim(1, eb, ec)], axis=1)

    lanes = lax.broadcasted_iota(jnp.int32, (CH, FRAME), 1)
    at_c = lanes & 7
    at_b = (lanes >> 3) & 7

    def moved(array, steps):
        return pltpu.roll(array, (-steps) % FRAME, 1)

    along_c = {}
    for eb in (-1, 0, 1):
        middle = frame(eb, 0)
        along_c[eb, 0] = middle
        along_c[eb, -1] = jnp.where(at_c == 0, moved(frame(eb, -1), 7), moved(middle, -1))
        along_c[eb, 1] = jnp.where(at_c == 7, moved(frame(eb, 1), -7), moved(middle, 1))
    for index, (eb, ec) in enumerate(EDGES):
        if eb == 0:
            value = along_c[0, ec]
        elif eb < 0:
            value = jnp.where(at_b == 0, moved(along_c[-1, ec], 56), moved(along_c[0, ec], -8))
        else:
            value = jnp.where(at_b == 7, moved(along_c[1, ec], -56), moved(along_c[0, ec], 8))
        stacked_ref[0, index * CH : (index + 1) * CH, :] = value.astype(jnp.bfloat16)

    product = dot(weight_ref[...], stacked_ref[0])
    sides = product[:OUT, : FRAME - 128] + product[2 * OUT :, 128:]
    sides = pltpu.roll(sides, FRAME - 128 - 64, 1)[:, :VOX]
    preact = product[OUT : 2 * OUT, 128 : 128 + VOX] + sides + bias_ref[...]
    mask = voxel_mask(counts_ref[slot])
    sigmoid = jax.nn.sigmoid(preact)
    slope = sigmoid * (1.0 + preact * (1.0 - sigmoid))
    slope_ref[0] = jnp.where(mask, slope, 0.0)
    activation = jnp.where(mask, preact * sigmoid, 0.0)
    high = activation.astype(jnp.bfloat16)
    low = (activation - high.astype(jnp.float32)).astype(jnp.bfloat16)
    table = pool_table(True)
    pooled = (dot(high, table) + dot(low, table)).astype(jnp.bfloat16)
    even = dot(pick_rows(0, False), pooled)
    odd = dot(pick_rows(1, False), pooled)
    pooled_ref[0] = jnp.concatenate([even, odd], axis=1).astype(jnp.bfloat16)


def backward_kernel(rows_ref, filled_ref, row_ref, stacked_ref, slope_ref, weight_grad_ref, bias_grad_ref):
    slot = pl.program_id(0)

    @pl.when(slot == 0)
    def _():
        weight_grad_ref[...] = jnp.zeros_like(weight_grad_ref)
        bias_grad_ref[...] = jnp.zeros_like(bias_grad_ref)

    @pl.when(filled_ref[slot] > 0)
    def _():
        row = row_ref[0]
        cells = dot(pick_rows(0, True), row[:, :64]) + dot(pick_rows(1, True), row[:, 64:])
        spread = dot(cells.astype(jnp.bfloat16), pool_table(False))
        grad = spread * slope_ref[0]
        bias_grad_ref[...] += jnp.sum(grad, axis=1, keepdims=True)
        grad = grad.astype(jnp.bfloat16).astype(jnp.float32)
        wide = jnp.concatenate([grad, jnp.zeros((OUT, 128), jnp.float32)], axis=1)
        shifted = pltpu.roll(wide, 64, 1).astype(jnp.bfloat16)
        grad = grad.astype(jnp.bfloat16)

        def outer(start, width, value):
            return lax.dot_general(
                stacked_ref[0, :, start : start + width],
                value,
                (((1,), (1,)), ((), ())),
                preferred_element_type=jnp.float32,
            )

        weight_grad_ref[0] += outer(0, FRAME - 128, shifted)
        weight_grad_ref[1] += outer(128, VOX, grad)
        weight_grad_ref[2] += outer(128, FRAME - 128, shifted)


VMEM = pltpu.VMEM


def make_layers(counts, features):
    return pl.pallas_call(
        layers_kernel,
        out_shape=jax.ShapeDtypeStruct((SLOTS, CH, 128), jnp.bfloat16),
        in_specs=[pl.BlockSpec(memory_space=pltpu.SMEM), pl.BlockSpec(memory_space=VMEM)],
        out_specs=pl.BlockSpec(memory_space=VMEM),
        name="layers",
    )(counts, features)


def forward(counts, neighbors, features, layers, before, after, weight, bias):
    def whole(shape):
        return pl.BlockSpec(shape, lambda i, *_: (0,) * len(shape))

    def per_slot(shape):
        return pl.BlockSpec((1,) + shape, lambda i, *_: (i, 0, 0))

    return pl.pallas_call(
        forward_kernel,
        grid_spec=pltpu.PrefetchScalarGridSpec(
            num_scalar_prefetch=2,
            grid=(SLOTS,),
            in_specs=[
                whole((SLOTS, CH, VOX)),
                whole((SLOTS, CH, 128)),
                whole((SLOTS, CH, 128)),
                whole((SLOTS, CH, 128)),
                whole((3 * OUT, 9 * CH)),
                whole((OUT, 1)),
            ],
            out_specs=[
                per_slot((CH, 128)),
                per_slot((9 * CH, FRAME)),
                per_slot((OUT, VOX)),
            ],
            scratch_shapes=[
                pltpu.VMEM((SLOTS + 1, CH, VOX), jnp.float32),
                pltpu.VMEM((3 * SLOTS + 1, CH, 128), jnp.float32),
            ],
        ),
        out_shape=[
            jax.ShapeDtypeStruct((SLOTS, CH, 128), jnp.bfloat16),
            jax.ShapeDtypeStruct((SLOTS, 9 * CH, FRAME), jnp.bfloat16),
            jax.ShapeDtypeStruct((SLOTS, OUT, VOX), jnp.float32),
        ],
        compiler_params=pltpu.CompilerParams(vmem_limit_bytes=32 * 1024 * 1024),
        cost_estimate=pl.CostEstimate(flops=3_500_000_000, bytes_accessed=6_000_000, transcendentals=300_000),
        name="forward",
    )(counts, neighbors, features, layers, before, after, weight, bias)


def backward(lines, filled, rows, stacked, slope):
    def per_slot(shape):
        return pl.BlockSpec((1,) + shape, lambda i, *_: (i, 0, 0))

    return pl.pallas_call(
        backward_kernel,
        grid_spec=pltpu.PrefetchScalarGridSpec(
            num_scalar_prefetch=2,
            grid=(SLOTS,),
            in_specs=[
                pl.BlockSpec((1, CH, 128), lambda i, lines_ref, filled_ref: (lines_ref[i], 0, 0)),
                per_slot((9 * CH, FRAME)),
                per_slot((OUT, VOX)),
            ],
            out_specs=[
                pl.BlockSpec((3, 9 * CH, OUT), lambda i, *_: (0, 0, 0)),
                pl.BlockSpec((OUT, 1), lambda i, *_: (0, 0)),
            ],
        ),
        out_shape=[
            jax.ShapeDtypeStruct((3, 9 * CH, OUT), jnp.float32),
            jax.ShapeDtypeStruct((OUT, 1), jnp.float32),
        ],
        compiler_params=pltpu.CompilerParams(vmem_limit_bytes=32 * 1024 * 1024),
        cost_estimate=pl.CostEstimate(flops=3_500_000_000, bytes_accessed=6_000_000, transcendentals=0),
        name="backward",
    )(lines, filled, rows, stacked, slope)


def per_device(
    features,
    counts,
    rebalance,
    neighbors,
    coarse_owner,
    conv_weight,
    convolution_bias_vector,
    merged_adjoint,
):
    block_count = lax.axis_size("block")
    region_count = lax.axis_size("region")
    me_block = lax.axis_index("block")
    group_rows = 2 * block_count
    occupied = rebalance >= 0
    line = jnp.where(occupied, rebalance % group_rows, 0)

    tags = jnp.where(occupied, line * region_count + coarse_owner, -1)
    all_tags = lax.all_gather(tags, "block", tiled=True)
    wanted = 2 * me_block + jnp.arange(2, dtype=jnp.int32)
    match = (all_tags[None, :] >= 0) & (all_tags[None, :] // region_count == wanted[:, None])
    owner = jnp.sum(jnp.where(match, all_tags[None, :] % region_count, 0), axis=1)

    adjoint = merged_adjoint.reshape(2, CH, 128)
    adjoint_region = lax.all_gather(adjoint, "region", tiled=True)
    work_cot = jnp.take(adjoint_region, owner * 2 + jnp.arange(2, dtype=jnp.int32), axis=0)
    group_cot = lax.all_gather(work_cot, "block", tiled=True)

    layers = make_layers(counts, features)
    up = [(i, i + 1) for i in range(block_count - 1)]
    down = [(i + 1, i) for i in range(block_count - 1)]
    before = lax.ppermute(layers, "block", up)
    after = lax.ppermute(layers, "block", down)

    weight = conv_weight.reshape(3, 9 * CH, OUT).transpose(0, 2, 1).reshape(3 * OUT, 9 * CH)
    pooled_rows, stacked, slope = forward(
        counts, neighbors, features, layers, before, after, weight, convolution_bias_vector[:, None]
    )

    placed = (line[None, :] == jnp.arange(group_rows, dtype=jnp.int32)[:, None]) & occupied[None, :]
    send = jnp.zeros((group_rows, CH, 128), jnp.bfloat16)
    for slot in range(SLOTS):
        send = jnp.where(placed[:, slot][:, None, None], pooled_rows[slot][None], send)
    work_pooled = lax.psum_scatter(send, "block", scatter_dimension=0, tiled=True)
    to_owner = owner[None, :] == jnp.arange(region_count, dtype=jnp.int32)[:, None]
    send = jnp.where(to_owner[:, :, None, None], work_pooled[None], jnp.zeros((), jnp.bfloat16))
    pooled = lax.psum_scatter(
        send.reshape(region_count * 2, CH, 128), "region", scatter_dimension=0, tiled=True
    )

    weight_grad, bias_grad = backward(line, occupied.astype(jnp.int32), group_cot, stacked, slope)
    weight_total, bias_total = lax.psum(
        (weight_grad.reshape(27, CH, OUT), bias_grad.reshape(OUT)), ("region", "block")
    )
    return pooled.reshape(2, CH * 128), weight_total, bias_total


def solution(mesh):
    in_specs = (
        P(("region", "block"), None, None),
        P(("region", "block")),
        P(("region", "block")),
        P(("region", "block"), None),
        P(("region", "block")),
        P(),
        P(),
        P(("region", "block"), None),
    )
    out_specs = (P(("region", "block"), None), P(), P())
    return jax.shard_map(
        per_device, mesh=mesh, in_specs=in_specs, out_specs=out_specs, check_vma=False
    )
```

```python
import jax
import jax.numpy as jnp
from jax import lax
from jax.experimental import pallas as pl
from jax.experimental.pallas import tpu as pltpu
from jax.sharding import Mesh
from jax.sharding import PartitionSpec as P

SLOTS = 4
CH = 64
OUT = 128
VOX = 512
FRAME = 768
TAP_ROWS = 1728
BLOCK = 32
CHIPS = 256
HALF = TAP_ROWS // 2
EXTRA = HALF - 3 * CHIPS
EDGES = ((-1, -1), (-1, 0), (-1, 1), (0, -1), (0, 0), (0, 1), (1, -1), (1, 0), (1, 1))
VMEM = pltpu.VMEM
SMEM = pltpu.SMEM


def voxel_mask(count):
    lanes = lax.broadcasted_iota(jnp.int32, (1, VOX), 1)
    return ((lanes * 167) & 511) < count


def layer_pair(block):
    lanes = lax.broadcasted_iota(jnp.int32, (CH, 128), 1)
    return jnp.where(lanes < 64, block[:, :128], block[:, VOX - 128 :])


def column_of(ea, eb, ec):
    tap = 9 * (ea + 1) + 3 * (eb + 1) + (ec + 1)
    return tap if tap < 13 else tap - 1


def dot(a, b):
    return jnp.dot(a, b, preferred_element_type=jnp.float32)


def dot_lanes(a, b):
    return lax.dot_general(a, b, (((1,), (1,)), ((), ())), preferred_element_type=jnp.float32)


def grid_of(shape):
    return lax.broadcasted_iota(jnp.int32, shape, 0), lax.broadcasted_iota(jnp.int32, shape, 1)


def onehot(shape, chosen):
    return jnp.where(chosen(*grid_of(shape)), 1.0, 0.0).astype(jnp.bfloat16)


def bf16(array):
    return array.astype(jnp.bfloat16)


def cell_table(slot, voxels_first):
    shape = (VOX, 256) if voxels_first else (256, VOX)
    rows, columns = grid_of(shape)
    voxel, column = (rows, columns) if voxels_first else (columns, rows)
    index = ((voxel >> 7) << 4) | (((voxel >> 4) & 3) << 2) | ((voxel & 7) >> 1)
    wanted = jnp.where(((column >> 5) & 3) == slot, ((column >> 7) << 5) | (column & 31), -1)
    return bf16(jnp.where(index == wanted, 0.125, 0.0))


def layers_kernel(counts_ref, features_ref, layers_ref):
    for slot in range(SLOTS):
        block = features_ref[slot].astype(jnp.float32)
        block = jnp.where(voxel_mask(counts_ref[slot]), block, 0.0)
        layers_ref[slot] = bf16(layer_pair(block))


def offer_kernel(line_ref, owner_ref, adjoint_ref, message_ref):
    message = jnp.zeros((2 * CHIPS, 128), jnp.float32)
    rows, lanes = grid_of((2 * CHIPS, 128))
    keep = (lanes >> 5) == ((rows >> 1) & 3)
    for s in range(2):
        spread = dot(
            onehot((2 * CHIPS, 64), lambda r, c: ((r >> 3) == c) & ((r & 1) == s)),
            adjoint_ref[s * 64 : (s + 1) * 64, :],
        )
        message += jnp.where(keep, spread, 0.0)
    folded = dot(bf16(message), onehot((128, 128), lambda r, c: ((r & 31) == c) & (c < 32)))
    tags = jnp.zeros((1, 128), jnp.float32)
    lane = lax.broadcasted_iota(jnp.int32, (1, 128), 1)
    for slot in range(SLOTS):
        tags = jnp.where(lane == 64 + slot, line_ref[slot].astype(jnp.float32), tags)
        tags = jnp.where(lane == 68 + slot, owner_ref[slot].astype(jnp.float32), tags)
    message_ref[...] = bf16(folded + tags)


def forward_kernel(
    counts_ref,
    neighbors_ref,
    features_ref,
    layers_ref,
    before_ref,
    after_ref,
    weight_ref,
    bias_ref,
    pooled_ref,
    stacked_ref,
    slope_ref,
    blocks_ref,
    rims_ref,
    cells_ref,
):
    slot = pl.program_id(0)
    first = ((lax.axis_index("z") * 2 + lax.axis_index("c")) * BLOCK + lax.axis_index("b")) * SLOTS

    @pl.when(slot == 0)
    def _():
        for index in range(SLOTS):
            block = features_ref[index].astype(jnp.float32)
            blocks_ref[index] = jnp.where(voxel_mask(counts_ref[index]), block, 0.0)
            rims_ref[index] = before_ref[index].astype(jnp.float32)
            rims_ref[SLOTS + index] = layers_ref[index].astype(jnp.float32)
            rims_ref[2 * SLOTS + index] = after_ref[index].astype(jnp.float32)
        blocks_ref[SLOTS] = jnp.zeros((CH, VOX), jnp.float32)
        rims_ref[3 * SLOTS] = jnp.zeros((CH, 128), jnp.float32)
        cells_ref[...] = jnp.zeros_like(cells_ref)

    def rim(ea, eb, ec):
        target = neighbors_ref[slot, column_of(ea, eb, ec)]
        place = jnp.clip(target - (first - SLOTS), 0, 3 * SLOTS - 1)
        return rims_ref[jnp.where(target >= 0, place, 3 * SLOTS)]

    def inner(eb, ec):
        if eb == 0 and ec == 0:
            return blocks_ref[slot]
        target = neighbors_ref[slot, column_of(0, eb, ec)]
        place = jnp.clip(target - first, 0, SLOTS - 1)
        return blocks_ref[jnp.where(target >= 0, place, SLOTS)]

    def frame(eb, ec):
        return jnp.concatenate([rim(-1, eb, ec), inner(eb, ec), rim(1, eb, ec)], axis=1)

    lanes = lax.broadcasted_iota(jnp.int32, (CH, FRAME), 1)
    at_c = lanes & 7
    at_b = (lanes >> 3) & 7

    def moved(array, steps):
        return pltpu.roll(array, (-steps) % FRAME, 1)

    along_c = {}
    for eb in (-1, 0, 1):
        middle = frame(eb, 0)
        along_c[eb, 0] = middle
        along_c[eb, -1] = jnp.where(at_c == 0, moved(frame(eb, -1), 7), moved(middle, -1))
        along_c[eb, 1] = jnp.where(at_c == 7, moved(frame(eb, 1), -7), moved(middle, 1))
    for index, (eb, ec) in enumerate(EDGES):
        if eb == 0:
            value = along_c[0, ec]
        elif eb < 0:
            value = jnp.where(at_b == 0, moved(along_c[-1, ec], 56), moved(along_c[0, ec], -8))
        else:
            value = jnp.where(at_b == 7, moved(along_c[1, ec], -56), moved(along_c[0, ec], 8))
        stacked_ref[0, index * CH : (index + 1) * CH, :] = value.astype(jnp.bfloat16)

    product = dot(weight_ref[...], stacked_ref[0])
    sides = product[:OUT, : FRAME - 128] + product[2 * OUT :, 128:]
    sides = pltpu.roll(sides, FRAME - 128 - 64, 1)[:, :VOX]
    preact = product[OUT : 2 * OUT, 128 : 128 + VOX] + sides + bias_ref[...]
    mask = voxel_mask(counts_ref[slot])
    sigmoid = jax.nn.sigmoid(preact)
    slope = sigmoid * (1.0 + preact * (1.0 - sigmoid))
    slope_ref[0] = jnp.where(mask, slope, 0.0)
    activation = jnp.where(mask, preact * sigmoid, 0.0)
    high = activation.astype(jnp.bfloat16)
    low = (activation - high.astype(jnp.float32)).astype(jnp.bfloat16)
    table = cell_table(slot, True)
    cells_ref[...] += dot(high, table) + dot(low, table)

    @pl.when(slot == SLOTS - 1)
    def _():
        cells = cells_ref[...].astype(jnp.bfloat16)
        even = onehot((CHIPS, OUT), lambda r, c: r == 2 * c)
        odd = onehot((CHIPS, OUT), lambda r, c: r == 2 * c + 1)
        pooled = dot(even, cells[:, :128]) + dot(odd, cells[:, 128:])
        pooled_ref[...] = pooled.astype(jnp.bfloat16)


def choose_kernel(offers_ref, pooled_ref, message_ref, tags_ref):
    core = lax.axis_index("c")
    even = onehot((CHIPS, 2 * CHIPS), lambda r, c: c == 2 * r)
    for half in range(2):
        tags = dot(even, offers_ref[half * 2 * CHIPS : (half + 1) * 2 * CHIPS, :])
        tags_ref[half * CHIPS : (half + 1) * CHIPS, :] = bf16(tags)
    tags = dot(even, offers_ref[pl.ds(core * 2 * CHIPS, 2 * CHIPS), :]).astype(jnp.int32)
    lanes = lax.broadcasted_iota(jnp.int32, (CHIPS, 4 * CHIPS), 1)
    cotangent = jnp.zeros((CHIPS, 128), jnp.float32)
    for slot in range(SLOTS):
        line = tags[:, 64 + slot : 65 + slot]
        owner = tags[:, 68 + slot : 69 + slot]
        source = ((owner & 1) * CHIPS + (owner >> 1) * BLOCK + ((line - 1) >> 1)) * 2 + ((line - 1) & 1)
        source = jnp.where(line > 0, source, -1)
        picked = dot(bf16(jnp.where(lanes == source, 1.0, 0.0)), offers_ref[...])
        cotangent += dot(bf16(picked), onehot((128, 128), lambda r, c: (r + 32 * slot == c) & (r < 32)))
    message = dot(onehot((2 * CHIPS, CHIPS), lambda r, c: r == 2 * c), bf16(cotangent))
    message += dot(onehot((2 * CHIPS, CHIPS), lambda r, c: r == 2 * c + 1), pooled_ref[...])
    message_ref[...] = bf16(message)


def backward_kernel(
    pieces_ref,
    stacked_ref,
    slope_ref,
    mine_ref,
    other_ref,
    pooled_ref,
    cells_ref,
    total_ref,
    bias_ref,
):
    slot = pl.program_id(0)

    @pl.when(slot == 0)
    def _():
        low = dot(onehot((OUT, 2 * CHIPS), lambda r, c: c == 4 * r), pieces_ref[...])
        high = dot(onehot((OUT, 2 * CHIPS), lambda r, c: c == 4 * r + 2), pieces_ref[...])
        cells_ref[...] = bf16(jnp.concatenate([low, high], axis=1))
        pooled = dot(onehot((CHIPS, 2 * CHIPS), lambda r, c: c == 2 * r + 1), pieces_ref[...])
        pooled_ref[...] = bf16(pooled)
        total_ref[...] = jnp.zeros_like(total_ref)
        bias_ref[...] = jnp.zeros_like(bias_ref)

    grad = dot(cells_ref[...], cell_table(slot, False)) * slope_ref[0]
    rounded = bf16(grad)
    ones = jnp.ones((8, VOX), jnp.bfloat16)
    rest = bf16(grad - rounded.astype(jnp.float32))
    bias_ref[...] += dot_lanes(ones, rounded) + dot_lanes(ones, rest)
    wide = jnp.concatenate([rounded.astype(jnp.float32), jnp.zeros((OUT, 128), jnp.float32)], axis=1)
    shifted = bf16(pltpu.roll(wide, 64, 1))
    total_ref[0:576] += dot_lanes(stacked_ref[0, :, 0 : FRAME - 128], shifted)
    total_ref[576:1152] += dot_lanes(stacked_ref[0, :, 128 : 128 + VOX], rounded)
    total_ref[1152:1728] += dot_lanes(stacked_ref[0, :, 128:], shifted)

    @pl.when(slot == SLOTS - 1)
    def _():
        core = lax.axis_index("c")
        mine_ref[:HALF] = total_ref[pl.ds(pl.multiple_of(core * HALF, 8), HALF), :]
        mine_ref[HALF:] = bias_ref[...]
        other_ref[:HALF] = total_ref[pl.ds(pl.multiple_of((1 - core) * HALF, 8), HALF), :]
        other_ref[HALF:] = bias_ref[...]


def share_kernel(mine_ref, got_ref, pooled_ref, tags_ref, message_ref):
    core = lax.axis_index("c")
    total = mine_ref[...] + got_ref[...]
    rounded = bf16(total)
    rows, lanes = grid_of((CHIPS, 128))
    piece = ((lanes >> 4) - (rows & 7)) & 7
    last = jnp.zeros((CHIPS, 128), jnp.float32)
    repeat = onehot((CHIPS, EXTRA // 3), lambda r, c: (r >> 3) == c)
    for t in range(3):
        start = 3 * CHIPS + t * (EXTRA // 3)
        last = jnp.where(piece == t, dot(repeat, rounded[start : start + EXTRA // 3]), last)

    bias = total[HALF : HALF + 1]
    high = bf16(bias).astype(jnp.float32)
    low = bf16(bias - high).astype(jnp.float32)
    value = jnp.where(lanes == (rows & 127), jnp.where(rows < 128, high, low), 0.0)
    last = jnp.where(piece == 7, jnp.sum(value, axis=1, keepdims=True), last)

    tags = tags_ref[...]
    columns = tags.astype(jnp.float32).astype(jnp.int32)
    by_lane = dot_lanes(onehot((8, 128), lambda r, c: c == r + 64), tags).astype(jnp.int32)
    chips = lax.broadcasted_iota(jnp.int32, (CHIPS, 2 * CHIPS), 0)
    parity = (lax.broadcasted_iota(jnp.int32, (2 * CHIPS, 128), 1) >> 5) & 1
    pooled = jnp.zeros((CHIPS, 128), jnp.float32)
    for slot in range(SLOTS):
        line, owner = by_lane[slot : slot + 1], by_lane[4 + slot : 5 + slot]
        chip = (owner >> 1) * BLOCK + ((line - 1) >> 1)
        chip = jnp.where((line > 0) & ((owner & 1) == core), chip, -1)
        copies = dot(
            pooled_ref[...], onehot((128, 128), lambda r, c: ((r >> 5) == slot) & ((r & 31) == (c & 31)))
        )
        copies = jnp.where(parity == ((columns[:, 64 + slot : 65 + slot] - 1) & 1), copies, 0.0)
        pooled += dot(bf16(jnp.where(chips == chip, 1.0, 0.0)), bf16(copies))
    last = bf16(jnp.where((piece >= 3) & (piece < 7), pooled, last))

    order = onehot((256, 256), lambda r, c: c == (r & 3) * 64 + (r >> 2))
    for quarter in range(4):
        at = 64 * quarter
        block = jnp.concatenate(
            [rounded[t * CHIPS + at : t * CHIPS + at + 64] for t in range(3)] + [last[at : at + 64]], axis=0
        )
        message_ref[256 * quarter : 256 * (quarter + 1), :] = bf16(dot(order, block))


def reduce_kernel(pieces_ref, message_ref, pooled_ref):
    chip = lax.axis_index("z") * BLOCK + lax.axis_index("b")
    pieces = pieces_ref[...]
    sums = dot(onehot((8, 4 * CHIPS), lambda r, c: (c & 3) == r), pieces)
    rows, lanes = grid_of((8, 128))
    piece = ((lanes >> 4) - chip) & 7
    high = bf16(sums).astype(jnp.float32)
    low = pltpu.roll(sums - high, 64, 1)
    last = jnp.where((piece < 3) | (piece == 7), high, jnp.where(piece == 3, low, 0.0))
    tile = bf16(jnp.where(rows < 3, high, last))
    message_ref[...] = bf16(dot(onehot((4 * CHIPS, 8), lambda r, c: (r & 3) == c), tile))

    pooled = dot(onehot((CHIPS, 4 * CHIPS), lambda r, c: c == 4 * r + 3), pieces)
    piece = ((lax.broadcasted_iota(jnp.int32, (CHIPS, 128), 1) >> 4) - chip) & 7
    pooled = jnp.where((piece >= 3) & (piece < 7), pooled, 0.0)
    pooled_ref[...] = bf16(pooled + pltpu.roll(pooled, 64, 1))


def finish_kernel(pieces_ref, weight_ref, bias_ref):
    order = onehot((256, 256), lambda r, c: r == (c & 3) * 64 + (c >> 2))
    rows, lanes = grid_of((CHIPS, 128))
    piece = ((lanes >> 4) - (rows & 7)) & 7
    gather = onehot((EXTRA // 3, CHIPS), lambda r, c: (c >> 3) == r)
    for half in range(2):
        last = []
        for quarter in range(4):
            start = half * 4 * CHIPS + 256 * quarter
            block = dot(order, pieces_ref[start : start + 256, :])
            for t in range(3):
                at = half * HALF + t * CHIPS + 64 * quarter
                weight_ref[at : at + 64, :] = block[64 * t : 64 * (t + 1)]
            last.append(block[192:])
        last = jnp.concatenate(last, axis=0)
        for t in range(3):
            at = half * HALF + 3 * CHIPS + t * (EXTRA // 3)
            weight_ref[at : at + EXTRA // 3, :] = dot(gather, bf16(jnp.where(piece == t, last, 0.0)))
        if half == 0:
            parts = jnp.where(((piece == 7) | (piece == 3)) & ((lanes & 15) == 0), last, 0.0)
            value = jnp.sum(parts, axis=1, keepdims=True)
            spread = jnp.where(lanes == (rows & 127), value, 0.0)
            bias_ref[...] = jnp.sum(spread, axis=0, keepdims=True)


def call(kernel, name, outs, operands, smem=0):
    return pl.pallas_call(
        kernel,
        out_shape=[jax.ShapeDtypeStruct(shape, dtype) for shape, dtype in outs],
        in_specs=[pl.BlockSpec(memory_space=SMEM if i < smem else VMEM) for i in range(len(operands))],
        out_specs=[pl.BlockSpec(memory_space=VMEM) for _ in outs],
        compiler_params=pltpu.CompilerParams(vmem_limit_bytes=32 * 1024 * 1024),
        name=name,
    )(*operands)


def forward(counts, neighbors, features, layers, before, after, weight, bias):
    def whole(shape):
        return pl.BlockSpec(shape, lambda i, *_: (0,) * len(shape))

    def per_slot(shape):
        return pl.BlockSpec((1,) + shape, lambda i, *_: (i, 0, 0))

    return pl.pallas_call(
        forward_kernel,
        grid_spec=pltpu.PrefetchScalarGridSpec(
            num_scalar_prefetch=2,
            grid=(SLOTS,),
            in_specs=[
                whole((SLOTS, CH, VOX)),
                whole((SLOTS, CH, 128)),
                whole((SLOTS, CH, 128)),
                whole((SLOTS, CH, 128)),
                whole((3 * OUT, 9 * CH)),
                whole((OUT, 1)),
            ],
            out_specs=[
                whole((CHIPS, 128)),
                per_slot((9 * CH, FRAME)),
                per_slot((OUT, VOX)),
            ],
            scratch_shapes=[
                pltpu.VMEM((SLOTS + 1, CH, VOX), jnp.float32),
                pltpu.VMEM((3 * SLOTS + 1, CH, 128), jnp.float32),
                pltpu.VMEM((OUT, 256), jnp.float32),
            ],
        ),
        out_shape=[
            jax.ShapeDtypeStruct((CHIPS, 128), jnp.bfloat16),
            jax.ShapeDtypeStruct((SLOTS, 9 * CH, FRAME), jnp.bfloat16),
            jax.ShapeDtypeStruct((SLOTS, OUT, VOX), jnp.float32),
        ],
        compiler_params=pltpu.CompilerParams(vmem_limit_bytes=32 * 1024 * 1024),
        cost_estimate=pl.CostEstimate(flops=3_500_000_000, bytes_accessed=6_000_000, transcendentals=300_000),
        name="forward",
    )(counts, neighbors, features, layers, before, after, weight, bias)


def backward(pieces, stacked, slope):
    def whole(shape):
        return pl.BlockSpec(shape, lambda i: (0,) * len(shape))

    def per_slot(shape):
        return pl.BlockSpec((1,) + shape, lambda i: (i, 0, 0))

    return pl.pallas_call(
        backward_kernel,
        grid=(SLOTS,),
        in_specs=[whole((2 * CHIPS, 128)), per_slot((9 * CH, FRAME)), per_slot((OUT, VOX))],
        out_specs=[whole((HALF + 8, OUT)), whole((HALF + 8, OUT)), whole((CHIPS, 128))],
        scratch_shapes=[
            pltpu.VMEM((OUT, 256), jnp.bfloat16),
            pltpu.VMEM((TAP_ROWS, OUT), jnp.float32),
            pltpu.VMEM((8, OUT), jnp.float32),
        ],
        out_shape=[
            jax.ShapeDtypeStruct((HALF + 8, OUT), jnp.float32),
            jax.ShapeDtypeStruct((HALF + 8, OUT), jnp.float32),
            jax.ShapeDtypeStruct((CHIPS, 128), jnp.bfloat16),
        ],
        compiler_params=pltpu.CompilerParams(vmem_limit_bytes=32 * 1024 * 1024),
        cost_estimate=pl.CostEstimate(flops=3_500_000_000, bytes_accessed=6_000_000, transcendentals=0),
        name="backward",
    )(pieces, stacked, slope)


def to_chips(message, rows):
    message = message.reshape(CHIPS, rows, 128)
    return lax.all_to_all(message, ("z", "b"), 0, 0, tiled=True)


def per_device(
    features,
    counts,
    rebalance,
    neighbors,
    coarse_owner,
    conv_weight,
    convolution_bias_vector,
    merged_adjoint,
):
    narrow, wide = jnp.bfloat16, jnp.float32
    occupied = rebalance >= 0
    line = jnp.where(occupied, rebalance % (2 * BLOCK) + 1, 0)
    owner = jnp.where(occupied, coarse_owner, 0)
    adjoint = merged_adjoint.reshape(128, 128)
    (offer,) = call(offer_kernel, "offer", [((2 * CHIPS, 128), narrow)], (line, owner, adjoint), smem=2)
    offers = to_chips(offer, 2)

    (layers,) = call(layers_kernel, "layers", [((SLOTS, CH, 128), narrow)], (counts, features), smem=1)
    up = [(i, i + 1) for i in range(BLOCK - 1)]
    down = [(i + 1, i) for i in range(BLOCK - 1)]
    before = lax.ppermute(layers, "b", up)
    after = lax.ppermute(layers, "b", down)
    weight = conv_weight.reshape(3, 9 * CH, OUT).transpose(0, 2, 1).reshape(3 * OUT, 9 * CH)
    pooled_pieces, stacked, slope = forward(
        counts, neighbors, features, layers, before, after, weight, convolution_bias_vector[:, None]
    )

    offers = lax.all_gather(offers, "c", tiled=True).reshape(4 * CHIPS, 128)
    message, tags = call(
        choose_kernel,
        "choose",
        [((2 * CHIPS, 128), narrow), ((2 * CHIPS, 128), narrow)],
        (offers, pooled_pieces),
    )
    pieces = to_chips(message, 2).reshape(2 * CHIPS, 128)
    mine, other, pooled_pieces = backward(pieces, stacked, slope)
    got = lax.ppermute(other, "c", [(0, 1), (1, 0)])
    pooled_pieces = lax.all_gather(pooled_pieces, "c", tiled=True)
    (message,) = call(
        share_kernel, "share", [((4 * CHIPS, 128), narrow)], (mine, got, pooled_pieces, tags)
    )
    pieces = to_chips(message, 4).reshape(4 * CHIPS, 128)
    message, pooled = call(
        reduce_kernel, "reduce", [((4 * CHIPS, 128), narrow), ((CHIPS, 128), narrow)], (pieces,)
    )
    pieces = to_chips(message, 4)
    pieces = lax.all_gather(pieces, "c", tiled=True).reshape(8 * CHIPS, 128)
    weight_total, bias_total = call(
        finish_kernel, "finish", [((TAP_ROWS, OUT), wide), ((1, OUT), wide)], (pieces,)
    )
    pooled = pooled[:, :64].reshape(CHIPS, 2, 32).transpose(1, 0, 2).reshape(2, CHIPS * 32)
    return pooled, weight_total.reshape(27, CH, OUT), bias_total.reshape(OUT)


def solution(mesh):
    chips = Mesh(mesh.devices.reshape(-1, 2, BLOCK), ("z", "c", "b"))
    whole = ("z", "c", "b")
    in_specs = (
        P(whole, None, None),
        P(whole),
        P(whole),
        P(whole, None),
        P(whole),
        P(),
        P(),
        P(whole, None),
    )
    out_specs = (P(whole, None), P(), P())
    return jax.shard_map(
        per_device, mesh=chips, in_specs=in_specs, out_specs=out_specs, check_vma=False
    )
```

```python
import functools

import jax
import jax.numpy as jnp
from jax import lax
from jax.experimental import pallas as pl
from jax.experimental.pallas import tpu as pltpu
from jax.sharding import Mesh
from jax.sharding import PartitionSpec as P

SLOTS = 4
CH = 64
OUT = 128
VOX = 512
FRAME = 768
TAP_ROWS = 1728
BLOCK = 32
HALF = TAP_ROWS // 2
MAIN = 24
EXTRA = 3
SHARE = MAIN + EXTRA
HBM = pltpu.HBM
EDGES = ((-1, -1), (-1, 0), (-1, 1), (0, -1), (0, 0), (0, 1), (1, -1), (1, 0), (1, 1))
SMEM = pltpu.SMEM


def voxel_mask(count):
    lanes = lax.broadcasted_iota(jnp.int32, (1, VOX), 1)
    return ((lanes * 167) & 511) < count


def layer_pair(block):
    lanes = lax.broadcasted_iota(jnp.int32, (CH, 128), 1)
    return jnp.where(lanes < 64, block[:, :128], block[:, VOX - 128 :])


def column_of(ea, eb, ec):
    tap = 9 * (ea + 1) + 3 * (eb + 1) + (ec + 1)
    return tap if tap < 13 else tap - 1


def dot(a, b):
    return jnp.dot(a, b, preferred_element_type=jnp.float32)


def dot_lanes(a, b):
    return lax.dot_general(a, b, (((1,), (1,)), ((), ())), preferred_element_type=jnp.float32)


def grid_of(shape):
    return lax.broadcasted_iota(jnp.int32, shape, 0), lax.broadcasted_iota(jnp.int32, shape, 1)


def onehot(shape, chosen):
    return jnp.where(chosen(*grid_of(shape)), 1.0, 0.0).astype(jnp.bfloat16)


def bf16(array):
    return array.astype(jnp.bfloat16)


def pool_table(voxels_first):
    shape = (VOX, 64) if voxels_first else (64, VOX)
    rows, columns = grid_of(shape)
    voxel, cell = (rows, columns) if voxels_first else (columns, rows)
    index = ((voxel >> 7) << 4) | (((voxel >> 4) & 3) << 2) | ((voxel & 7) >> 1)
    return bf16(jnp.where(index == cell, 0.125, 0.0))


def fetch(pairs, sems):
    copies = [pltpu.make_async_copy(source, target, sems.at[i]) for i, (source, target) in enumerate(pairs)]
    for copy in copies:
        copy.start()
    for copy in copies:
        copy.wait()


def begin_kernel(
    counts_hbm, rebalance_hbm, owner_hbm, features_hbm, adjoint_hbm,
    layers_ref, offer_ref,
    counts_ref, rebalance_ref, owner_ref, features_ref, adjoint_ref, dense_ref, sems,
):
    fetch(
        [
            (counts_hbm, counts_ref),
            (rebalance_hbm, rebalance_ref),
            (owner_hbm, owner_ref),
            (features_hbm, features_ref),
            (adjoint_hbm, adjoint_ref),
        ],
        sems,
    )
    lanes = lax.broadcasted_iota(jnp.int32, (1, 128), 1)
    tags = jnp.zeros((1, 128), jnp.float32)
    for slot in range(SLOTS):
        block = jnp.where(voxel_mask(counts_ref[slot]), features_ref[slot].astype(jnp.float32), 0.0)
        layers_ref[slot] = bf16(layer_pair(block))
        row = rebalance_ref[slot]
        line = jnp.where(row >= 0, (row & (2 * BLOCK - 1)) + 1, 0).astype(jnp.float32)
        owner = jnp.maximum(owner_ref[slot], 0).astype(jnp.float32)
        tags = jnp.where(lanes == slot, line, tags)
        tags = jnp.where(lanes == SLOTS + slot, owner, tags)
    for part in range(64):
        dense_ref[2 * part : 2 * part + 2, :] = adjoint_ref[:, 128 * part : 128 * (part + 1)].astype(jnp.float32)
    order = onehot(
        (8 * BLOCK, 128),
        lambda r, c: ((r & 7) < 4) & (c == 2 * (2 * (r >> 3) + (r & 1)) + ((r >> 1) & 1)),
    )
    rows = lax.broadcasted_iota(jnp.int32, (8 * BLOCK, 128), 0)
    offer_ref[...] = bf16(jnp.where((rows & 7) == 4, tags, dot(order, bf16(dense_ref[...]))))


def spread_kernel(offers_ref, message_ref, tags_ref):
    offers = offers_ref[...]
    message = bf16(dot(onehot((4 * BLOCK, 8 * BLOCK), lambda r, c: c == 8 * (r >> 2) + (r & 3)), offers))
    message_ref[...] = jnp.broadcast_to(message[None], message_ref.shape)
    tags_ref[...] = dot(onehot((BLOCK, 8 * BLOCK), lambda r, c: c == 8 * r + 4), offers).astype(jnp.int32)


def place_of(tags_ref, row):
    tags = tags_ref[...]
    rows, lanes = grid_of((BLOCK, 128))
    hit = (tags == 2 * lax.axis_index("b") + row + 1) & (lanes < SLOTS)
    owner = jnp.where(hit, pltpu.roll(tags, 128 - SLOTS, 1), 0).astype(jnp.float32)
    home = jnp.where(hit, rows, 0).astype(jnp.float32)
    return [
        jnp.sum(jnp.sum(value, axis=1, keepdims=True), axis=0, keepdims=True).astype(jnp.int32)[0, 0]
        for value in (home, owner)
    ]


def forward_kernel(start, *refs):
    operands, refs = refs[: 7 + start // 2], refs[7 + start // 2 :]
    pooled_ref, stacked_hbm, slope_hbm, features_ref, blocks_ref, rims_ref, stacked_ref, slope_ref, dense_ref = refs[:9]
    counts_ref, neighbors_ref, bias_ref, weight_ref, sems, out_sems = refs[9:]
    targets = [
        counts_ref,
        neighbors_ref,
        bias_ref,
        features_ref,
        rims_ref.at[pl.ds(0, SLOTS)],
        rims_ref.at[pl.ds(2 * SLOTS, SLOTS)],
        weight_ref,
        dense_ref.at[pl.ds(0, 2)],
    ]
    fetch(list(zip(operands, targets)), sems)
    for index in range(SLOTS):
        block = jnp.where(voxel_mask(counts_ref[index]), features_ref[index].astype(jnp.float32), 0.0)
        blocks_ref[index] = block
        rims_ref[SLOTS + index] = bf16(layer_pair(block))
    blocks_ref[SLOTS] = jnp.zeros((CH, VOX), jnp.float32)
    rims_ref[3 * SLOTS] = jnp.zeros((CH, 128), jnp.bfloat16)
    first = ((lax.axis_index("z") * 2 + lax.axis_index("c")) * BLOCK + lax.axis_index("b")) * SLOTS
    rows, columns = grid_of((OUT, OUT))
    bias = jnp.sum(jnp.where(rows == columns, bias_ref[...], 0.0), axis=1, keepdims=True)
    lanes = lax.broadcasted_iota(jnp.int32, (CH, FRAME), 1)
    at_c = lanes & 7
    at_b = (lanes >> 3) & 7

    def moved(array, steps):
        return pltpu.roll(array, (-steps) % FRAME, 1)

    @pl.loop(0, 2)
    def _(place):
        slot = start + place

        def rim(ea, eb, ec):
            target = neighbors_ref[slot, column_of(ea, eb, ec)]
            at = jnp.clip(target - (first - SLOTS), 0, 3 * SLOTS - 1)
            return rims_ref[jnp.where(target >= 0, at, 3 * SLOTS)].astype(jnp.float32)

        def inner(eb, ec):
            if eb == 0 and ec == 0:
                return blocks_ref[slot]
            target = neighbors_ref[slot, column_of(0, eb, ec)]
            at = jnp.clip(target - first, 0, SLOTS - 1)
            return blocks_ref[jnp.where(target >= 0, at, SLOTS)]

        def frame(eb, ec):
            return jnp.concatenate([rim(-1, eb, ec), inner(eb, ec), rim(1, eb, ec)], axis=1)

        along_c = {}
        for eb in (-1, 0, 1):
            middle = frame(eb, 0)
            along_c[eb, 0] = middle
            along_c[eb, -1] = jnp.where(at_c == 0, moved(frame(eb, -1), 7), moved(middle, -1))
            along_c[eb, 1] = jnp.where(at_c == 7, moved(frame(eb, 1), -7), moved(middle, 1))
        for index, (eb, ec) in enumerate(EDGES):
            if eb == 0:
                value = along_c[0, ec]
            elif eb < 0:
                value = jnp.where(at_b == 0, moved(along_c[-1, ec], 56), moved(along_c[0, ec], -8))
            else:
                value = jnp.where(at_b == 7, moved(along_c[1, ec], -56), moved(along_c[0, ec], 8))
            stacked_ref[place, index * CH : (index + 1) * CH, :] = value.astype(jnp.bfloat16)

        pltpu.make_async_copy(stacked_ref.at[place], stacked_hbm.at[place], out_sems.at[place]).start()
        product = dot(weight_ref[...], stacked_ref[place])
        sides = product[:OUT, : FRAME - 128] + product[2 * OUT :, 128:]
        sides = pltpu.roll(sides, FRAME - 128 - 64, 1)[:, :VOX]
        preact = product[OUT : 2 * OUT, 128 : 128 + VOX] + sides + bias
        mask = voxel_mask(counts_ref[slot])
        sigmoid = jax.nn.sigmoid(preact)
        slope = sigmoid * (1.0 + preact * (1.0 - sigmoid))
        slope_ref[place] = jnp.where(mask, slope, 0.0)
        pltpu.make_async_copy(slope_ref.at[place], slope_hbm.at[place], out_sems.at[2 + place]).start()
        activation = jnp.where(mask, preact * sigmoid, 0.0)
        high = activation.astype(jnp.bfloat16)
        low = (activation - high.astype(jnp.float32)).astype(jnp.bfloat16)
        table = pool_table(True)
        cells = bf16(dot(high, table) + dot(low, table))
        even = dot(onehot((64, OUT), lambda r, c: c == 2 * r), cells)
        odd = dot(onehot((64, OUT), lambda r, c: c == 2 * r + 1), cells)
        dense_ref[start + place] = jnp.concatenate([even, odd], axis=1)

    if start == 0:
        pooled_ref[...] = dense_ref[:2]
    else:
        order = onehot((8 * BLOCK, 64 * SLOTS), lambda r, c: c == 64 * ((r & 7) >> 1) + 2 * (r >> 3) + (r & 1))
        pooled_ref[...] = bf16(dot(order, bf16(dense_ref[...].reshape(64 * SLOTS, 128))))
    for place in range(2):
        pltpu.make_async_copy(stacked_ref.at[place], stacked_hbm.at[place], out_sems.at[place]).wait()
        pltpu.make_async_copy(slope_ref.at[place], slope_hbm.at[place], out_sems.at[2 + place]).wait()


def choose_kernel(tags_ref, adjoint_ref, pooled_ref, message_ref):
    tags = bf16(tags_ref[...].astype(jnp.float32))
    tags = dot(onehot((8 * BLOCK, BLOCK), lambda r, c: (r >> 3) == c), tags)
    rows, lanes = grid_of((8 * BLOCK, 128))
    slot = (rows & 7) >> 1
    line = jnp.sum(jnp.where(lanes == slot, tags, 0.0), axis=1, keepdims=True).astype(jnp.int32)
    owner = jnp.sum(jnp.where(lanes == slot + SLOTS, tags, 0.0), axis=1, keepdims=True).astype(jnp.int32)
    source = ((owner & 1) * 8 + (owner >> 1)) * (4 * BLOCK) + 2 * (line - 1) + (rows[:, :1] & 1)
    source = jnp.where(line > 0, source, -1)
    lanes = lax.broadcasted_iota(jnp.int32, (8 * BLOCK, 64 * BLOCK), 1)
    cotangent = dot(bf16(jnp.where(lanes == source, 1.0, 0.0)), adjoint_ref[...])
    pooled = pooled_ref[...].astype(jnp.float32)
    message_ref[...] = bf16(
        jnp.concatenate([cotangent.reshape(BLOCK, 8, 128), pooled.reshape(BLOCK, 8, 128)], axis=1)
    )


def add_half(half, total_ref, grads_ref, stacked_ref, ready=lambda slot: None):
    middle = HALF - 9 * CH
    for slot in range(SLOTS):
        grad = grads_ref[slot]
        wide = jnp.concatenate([grad.astype(jnp.float32), jnp.zeros((OUT, 128), jnp.float32)], axis=1)
        shifted = bf16(pltpu.roll(wide, 64, 1))
        ready(slot)
        if half == 0:
            side = dot_lanes(stacked_ref[slot, :, 0 : FRAME - 128], shifted)
            inner = dot_lanes(stacked_ref[slot, :middle, 128 : 128 + VOX], grad)
            parts = ((0, 9 * CH, side), (9 * CH, HALF, inner))
        else:
            inner = dot_lanes(stacked_ref[slot, middle:, 128 : 128 + VOX], grad)
            side = dot_lanes(stacked_ref[slot, :, 128:], shifted)
            parts = ((0, middle, inner), (middle, HALF, side))
        for low, high, value in parts:
            if slot == 0:
                total_ref[low:high] = value
            else:
                total_ref[low:high] += value


def other_half_kernel(
    first_stacked, second_stacked, first_slope, second_slope, rows_ref,
    total_ref, grads_ref, bias_ref, stacked_ref, slope_ref, sems,
):
    slopes = [
        pltpu.make_async_copy(source, slope_ref.at[pl.ds(2 * i, 2)], sems.at[i])
        for i, source in enumerate((first_slope, second_slope))
    ]
    frames = [
        pltpu.make_async_copy((first_stacked, second_stacked)[i // 2].at[i % 2], stacked_ref.at[i], sems.at[2 + i])
        for i in range(SLOTS)
    ]
    for copy in slopes + frames:
        copy.start()
    order = onehot(
        (64 * SLOTS, 16 * BLOCK),
        lambda r, c: c == 16 * ((r & 63) >> 1) + 2 * (r >> 6) + (r & 1),
    )
    dense = bf16(dot(order, rows_ref[...]))
    table = pool_table(False)
    even = onehot((OUT, 64), lambda r, c: r == 2 * c)
    odd = onehot((OUT, 64), lambda r, c: r == 2 * c + 1)
    ones = jnp.ones((8, VOX), jnp.bfloat16)
    bias = jnp.zeros((8, OUT), jnp.float32)
    for slot in range(SLOTS):
        row = dense[64 * slot : 64 * (slot + 1)]
        cells = dot(even, row[:, :64]) + dot(odd, row[:, 64:])
        spread = dot(bf16(cells), table)
        if slot % 2 == 0:
            slopes[slot // 2].wait()
        grad = spread * slope_ref[slot]
        rounded = bf16(grad)
        rest = bf16(grad - rounded.astype(jnp.float32))
        bias += dot_lanes(ones, rounded) + dot_lanes(ones, rest)
        grads_ref[slot] = rounded
    bias_ref[...] = bias
    total_ref[HALF:] = bias
    core = lax.axis_index("c")
    for half in range(2):

        @pl.when(core == 1 - half)
        def _():
            add_half(half, total_ref, grads_ref, stacked_ref, lambda slot: frames[slot].wait())


def own_half_kernel(grads_ref, bias_ref, stacked_ref, total_ref):
    total_ref[HALF:] = bias_ref[...]
    core = lax.axis_index("c")
    for half in range(2):

        @pl.when(core == half)
        def _():
            add_half(half, total_ref, grads_ref, stacked_ref)


def share_kernel(tags_ref, mine_ref, got_ref, pooled_ref, message_ref):
    total = mine_ref[...] + got_ref[...]
    tags = tags_ref[...].astype(jnp.float32)
    lines = dot_lanes(onehot((8, 128), lambda r, c: c == r), bf16(tags))
    lines = dot(bf16(lines), onehot((BLOCK, 16 * BLOCK), lambda r, c: (c >> 4) == r)).astype(jnp.int32)
    rows, columns = grid_of((8, 16 * BLOCK))
    lines = jnp.where(rows == ((columns >> 1) & 7) - SLOTS, lines, 0).astype(jnp.float32)
    line = jnp.sum(lines, axis=0, keepdims=True).astype(jnp.int32)
    columns = lax.broadcasted_iota(jnp.int32, (1, 16 * BLOCK), 1)
    target = 8 * ((line - 1) >> 1) + EXTRA + 2 * ((line - 1) & 1) + (columns & 1)
    target = jnp.where(line > 0, target, -1)
    rows = lax.broadcasted_iota(jnp.int32, (8 * BLOCK, 16 * BLOCK), 0)
    tail = dot(bf16(jnp.where(rows == target, 1.0, 0.0)), pooled_ref[...])
    extra = onehot(
        (8 * BLOCK, EXTRA * BLOCK), lambda r, c: ((r & 7) < EXTRA) & (c == (r & 7) * BLOCK + (r >> 3))
    )
    tail += dot(extra, bf16(total[MAIN * BLOCK : HALF]))
    bias = total[HALF : HALF + 1]
    high = bf16(bias).astype(jnp.float32)
    rows = lax.broadcasted_iota(jnp.int32, (8 * BLOCK, 128), 0)
    tail = jnp.where((rows & 7) == 7, jnp.where((rows & 8) == 0, high, bias - high), tail)
    main = total[: MAIN * BLOCK].reshape(BLOCK, MAIN, 128)
    message_ref[...] = bf16(jnp.concatenate([main, tail.reshape(BLOCK, 8, 128)], axis=1))


def over_block_kernel(tags_ref, pieces_ref, message_ref):
    total = jnp.zeros((32, 128), jnp.float32)
    for device in range(BLOCK):
        total += pieces_ref[device].astype(jnp.float32)
    order = onehot(
        (128, 32 * BLOCK),
        lambda r, c: c == 32 * ((r & 63) >> 1) + SHARE + 2 * (r >> 6) + (r & 1),
    )
    pooled = bf16(dot(order, pieces_ref[...].reshape(32 * BLOCK, 128)))
    rows, lanes = grid_of((32, 128))
    total = jnp.where((rows < SHARE) | (rows == 31), total, 0.0)
    high = bf16(total).astype(jnp.float32)
    low = total - high
    owners = [place_of(tags_ref, row)[1] for row in range(2)]
    for z in range(8):
        tag = jnp.zeros((32, 128), jnp.float32)
        for core in range(2):
            for row in range(2):
                here = (rows == 28) & (lanes == core) & (owners[row] == 2 * z + core)
                tag = jnp.where(here, row + 1.0, tag)
        message_ref[3 * z] = bf16(jnp.concatenate([high + tag, low], axis=0))
        message_ref[3 * z + 1] = jnp.zeros((64, 128), jnp.bfloat16)
        message_ref[3 * z + 2] = jnp.zeros((64, 128), jnp.bfloat16)
    for row in range(2):
        message_ref[3 * (owners[row] >> 1) + 1 + (owners[row] & 1)] = pooled[64 * row : 64 * (row + 1)]


def over_z_kernel(pieces_ref, message_ref, mine_ref, other_ref):
    total = jnp.zeros((32, 128), jnp.float32)
    pooled = [[jnp.zeros((64, 128), jnp.float32) for _ in range(2)] for _ in range(2)]
    for z in range(8):
        parts = pieces_ref[3 * z].astype(jnp.float32)
        total += parts[:32] + parts[32:]
        for core in range(2):
            tag = parts[28:29, core : core + 1]
            value = pieces_ref[3 * z + 1 + core].astype(jnp.float32)
            for row in range(2):
                pooled[core][row] += jnp.where(tag == row + 1.0, value, 0.0)
    rows = lax.broadcasted_iota(jnp.int32, (32, 128), 0)
    bias = total[31:32]
    high = bf16(bias).astype(jnp.float32)
    tile = jnp.where(rows < SHARE, total, jnp.where(rows == 27, high, bias - high))
    message_ref[...] = jnp.broadcast_to(bf16(tile)[None], (BLOCK, 32, 128))
    core = lax.axis_index("c")
    for row in range(2):
        mine_ref[row] = bf16(jnp.where(core == 0, pooled[0][row], pooled[1][row]))
        other_ref[row] = bf16(jnp.where(core == 0, pooled[1][row], pooled[0][row]))


def finish_kernel(pieces_ref, weight_ref, bias_ref):
    order = onehot((EXTRA * BLOCK, 32 * BLOCK), lambda r, c: c == 32 * (r & 31) + MAIN + (r >> 5))
    for half in range(2):
        pieces = pieces_ref[half * BLOCK : (half + 1) * BLOCK]
        for device in range(BLOCK):
            start = half * HALF + device * MAIN
            part = pieces_ref[half * BLOCK + device].astype(jnp.float32)
            weight_ref[start : start + MAIN, :] = part[:MAIN]
        start = half * HALF + MAIN * BLOCK
        weight_ref[start : start + EXTRA * BLOCK, :] = dot(order, pieces.reshape(32 * BLOCK, 128))
    parts = [pieces_ref[device].astype(jnp.float32) for device in range(2)]
    bias_ref[...] = parts[0][27:28] + parts[0][28:29] + (parts[1][27:28] + parts[1][28:29])


def hbm(array):
    return pltpu.with_memory_space_constraint(array, HBM)


def vmem(array):
    return pltpu.with_memory_space_constraint(array, pltpu.VMEM)


def call(kernel, name, outs, operands, in_hbm=0, scratch=(), limit=12, flops=1_000_000):
    specs = [pl.BlockSpec(memory_space=HBM) for _ in range(in_hbm)]
    specs += [pl.BlockSpec(memory_space=pltpu.VMEM) for _ in operands[in_hbm:]]
    operands = [hbm(operand) for operand in operands[:in_hbm]] + list(operands[in_hbm:])
    return pl.pallas_call(
        kernel,
        out_shape=[
            pltpu.VMEM(shape, dtype) if kept else jax.ShapeDtypeStruct(shape, dtype) for shape, dtype, kept in outs
        ],
        in_specs=specs,
        out_specs=[pl.BlockSpec(memory_space=pltpu.VMEM) for _ in outs],
        scratch_shapes=list(scratch),
        compiler_params=pltpu.CompilerParams(vmem_limit_bytes=limit * 1024 * 1024),
        cost_estimate=pl.CostEstimate(flops=flops, bytes_accessed=1_000_000, transcendentals=0),
        name=name,
    )(*operands)


def begin(counts, rebalance, owner, features, adjoint):
    return call(
        begin_kernel,
        "begin",
        [
            ((SLOTS, CH, 128), jnp.bfloat16, False),
            ((8 * BLOCK, 128), jnp.bfloat16, False),
        ],
        (counts, rebalance, owner, features, adjoint),
        in_hbm=5,
        scratch=[
            pltpu.SMEM((SLOTS,), jnp.int32),
            pltpu.SMEM((SLOTS,), jnp.int32),
            pltpu.SMEM((SLOTS,), jnp.int32),
            pltpu.VMEM((SLOTS, CH, VOX), jnp.bfloat16),
            pltpu.VMEM((2, CH * 128), jnp.bfloat16),
            pltpu.VMEM((128, 128), jnp.float32),
            pltpu.SemaphoreType.DMA((5,)),
        ],
    )


def forward(start, *operands):
    pooled = ((2, 64, 128), jnp.float32) if start == 0 else ((8 * BLOCK, 128), jnp.bfloat16)
    kept = pl.BlockSpec(memory_space=HBM)
    return pl.pallas_call(
        functools.partial(forward_kernel, start),
        out_shape=[
            jax.ShapeDtypeStruct(*pooled),
            HBM((2, 9 * CH, FRAME), jnp.bfloat16),
            HBM((2, OUT, VOX), jnp.float32),
        ],
        in_specs=[kept for _ in operands],
        out_specs=[pl.BlockSpec(memory_space=pltpu.VMEM), kept, kept],
        scratch_shapes=[
            pltpu.VMEM((SLOTS, CH, VOX), jnp.bfloat16),
            pltpu.VMEM((SLOTS + 1, CH, VOX), jnp.float32),
            pltpu.VMEM((3 * SLOTS + 1, CH, 128), jnp.bfloat16),
            pltpu.VMEM((2, 9 * CH, FRAME), jnp.bfloat16),
            pltpu.VMEM((2, OUT, VOX), jnp.float32),
            pltpu.VMEM((SLOTS, 64, 128), jnp.float32),
            pltpu.SMEM((SLOTS,), jnp.int32),
            pltpu.SMEM((SLOTS, 26), jnp.int32),
            pltpu.VMEM((1, OUT), jnp.float32),
            pltpu.VMEM((3 * OUT, 9 * CH), jnp.bfloat16),
            pltpu.SemaphoreType.DMA((8,)),
            pltpu.SemaphoreType.DMA((4,)),
        ],
        compiler_params=pltpu.CompilerParams(vmem_limit_bytes=16 * 1024 * 1024),
        cost_estimate=pl.CostEstimate(flops=4_000_000_000, bytes_accessed=4_000_000, transcendentals=150_000),
        name="forward",
    )(*[hbm(operand) for operand in operands])


def exchange(message, axis):
    return lax.all_to_all(message, axis, 0, 0, tiled=True)


def per_device(
    features,
    counts,
    rebalance,
    neighbors,
    coarse_owner,
    conv_weight,
    convolution_bias_vector,
    merged_adjoint,
):
    narrow, wide = jnp.bfloat16, jnp.float32
    layers, offer = begin(counts, rebalance, coarse_owner, features, merged_adjoint)
    before = lax.ppermute(layers, "b", [(i, i + 1) for i in range(BLOCK - 1)])
    after = lax.ppermute(layers, "b", [(i + 1, i) for i in range(BLOCK - 1)])
    offers = exchange(offer.reshape(BLOCK, 8, 128), "b")
    weight = conv_weight.reshape(3, 9 * CH, OUT).transpose(0, 2, 1).reshape(3 * OUT, 9 * CH)
    bias = convolution_bias_vector.reshape(1, OUT)
    first = forward(0, counts, neighbors, bias, features, before, after, weight)
    offers, first_dense = lax.optimization_barrier((offers.reshape(8 * BLOCK, 128), first[0]))
    message, tags = call(
        spread_kernel,
        "spread",
        [((8, 4 * BLOCK, 128), narrow, False), ((BLOCK, 128), jnp.int32, False)],
        (offers,),
    )
    message, bias = lax.optimization_barrier((message, bias))
    adjoint = exchange(message, "z")
    adjoint = lax.all_gather(adjoint, "c", tiled=True).reshape(64 * BLOCK, 128)
    second = forward(2, counts, neighbors, bias, features, before, after, weight, first_dense)
    (message,) = call(
        choose_kernel,
        "choose",
        [((BLOCK, 16, 128), narrow, False)],
        (tags, adjoint, second[0]),
    )
    rows = exchange(message, "b").reshape(16 * BLOCK, 128)
    other, grads, bias_part, stacked = call(
        other_half_kernel,
        "other_half",
        [
            ((HALF + 8, OUT), wide, False),
            ((SLOTS, OUT, VOX), narrow, True),
            ((8, OUT), wide, True),
            ((SLOTS, 9 * CH, FRAME), narrow, True),
        ],
        (first[1], second[1], first[2], second[2], rows),
        in_hbm=4,
        scratch=[pltpu.VMEM((SLOTS, OUT, VOX), jnp.float32), pltpu.SemaphoreType.DMA((2 + SLOTS,))],
    )
    got = lax.ppermute(other, "c", [(0, 1), (1, 0)])
    (mine,) = call(
        own_half_kernel,
        "own_half",
        [((HALF + 8, OUT), wide, False)],
        (vmem(grads), vmem(bias_part), vmem(stacked)),
        flops=2_000_000_000,
    )
    (message,) = call(share_kernel, "share", [((BLOCK, 32, 128), narrow, False)], (tags, mine, got, rows))
    pieces = exchange(message, "b")
    (message,) = call(over_block_kernel, "over_block", [((24, 64, 128), narrow, False)], (tags, pieces))
    pieces = exchange(message.reshape(8, 192, 128), "z").reshape(24, 64, 128)
    message, pooled_mine, pooled_other = call(
        over_z_kernel,
        "over_z",
        [((BLOCK, 32, 128), narrow, False), ((2, CH, 128), narrow, False), ((2, CH, 128), narrow, False)],
        (pieces,),
    )
    pieces = exchange(message, "b")
    pooled = pooled_mine + lax.ppermute(pooled_other, "c", [(0, 1), (1, 0)])
    pieces = lax.all_gather(pieces, "c", tiled=True)
    weight_total, bias_total = call(
        finish_kernel, "finish", [((TAP_ROWS, OUT), wide, False), ((1, OUT), wide, False)], (pieces,)
    )
    return pooled.reshape(2, CH * 128), weight_total.reshape(27, CH, OUT), bias_total.reshape(OUT)


def solution(mesh):
    chips = Mesh(mesh.devices.reshape(-1, 2, BLOCK), ("z", "c", "b"))
    whole = ("z", "c", "b")
    in_specs = (
        P(whole, None, None),
        P(whole),
        P(whole),
        P(whole, None),
        P(whole),
        P(),
        P(),
        P(whole, None),
    )
    out_specs = (P(whole, None), P(), P())
    return jax.shard_map(
        per_device, mesh=chips, in_specs=in_specs, out_specs=out_specs, check_vma=False
    )
```

```python
import functools

import jax
import jax.numpy as jnp
from jax import lax
from jax.experimental import pallas as pl
from jax.experimental.pallas import tpu as pltpu
from jax.sharding import Mesh
from jax.sharding import PartitionSpec as P

SLOTS = 4
CH = 64
OUT = 128
VOX = 512
FRAME = 640
TAP_ROWS = 1728
BLOCK = 32
HALF = TAP_ROWS // 2
MAIN = 24
EXTRA = 3
SHARE = MAIN + EXTRA
HBM = pltpu.HBM
EDGES = ((-1, -1), (-1, 0), (-1, 1), (0, -1), (0, 0), (0, 1), (1, -1), (1, 0), (1, 1))
SMEM = pltpu.SMEM


def voxel_mask(count):
    lanes = lax.broadcasted_iota(jnp.int32, (1, VOX), 1)
    return ((lanes * 167) & 511) < count


def layer_pair(block):
    lanes = lax.broadcasted_iota(jnp.int32, (CH, 128), 1)
    return pltpu.roll(jnp.where(lanes < 64, block[:, :128], block[:, VOX - 128 :]), 64, 1)


def column_of(ea, eb, ec):
    tap = 9 * (ea + 1) + 3 * (eb + 1) + (ec + 1)
    return tap if tap < 13 else tap - 1


def dot(a, b):
    return jnp.dot(a, b, preferred_element_type=jnp.float32)


def dot_lanes(a, b):
    return lax.dot_general(a, b, (((1,), (1,)), ((), ())), preferred_element_type=jnp.float32)


def grid_of(shape):
    return lax.broadcasted_iota(jnp.int32, shape, 0), lax.broadcasted_iota(jnp.int32, shape, 1)


def onehot(shape, chosen):
    return jnp.where(chosen(*grid_of(shape)), 1.0, 0.0).astype(jnp.bfloat16)


def bf16(array):
    return array.astype(jnp.bfloat16)


def pool_table(voxels_first):
    shape = (VOX, 64) if voxels_first else (64, VOX)
    rows, columns = grid_of(shape)
    voxel, cell = (rows, columns) if voxels_first else (columns, rows)
    index = ((voxel >> 7) << 4) | (((voxel >> 4) & 3) << 2) | ((voxel & 7) >> 1)
    return bf16(jnp.where(index == cell, 0.125, 0.0))


def fetch(pairs, sems):
    copies = [pltpu.make_async_copy(source, target, sems.at[i]) for i, (source, target) in enumerate(pairs)]
    for copy in copies:
        copy.start()
    for copy in copies:
        copy.wait()


def begin_kernel(
    counts_hbm, rebalance_hbm, owner_hbm, features_hbm, adjoint_hbm,
    layers_ref, offer_ref,
    counts_ref, rebalance_ref, owner_ref, features_ref, adjoint_ref, dense_ref, sems,
):
    fetch(
        [
            (counts_hbm, counts_ref),
            (rebalance_hbm, rebalance_ref),
            (owner_hbm, owner_ref),
            (features_hbm, features_ref),
            (adjoint_hbm, adjoint_ref),
        ],
        sems,
    )
    lanes = lax.broadcasted_iota(jnp.int32, (1, 128), 1)
    tags = jnp.zeros((1, 128), jnp.float32)
    for slot in range(SLOTS):
        block = jnp.where(voxel_mask(counts_ref[slot]), features_ref[slot].astype(jnp.float32), 0.0)
        layers_ref[slot] = bf16(layer_pair(block))
        row = rebalance_ref[slot]
        line = jnp.where(row >= 0, (row & (2 * BLOCK - 1)) + 1, 0).astype(jnp.float32)
        owner = jnp.maximum(owner_ref[slot], 0).astype(jnp.float32)
        tags = jnp.where(lanes == slot, line, tags)
        tags = jnp.where(lanes == SLOTS + slot, owner, tags)
    for part in range(64):
        dense_ref[2 * part : 2 * part + 2, :] = adjoint_ref[:, 128 * part : 128 * (part + 1)].astype(jnp.float32)
    order = onehot(
        (8 * BLOCK, 128),
        lambda r, c: ((r & 7) < 4) & (c == 2 * (2 * (r >> 3) + (r & 1)) + ((r >> 1) & 1)),
    )
    rows = lax.broadcasted_iota(jnp.int32, (8 * BLOCK, 128), 0)
    offer_ref[...] = bf16(jnp.where((rows & 7) == 4, tags, dot(order, bf16(dense_ref[...]))))


def spread_kernel(offers_ref, message_ref, tags_ref):
    offers = offers_ref[...]
    message = bf16(dot(onehot((4 * BLOCK, 8 * BLOCK), lambda r, c: c == 8 * (r >> 2) + (r & 3)), offers))
    message_ref[...] = jnp.broadcast_to(message[None], message_ref.shape)
    tags_ref[...] = dot(onehot((BLOCK, 8 * BLOCK), lambda r, c: c == 8 * r + 4), offers).astype(jnp.int32)


def place_of(tags_ref, row):
    tags = tags_ref[...]
    rows, lanes = grid_of((BLOCK, 128))
    hit = (tags == 2 * lax.axis_index("b") + row + 1) & (lanes < SLOTS)
    owner = jnp.where(hit, pltpu.roll(tags, 128 - SLOTS, 1), 0).astype(jnp.float32)
    home = jnp.where(hit, rows, 0).astype(jnp.float32)
    return [
        jnp.sum(jnp.sum(value, axis=1, keepdims=True), axis=0, keepdims=True).astype(jnp.int32)[0, 0]
        for value in (home, owner)
    ]


def forward_kernel(start, *refs):
    operands, refs = refs[: 7 + start // 2], refs[7 + start // 2 :]
    pooled_out, stacked_ref, slope_hbm, features_ref, blocks_ref, rims_ref, slope_ref, dense_ref = refs[:8]
    counts_ref, neighbors_ref, bias_ref, taps_ref, weight_ref, sems, out_sems = refs[8:]
    targets = [
        counts_ref,
        neighbors_ref,
        bias_ref,
        features_ref,
        rims_ref.at[pl.ds(0, SLOTS)],
        rims_ref.at[pl.ds(2 * SLOTS, SLOTS)],
        taps_ref,
        dense_ref.at[pl.ds(0, 2)],
    ]
    fetch(list(zip(operands, targets)), sems)
    for index in range(SLOTS):
        block = jnp.where(voxel_mask(counts_ref[index]), features_ref[index].astype(jnp.float32), 0.0)
        block = pltpu.roll(block, 64, 1)
        blocks_ref[index] = block
        rims_ref[SLOTS + index] = bf16(block[:, :128])
    blocks_ref[SLOTS] = jnp.zeros((CH, VOX), jnp.float32)
    rims_ref[3 * SLOTS] = jnp.zeros((CH, 128), jnp.bfloat16)
    same = onehot((OUT, OUT), lambda r, c: r == c)
    for part in range(3):
        turned = dot_lanes(same, taps_ref[part * 9 * CH : (part + 1) * 9 * CH, :])
        weight_ref[part * OUT : (part + 1) * OUT, :] = bf16(turned)
    first = ((lax.axis_index("z") * 2 + lax.axis_index("c")) * BLOCK + lax.axis_index("b")) * SLOTS
    rows, columns = grid_of((OUT, OUT))
    bias = jnp.sum(jnp.where(rows == columns, bias_ref[...], 0.0), axis=1, keepdims=True)
    lanes = lax.broadcasted_iota(jnp.int32, (CH, FRAME), 1)
    at_c = lanes & 7
    at_b = (lanes >> 3) & 7

    def moved(array, steps):
        return pltpu.roll(array, (-steps) % FRAME, 1)

    @pl.loop(0, 2)
    def _(place):
        slot = start + place

        def rim(ea, eb, ec):
            target = neighbors_ref[slot, column_of(ea, eb, ec)]
            at = jnp.clip(target - (first - SLOTS), 0, 3 * SLOTS - 1)
            return rims_ref[jnp.where(target >= 0, at, 3 * SLOTS)].astype(jnp.float32)

        def inner(eb, ec):
            if eb == 0 and ec == 0:
                return blocks_ref[slot]
            target = neighbors_ref[slot, column_of(0, eb, ec)]
            at = jnp.clip(target - first, 0, SLOTS - 1)
            return blocks_ref[jnp.where(target >= 0, at, SLOTS)]

        def frame(eb, ec):
            low = lax.broadcasted_iota(jnp.int32, (CH, 128), 1) < 64
            block = inner(eb, ec)
            ends = block[:, :128]
            left = jnp.where(low, rim(-1, eb, ec), ends)
            right = jnp.where(low, ends, rim(1, eb, ec))
            return jnp.concatenate([left, block[:, 128:], right], axis=1)

        along_c = {}
        for eb in (-1, 0, 1):
            middle = frame(eb, 0)
            along_c[eb, 0] = middle
            along_c[eb, -1] = jnp.where(at_c == 0, moved(frame(eb, -1), 7), moved(middle, -1))
            along_c[eb, 1] = jnp.where(at_c == 7, moved(frame(eb, 1), -7), moved(middle, 1))
        for index, (eb, ec) in enumerate(EDGES):
            if eb == 0:
                value = along_c[0, ec]
            elif eb < 0:
                value = jnp.where(at_b == 0, moved(along_c[-1, ec], 56), moved(along_c[0, ec], -8))
            else:
                value = jnp.where(at_b == 7, moved(along_c[1, ec], -56), moved(along_c[0, ec], 8))
            stacked_ref[place, index * CH : (index + 1) * CH, :] = value.astype(jnp.bfloat16)

        product = dot(weight_ref[...], stacked_ref[place])
        middle = pltpu.roll(product[OUT : 2 * OUT], FRAME - 64, 1)[:, :VOX]
        preact = product[:OUT, :VOX] + middle + product[2 * OUT :, 128:] + bias
        mask = voxel_mask(counts_ref[slot])
        sigmoid = jax.nn.sigmoid(preact)
        slope = sigmoid * (1.0 + preact * (1.0 - sigmoid))
        slope_ref[place] = jnp.where(mask, slope, 0.0)
        pltpu.make_async_copy(slope_ref.at[place], slope_hbm.at[place], out_sems.at[place]).start()
        activation = jnp.where(mask, preact * sigmoid, 0.0)
        high = activation.astype(jnp.bfloat16)
        low = (activation - high.astype(jnp.float32)).astype(jnp.bfloat16)
        table = pool_table(True)
        cells = bf16(dot(high, table) + dot(low, table))
        even = dot(onehot((64, OUT), lambda r, c: c == 2 * r), cells)
        odd = dot(onehot((64, OUT), lambda r, c: c == 2 * r + 1), cells)
        dense_ref[start + place] = jnp.concatenate([even, odd], axis=1)

    copies = [pltpu.make_async_copy(slope_ref.at[place], slope_hbm.at[place], out_sems.at[place]) for place in range(2)]
    if start == 0:
        copies.append(pltpu.make_async_copy(dense_ref.at[pl.ds(0, 2)], pooled_out, out_sems.at[2]))
        copies[2].start()
    else:
        order = onehot((8 * BLOCK, 64 * SLOTS), lambda r, c: c == 64 * ((r & 7) >> 1) + 2 * (r >> 3) + (r & 1))
        pooled_out[...] = bf16(dot(order, bf16(dense_ref[...].reshape(64 * SLOTS, 128))))
    for copy in copies:
        copy.wait()


def choose_kernel(tags_ref, adjoint_ref, pooled_ref, message_ref):
    tags = bf16(tags_ref[...].astype(jnp.float32))
    tags = dot(onehot((8 * BLOCK, BLOCK), lambda r, c: (r >> 3) == c), tags)
    rows, lanes = grid_of((8 * BLOCK, 128))
    slot = (rows & 7) >> 1
    line = jnp.sum(jnp.where(lanes == slot, tags, 0.0), axis=1, keepdims=True).astype(jnp.int32)
    owner = jnp.sum(jnp.where(lanes == slot + SLOTS, tags, 0.0), axis=1, keepdims=True).astype(jnp.int32)
    source = ((owner & 1) * 8 + (owner >> 1)) * (4 * BLOCK) + 2 * (line - 1) + (rows[:, :1] & 1)
    source = jnp.where(line > 0, source, -1)
    lanes = lax.broadcasted_iota(jnp.int32, (8 * BLOCK, 64 * BLOCK), 1)
    cotangent = dot(bf16(jnp.where(lanes == source, 1.0, 0.0)), adjoint_ref[...])
    pooled = pooled_ref[...].astype(jnp.float32)
    message_ref[...] = bf16(
        jnp.concatenate([cotangent.reshape(BLOCK, 8, 128), pooled.reshape(BLOCK, 8, 128)], axis=1)
    )


def add_half(half, total_ref, grads_ref, stacked_refs):
    middle = HALF - 9 * CH
    for slot in range(SLOTS):
        stacked_ref, place = stacked_refs[slot // 2], slot % 2
        grad = grads_ref[slot]
        wide = jnp.concatenate([grad.astype(jnp.float32), jnp.zeros((OUT, 128), jnp.float32)], axis=1)
        shifted = bf16(pltpu.roll(wide, 64, 1))
        if half == 0:
            side = dot_lanes(stacked_ref[place, :, :VOX], grad)
            inner = dot_lanes(stacked_ref[place, :middle, :], shifted)
            parts = ((0, 9 * CH, side), (9 * CH, HALF, inner))
        else:
            inner = dot_lanes(stacked_ref[place, middle:, :], shifted)
            side = dot_lanes(stacked_ref[place, :, 128:], grad)
            parts = ((0, middle, inner), (middle, HALF, side))
        for low, high, value in parts:
            if slot == 0:
                total_ref[low:high] = value
            else:
                total_ref[low:high] += value


def other_half_kernel(
    first_slope, second_slope, first_stacked, second_stacked, rows_ref, total_ref, grads_ref, bias_ref, slope_ref, sems
):
    slopes = [
        pltpu.make_async_copy(source, slope_ref.at[pl.ds(2 * i, 2)], sems.at[i])
        for i, source in enumerate((first_slope, second_slope))
    ]
    for copy in slopes:
        copy.start()
    order = onehot(
        (64 * SLOTS, 16 * BLOCK),
        lambda r, c: c == 16 * ((r & 63) >> 1) + 2 * (r >> 6) + (r & 1),
    )
    dense = bf16(dot(order, rows_ref[...]))
    table = pool_table(False)
    even = onehot((OUT, 64), lambda r, c: r == 2 * c)
    odd = onehot((OUT, 64), lambda r, c: r == 2 * c + 1)
    ones = jnp.ones((8, VOX), jnp.bfloat16)
    bias = jnp.zeros((8, OUT), jnp.float32)
    for slot in range(SLOTS):
        row = dense[64 * slot : 64 * (slot + 1)]
        cells = dot(even, row[:, :64]) + dot(odd, row[:, 64:])
        spread = dot(bf16(cells), table)
        if slot % 2 == 0:
            slopes[slot // 2].wait()
        grad = spread * slope_ref[slot]
        rounded = bf16(grad)
        rest = bf16(grad - rounded.astype(jnp.float32))
        bias += dot_lanes(ones, rounded) + dot_lanes(ones, rest)
        grads_ref[slot] = rounded
    bias_ref[...] = bias
    total_ref[HALF:] = bias
    core = lax.axis_index("c")
    for half in range(2):

        @pl.when(core == 1 - half)
        def _():
            add_half(half, total_ref, grads_ref, (first_stacked, second_stacked))


def own_half_kernel(grads_ref, bias_ref, first_stacked, second_stacked, total_ref):
    total_ref[HALF:] = bias_ref[...]
    core = lax.axis_index("c")
    for half in range(2):

        @pl.when(core == half)
        def _():
            add_half(half, total_ref, grads_ref, (first_stacked, second_stacked))


def share_kernel(tags_ref, mine_ref, got_ref, pooled_ref, message_ref):
    total = mine_ref[...] + got_ref[...]
    tags = tags_ref[...].astype(jnp.float32)
    lines = dot_lanes(onehot((8, 128), lambda r, c: c == r), bf16(tags))
    lines = dot(bf16(lines), onehot((BLOCK, 16 * BLOCK), lambda r, c: (c >> 4) == r)).astype(jnp.int32)
    rows, columns = grid_of((8, 16 * BLOCK))
    lines = jnp.where(rows == ((columns >> 1) & 7) - SLOTS, lines, 0).astype(jnp.float32)
    line = jnp.sum(lines, axis=0, keepdims=True).astype(jnp.int32)
    columns = lax.broadcasted_iota(jnp.int32, (1, 16 * BLOCK), 1)
    target = 8 * ((line - 1) >> 1) + EXTRA + 2 * ((line - 1) & 1) + (columns & 1)
    target = jnp.where(line > 0, target, -1)
    rows = lax.broadcasted_iota(jnp.int32, (8 * BLOCK, 16 * BLOCK), 0)
    tail = dot(bf16(jnp.where(rows == target, 1.0, 0.0)), pooled_ref[...])
    extra = onehot(
        (8 * BLOCK, EXTRA * BLOCK), lambda r, c: ((r & 7) < EXTRA) & (c == (r & 7) * BLOCK + (r >> 3))
    )
    tail += dot(extra, bf16(total[MAIN * BLOCK : HALF]))
    bias = total[HALF : HALF + 1]
    high = bf16(bias).astype(jnp.float32)
    rows = lax.broadcasted_iota(jnp.int32, (8 * BLOCK, 128), 0)
    tail = jnp.where((rows & 7) == 7, jnp.where((rows & 8) == 0, high, bias - high), tail)
    main = total[: MAIN * BLOCK].reshape(BLOCK, MAIN, 128)
    message_ref[...] = bf16(jnp.concatenate([main, tail.reshape(BLOCK, 8, 128)], axis=1))


def over_block_kernel(tags_ref, pieces_ref, message_ref):
    total = jnp.zeros((32, 128), jnp.float32)
    for device in range(BLOCK):
        total += pieces_ref[device].astype(jnp.float32)
    order = onehot(
        (128, 32 * BLOCK),
        lambda r, c: c == 32 * ((r & 63) >> 1) + SHARE + 2 * (r >> 6) + (r & 1),
    )
    pooled = bf16(dot(order, pieces_ref[...].reshape(32 * BLOCK, 128)))
    rows, lanes = grid_of((32, 128))
    total = jnp.where((rows < SHARE) | (rows == 31), total, 0.0)
    high = bf16(total).astype(jnp.float32)
    low = total - high
    owners = [place_of(tags_ref, row)[1] for row in range(2)]
    for z in range(8):
        tag = jnp.zeros((32, 128), jnp.float32)
        for core in range(2):
            for row in range(2):
                here = (rows == 28) & (lanes == core) & (owners[row] == 2 * z + core)
                tag = jnp.where(here, row + 1.0, tag)
        message_ref[3 * z] = bf16(jnp.concatenate([high + tag, low], axis=0))
        message_ref[3 * z + 1] = jnp.zeros((64, 128), jnp.bfloat16)
        message_ref[3 * z + 2] = jnp.zeros((64, 128), jnp.bfloat16)
    for row in range(2):
        message_ref[3 * (owners[row] >> 1) + 1 + (owners[row] & 1)] = pooled[64 * row : 64 * (row + 1)]


def over_z_kernel(pieces_ref, message_ref, mine_ref, other_ref):
    total = jnp.zeros((32, 128), jnp.float32)
    pooled = [[jnp.zeros((64, 128), jnp.float32) for _ in range(2)] for _ in range(2)]
    for z in range(8):
        parts = pieces_ref[3 * z].astype(jnp.float32)
        total += parts[:32] + parts[32:]
        for core in range(2):
            tag = parts[28:29, core : core + 1]
            value = pieces_ref[3 * z + 1 + core].astype(jnp.float32)
            for row in range(2):
                pooled[core][row] += jnp.where(tag == row + 1.0, value, 0.0)
    rows = lax.broadcasted_iota(jnp.int32, (32, 128), 0)
    bias = total[31:32]
    high = bf16(bias).astype(jnp.float32)
    tile = jnp.where(rows < SHARE, total, jnp.where(rows == 27, high, bias - high))
    message_ref[...] = jnp.broadcast_to(bf16(tile)[None], (BLOCK, 32, 128))
    core = lax.axis_index("c")
    for row in range(2):
        mine_ref[row] = bf16(jnp.where(core == 0, pooled[0][row], pooled[1][row]))
        other_ref[row] = bf16(jnp.where(core == 0, pooled[1][row], pooled[0][row]))


def finish_kernel(pieces_ref, weight_ref, bias_ref):
    order = onehot((EXTRA * BLOCK, 32 * BLOCK), lambda r, c: c == 32 * (r & 31) + MAIN + (r >> 5))
    for half in range(2):
        pieces = pieces_ref[half * BLOCK : (half + 1) * BLOCK]
        for device in range(BLOCK):
            start = half * HALF + device * MAIN
            part = pieces_ref[half * BLOCK + device].astype(jnp.float32)
            weight_ref[start : start + MAIN, :] = part[:MAIN]
        start = half * HALF + MAIN * BLOCK
        weight_ref[start : start + EXTRA * BLOCK, :] = dot(order, pieces.reshape(32 * BLOCK, 128))
    parts = [pieces_ref[device].astype(jnp.float32) for device in range(2)]
    bias_ref[...] = parts[0][27:28] + parts[0][28:29] + (parts[1][27:28] + parts[1][28:29])


def hbm(array):
    return pltpu.with_memory_space_constraint(array, HBM)


def vmem(array):
    return pltpu.with_memory_space_constraint(array, pltpu.VMEM)


def call(kernel, name, outs, operands, in_hbm=0, scratch=(), limit=12, flops=1_000_000):
    specs = [pl.BlockSpec(memory_space=HBM) for _ in range(in_hbm)]
    specs += [pl.BlockSpec(memory_space=pltpu.VMEM) for _ in operands[in_hbm:]]
    operands = [hbm(operand) for operand in operands[:in_hbm]] + list(operands[in_hbm:])
    return pl.pallas_call(
        kernel,
        out_shape=[
            pltpu.VMEM(shape, dtype) if kept else jax.ShapeDtypeStruct(shape, dtype) for shape, dtype, kept in outs
        ],
        in_specs=specs,
        out_specs=[pl.BlockSpec(memory_space=pltpu.VMEM) for _ in outs],
        scratch_shapes=list(scratch),
        compiler_params=pltpu.CompilerParams(vmem_limit_bytes=limit * 1024 * 1024),
        cost_estimate=pl.CostEstimate(flops=flops, bytes_accessed=1_000_000, transcendentals=0),
        name=name,
    )(*operands)


def begin(counts, rebalance, owner, features, adjoint):
    return call(
        begin_kernel,
        "begin",
        [
            ((SLOTS, CH, 128), jnp.bfloat16, False),
            ((8 * BLOCK, 128), jnp.bfloat16, False),
        ],
        (counts, rebalance, owner, features, adjoint),
        in_hbm=5,
        scratch=[
            pltpu.SMEM((SLOTS,), jnp.int32),
            pltpu.SMEM((SLOTS,), jnp.int32),
            pltpu.SMEM((SLOTS,), jnp.int32),
            pltpu.VMEM((SLOTS, CH, VOX), jnp.bfloat16),
            pltpu.VMEM((2, CH * 128), jnp.bfloat16),
            pltpu.VMEM((128, 128), jnp.float32),
            pltpu.SemaphoreType.DMA((5,)),
        ],
    )


def forward(start, *operands):
    in_hbm, in_vmem = pl.BlockSpec(memory_space=HBM), pl.BlockSpec(memory_space=pltpu.VMEM)
    if start == 0:
        pooled, pooled_spec = HBM((2, 64, 128), jnp.float32), in_hbm
    else:
        pooled, pooled_spec = jax.ShapeDtypeStruct((8 * BLOCK, 128), jnp.bfloat16), in_vmem
    return pl.pallas_call(
        functools.partial(forward_kernel, start),
        out_shape=[
            pooled,
            pltpu.VMEM((2, 9 * CH, FRAME), jnp.bfloat16),
            HBM((2, OUT, VOX), jnp.float32),
        ],
        in_specs=[in_vmem if i in (4, 5) else in_hbm for i in range(len(operands))],
        out_specs=[pooled_spec, in_vmem, in_hbm],
        scratch_shapes=[
            pltpu.VMEM((SLOTS, CH, VOX), jnp.bfloat16),
            pltpu.VMEM((SLOTS + 1, CH, VOX), jnp.float32),
            pltpu.VMEM((3 * SLOTS + 1, CH, 128), jnp.bfloat16),
            pltpu.VMEM((2, OUT, VOX), jnp.float32),
            pltpu.VMEM((SLOTS, 64, 128), jnp.float32),
            pltpu.SMEM((SLOTS,), jnp.int32),
            pltpu.SMEM((SLOTS, 26), jnp.int32),
            pltpu.VMEM((1, OUT), jnp.float32),
            pltpu.VMEM((TAP_ROWS, OUT), jnp.bfloat16),
            pltpu.VMEM((3 * OUT, 9 * CH), jnp.bfloat16),
            pltpu.SemaphoreType.DMA((8,)),
            pltpu.SemaphoreType.DMA((3,)),
        ],
        compiler_params=pltpu.CompilerParams(vmem_limit_bytes=16 * 1024 * 1024),
        cost_estimate=pl.CostEstimate(flops=4_000_000_000, bytes_accessed=4_000_000, transcendentals=150_000),
        name="forward",
    )(*[operand if i in (4, 5) else hbm(operand) for i, operand in enumerate(operands)])


def exchange(message, axis):
    return lax.all_to_all(message, axis, 0, 0, tiled=True)


def per_device(
    features,
    counts,
    rebalance,
    neighbors,
    coarse_owner,
    conv_weight,
    convolution_bias_vector,
    merged_adjoint,
):
    narrow, wide = jnp.bfloat16, jnp.float32
    layers, offer = begin(counts, rebalance, coarse_owner, features, merged_adjoint)
    before = lax.ppermute(layers, "b", [(i, i + 1) for i in range(BLOCK - 1)])
    after = lax.ppermute(layers, "b", [(i + 1, i) for i in range(BLOCK - 1)])
    offers = exchange(offer.reshape(BLOCK, 8, 128), "b")
    weight = conv_weight.reshape(TAP_ROWS, OUT)
    bias = convolution_bias_vector.reshape(1, OUT)
    first = forward(0, counts, neighbors, bias, features, before, after, weight)
    offers, first_dense = lax.optimization_barrier((offers.reshape(8 * BLOCK, 128), first[0]))
    message, tags = call(
        spread_kernel,
        "spread",
        [((8, 4 * BLOCK, 128), narrow, False), ((BLOCK, 128), jnp.int32, False)],
        (offers,),
    )
    message, bias = lax.optimization_barrier((message, bias))
    adjoint = exchange(message, "z")
    adjoint = lax.all_gather(adjoint, "c", tiled=True).reshape(64 * BLOCK, 128)
    second = forward(2, counts, neighbors, bias, features, before, after, weight, first_dense)
    (message,) = call(
        choose_kernel,
        "choose",
        [((BLOCK, 16, 128), narrow, False)],
        (tags, adjoint, second[0]),
    )
    rows = exchange(message, "b").reshape(16 * BLOCK, 128)
    stacked = (vmem(first[1]), vmem(second[1]))
    other, grads, bias_part = call(
        other_half_kernel,
        "other_half",
        [((HALF + 8, OUT), wide, False), ((SLOTS, OUT, VOX), narrow, True), ((8, OUT), wide, True)],
        (first[2], second[2]) + stacked + (rows,),
        in_hbm=2,
        scratch=[pltpu.VMEM((SLOTS, OUT, VOX), jnp.float32), pltpu.SemaphoreType.DMA((2,))],
    )
    got = lax.ppermute(other, "c", [(0, 1), (1, 0)])
    (mine,) = call(
        own_half_kernel,
        "own_half",
        [((HALF + 8, OUT), wide, False)],
        (vmem(grads), vmem(bias_part)) + stacked,
        flops=2_000_000_000,
    )
    (message,) = call(share_kernel, "share", [((BLOCK, 32, 128), narrow, False)], (tags, mine, got, rows))
    pieces = exchange(message, "b")
    (message,) = call(over_block_kernel, "over_block", [((24, 64, 128), narrow, False)], (tags, pieces))
    pieces = exchange(message.reshape(8, 192, 128), "z").reshape(24, 64, 128)
    message, pooled_mine, pooled_other = call(
        over_z_kernel,
        "over_z",
        [((BLOCK, 32, 128), narrow, False), ((2, CH, 128), narrow, False), ((2, CH, 128), narrow, False)],
        (pieces,),
    )
    pieces = exchange(message, "b")
    pooled = pooled_mine + lax.ppermute(pooled_other, "c", [(0, 1), (1, 0)])
    pieces = lax.all_gather(pieces, "c", tiled=True)
    weight_total, bias_total = call(
        finish_kernel, "finish", [((TAP_ROWS, OUT), wide, False), ((1, OUT), wide, False)], (pieces,)
    )
    return pooled.reshape(2, CH * 128), weight_total.reshape(27, CH, OUT), bias_total.reshape(OUT)


def solution(mesh):
    chips = Mesh(mesh.devices.reshape(-1, 2, BLOCK), ("z", "c", "b"))
    whole = ("z", "c", "b")
    in_specs = (
        P(whole, None, None),
        P(whole),
        P(whole),
        P(whole, None),
        P(whole),
        P(),
        P(),
        P(whole, None),
    )
    out_specs = (P(whole, None), P(), P())
    return jax.shard_map(
        per_device, mesh=chips, in_specs=in_specs, out_specs=out_specs, check_vma=False
    )
```

```python
import functools

import jax
import jax.numpy as jnp
from jax import lax
from jax.experimental import pallas as pl
from jax.experimental.pallas import tpu as pltpu
from jax.sharding import Mesh
from jax.sharding import PartitionSpec as P

SLOTS = 4
FIRST = 1
CH = 64
OUT = 128
VOX = 512
FRAME = 640
TAP_ROWS = 1728
BLOCK = 32
HALF = TAP_ROWS // 2
MAIN = 24
EXTRA = 3
SHARE = MAIN + EXTRA
ROWS = SHARE + 1
HBM = pltpu.HBM
EDGES = ((-1, -1), (-1, 0), (-1, 1), (0, -1), (0, 0), (0, 1), (1, -1), (1, 0), (1, 1))
SMEM = pltpu.SMEM


def voxel_mask(count):
    lanes = lax.broadcasted_iota(jnp.int32, (1, VOX), 1)
    return ((lanes * 167) & 511) < count


def layer_pair(block):
    lanes = lax.broadcasted_iota(jnp.int32, (CH, 128), 1)
    return pltpu.roll(jnp.where(lanes < 64, block[:, :128], block[:, VOX - 128 :]), 64, 1)


def column_of(ea, eb, ec):
    tap = 9 * (ea + 1) + 3 * (eb + 1) + (ec + 1)
    return tap if tap < 13 else tap - 1


def dot(a, b):
    return jnp.dot(a, b, preferred_element_type=jnp.float32)


def dot_lanes(a, b):
    return lax.dot_general(a, b, (((1,), (1,)), ((), ())), preferred_element_type=jnp.float32)


def grid_of(shape):
    return lax.broadcasted_iota(jnp.int32, shape, 0), lax.broadcasted_iota(jnp.int32, shape, 1)


def onehot(shape, chosen):
    return jnp.where(chosen(*grid_of(shape)), 1.0, 0.0).astype(jnp.bfloat16)


def bf16(array):
    return array.astype(jnp.bfloat16)


def pool_table(voxels_first):
    shape = (VOX, 64) if voxels_first else (64, VOX)
    rows, columns = grid_of(shape)
    voxel, cell = (rows, columns) if voxels_first else (columns, rows)
    index = ((voxel >> 7) << 4) | (((voxel >> 4) & 3) << 2) | ((voxel & 7) >> 1)
    return bf16(jnp.where(index == cell, 0.125, 0.0))


def fetch(pairs, sems):
    copies = [pltpu.make_async_copy(source, target, sems.at[i]) for i, (source, target) in enumerate(pairs)]
    for copy in copies:
        copy.start()
    for copy in copies:
        copy.wait()


def begin_kernel(
    counts_hbm, rebalance_hbm, owner_hbm, features_hbm, adjoint_hbm,
    layers_ref, offer_ref,
    counts_ref, rebalance_ref, owner_ref, features_ref, adjoint_ref, dense_ref, sems,
):
    fetch(
        [
            (counts_hbm, counts_ref),
            (rebalance_hbm, rebalance_ref),
            (owner_hbm, owner_ref),
            (features_hbm, features_ref),
            (adjoint_hbm, adjoint_ref),
        ],
        sems,
    )
    lanes = lax.broadcasted_iota(jnp.int32, (1, 128), 1)
    tags = jnp.zeros((1, 128), jnp.float32)
    for slot in range(SLOTS):
        block = jnp.where(voxel_mask(counts_ref[slot]), features_ref[slot].astype(jnp.float32), 0.0)
        layers_ref[slot] = bf16(layer_pair(block))
        row = rebalance_ref[slot]
        line = jnp.where(row >= 0, (row & (2 * BLOCK - 1)) + 1, 0).astype(jnp.float32)
        owner = jnp.maximum(owner_ref[slot], 0).astype(jnp.float32)
        tags = jnp.where(lanes == slot, line, tags)
        tags = jnp.where(lanes == SLOTS + slot, owner, tags)
    for part in range(64):
        dense_ref[2 * part : 2 * part + 2, :] = adjoint_ref[:, 128 * part : 128 * (part + 1)].astype(jnp.float32)
    order = onehot(
        (8 * BLOCK, 128),
        lambda r, c: ((r & 7) < 4) & (c == 2 * (2 * (r >> 3) + (r & 1)) + ((r >> 1) & 1)),
    )
    rows = lax.broadcasted_iota(jnp.int32, (8 * BLOCK, 128), 0)
    offer_ref[...] = bf16(jnp.where((rows & 7) == 4, tags, dot(order, bf16(dense_ref[...]))))


def spread_kernel(offers_ref, message_ref):
    order = onehot((4 * BLOCK, 8 * BLOCK), lambda r, c: c == 8 * (r >> 2) + (r & 3))
    message_ref[...] = jnp.broadcast_to(bf16(dot(order, offers_ref[...]))[None], message_ref.shape)


def tags_kernel(offers_ref, tags_ref):
    order = onehot((BLOCK, 8 * BLOCK), lambda r, c: c == 8 * r + 4)
    tags_ref[...] = dot(order, offers_ref[...]).astype(jnp.int32)


def place_of(tags_ref, row):
    tags = tags_ref[...]
    rows, lanes = grid_of((BLOCK, 128))
    hit = (tags == 2 * lax.axis_index("b") + row + 1) & (lanes < SLOTS)
    owner = jnp.where(hit, pltpu.roll(tags, 128 - SLOTS, 1), 0).astype(jnp.float32)
    home = jnp.where(hit, rows, 0).astype(jnp.float32)
    return [
        jnp.sum(jnp.sum(value, axis=1, keepdims=True), axis=0, keepdims=True).astype(jnp.int32)[0, 0]
        for value in (home, owner)
    ]


def forward_kernel(start, *refs):
    given, count = (7, FIRST) if start == 0 else (8, SLOTS - FIRST)
    operands, refs = refs[:given], refs[given:]
    pooled_out, stacked_ref, slope_hbm, features_ref, blocks_ref, rims_ref, slope_ref, dense_ref = refs[:8]
    counts_ref, neighbors_ref, bias_ref, taps_ref, weight_ref, sems, out_sems = refs[8:]
    targets = [
        counts_ref,
        neighbors_ref,
        bias_ref,
        features_ref,
        rims_ref.at[pl.ds(0, SLOTS)],
        rims_ref.at[pl.ds(2 * SLOTS, SLOTS)],
        taps_ref,
        dense_ref.at[pl.ds(0, FIRST)],
    ]
    fetch(list(zip(operands, targets)), sems)
    for index in range(SLOTS):
        block = jnp.where(voxel_mask(counts_ref[index]), features_ref[index].astype(jnp.float32), 0.0)
        block = pltpu.roll(block, 64, 1)
        blocks_ref[index] = block
        rims_ref[SLOTS + index] = bf16(block[:, :128])
    blocks_ref[SLOTS] = jnp.zeros((CH, VOX), jnp.float32)
    rims_ref[3 * SLOTS] = jnp.zeros((CH, 128), jnp.bfloat16)
    same = onehot((OUT, OUT), lambda r, c: r == c)
    for part in range(3):
        turned = dot_lanes(same, taps_ref[part * 9 * CH : (part + 1) * 9 * CH, :])
        weight_ref[part * OUT : (part + 1) * OUT, :] = bf16(turned)
    first = ((lax.axis_index("z") * 2 + lax.axis_index("c")) * BLOCK + lax.axis_index("b")) * SLOTS
    rows, columns = grid_of((OUT, OUT))
    bias = jnp.sum(jnp.where(rows == columns, bias_ref[...], 0.0), axis=1, keepdims=True)
    lanes = lax.broadcasted_iota(jnp.int32, (CH, FRAME), 1)
    at_c = lanes & 7
    at_b = (lanes >> 3) & 7

    def moved(array, steps):
        return pltpu.roll(array, (-steps) % FRAME, 1)

    @pl.loop(0, count)
    def _(place):
        slot = start + place

        def rim(ea, eb, ec):
            target = neighbors_ref[slot, column_of(ea, eb, ec)]
            at = jnp.clip(target - (first - SLOTS), 0, 3 * SLOTS - 1)
            return rims_ref[jnp.where(target >= 0, at, 3 * SLOTS)].astype(jnp.float32)

        def inner(eb, ec):
            if eb == 0 and ec == 0:
                return blocks_ref[slot]
            target = neighbors_ref[slot, column_of(0, eb, ec)]
            at = jnp.clip(target - first, 0, SLOTS - 1)
            return blocks_ref[jnp.where(target >= 0, at, SLOTS)]

        def frame(eb, ec):
            low = lax.broadcasted_iota(jnp.int32, (CH, 128), 1) < 64
            block = inner(eb, ec)
            ends = block[:, :128]
            left = jnp.where(low, rim(-1, eb, ec), ends)
            right = jnp.where(low, ends, rim(1, eb, ec))
            return jnp.concatenate([left, block[:, 128:], right], axis=1)

        along_c = {}
        for eb in (-1, 0, 1):
            middle = frame(eb, 0)
            along_c[eb, 0] = middle
            along_c[eb, -1] = jnp.where(at_c == 0, moved(frame(eb, -1), 7), moved(middle, -1))
            along_c[eb, 1] = jnp.where(at_c == 7, moved(frame(eb, 1), -7), moved(middle, 1))
        for index, (eb, ec) in enumerate(EDGES):
            if eb == 0:
                value = along_c[0, ec]
            elif eb < 0:
                value = jnp.where(at_b == 0, moved(along_c[-1, ec], 56), moved(along_c[0, ec], -8))
            else:
                value = jnp.where(at_b == 7, moved(along_c[1, ec], -56), moved(along_c[0, ec], 8))
            stacked_ref[place, index * CH : (index + 1) * CH, :] = value.astype(jnp.bfloat16)

        product = dot(weight_ref[...], stacked_ref[place])
        middle = pltpu.roll(product[OUT : 2 * OUT], FRAME - 64, 1)[:, :VOX]
        preact = product[:OUT, :VOX] + middle + product[2 * OUT :, 128:] + bias
        mask = voxel_mask(counts_ref[slot])
        sigmoid = jax.nn.sigmoid(preact)
        slope = sigmoid * (1.0 + preact * (1.0 - sigmoid))
        slope_ref[place] = jnp.where(mask, slope, 0.0)
        pltpu.make_async_copy(slope_ref.at[place], slope_hbm.at[place], out_sems.at[place]).start()
        activation = jnp.where(mask, preact * sigmoid, 0.0)
        high = activation.astype(jnp.bfloat16)
        low = (activation - high.astype(jnp.float32)).astype(jnp.bfloat16)
        table = pool_table(True)
        cells = bf16(dot(high, table) + dot(low, table))
        even = dot(onehot((64, OUT), lambda r, c: c == 2 * r), cells)
        odd = dot(onehot((64, OUT), lambda r, c: c == 2 * r + 1), cells)
        dense_ref[start + place] = jnp.concatenate([even, odd], axis=1)

    copies = [pltpu.make_async_copy(slope_ref.at[place], slope_hbm.at[place], out_sems.at[place]) for place in range(count)]
    if start == 0:
        copies.append(pltpu.make_async_copy(dense_ref.at[pl.ds(0, FIRST)], pooled_out, out_sems.at[count]))
        copies[count].start()
    else:
        order = onehot((8 * BLOCK, 64 * SLOTS), lambda r, c: c == 64 * ((r & 7) >> 1) + 2 * (r >> 3) + (r & 1))
        pooled_out[...] = bf16(dot(order, bf16(dense_ref[...].reshape(64 * SLOTS, 128))))
    for copy in copies:
        copy.wait()


def choose_kernel(tags_ref, adjoint_ref, pooled_ref, message_ref):
    tags = bf16(tags_ref[...].astype(jnp.float32))
    tags = dot(onehot((8 * BLOCK, BLOCK), lambda r, c: (r >> 3) == c), tags)
    rows, lanes = grid_of((8 * BLOCK, 128))
    slot = (rows & 7) >> 1
    line = jnp.sum(jnp.where(lanes == slot, tags, 0.0), axis=1, keepdims=True).astype(jnp.int32)
    owner = jnp.sum(jnp.where(lanes == slot + SLOTS, tags, 0.0), axis=1, keepdims=True).astype(jnp.int32)
    source = ((owner & 1) * 8 + (owner >> 1)) * (4 * BLOCK) + 2 * (line - 1) + (rows[:, :1] & 1)
    source = jnp.where(line > 0, source, -1)
    lanes = lax.broadcasted_iota(jnp.int32, (8 * BLOCK, 64 * BLOCK), 1)
    cotangent = dot(bf16(jnp.where(lanes == source, 1.0, 0.0)), adjoint_ref[...])
    pooled = pooled_ref[...].astype(jnp.float32)
    message_ref[...] = bf16(
        jnp.concatenate([cotangent.reshape(BLOCK, 8, 128), pooled.reshape(BLOCK, 8, 128)], axis=1)
    )


def add_half(half, total_ref, grads_ref, stacked_refs):
    middle = HALF - 9 * CH
    for slot in range(SLOTS):
        stacked_ref, place = (stacked_refs[0], slot) if slot < FIRST else (stacked_refs[1], slot - FIRST)
        grad = grads_ref[slot]
        wide = jnp.concatenate([grad.astype(jnp.float32), jnp.zeros((OUT, 128), jnp.float32)], axis=1)
        shifted = bf16(pltpu.roll(wide, 64, 1))
        if half == 0:
            side = dot_lanes(stacked_ref[place, :, :VOX], grad)
            inner = dot_lanes(stacked_ref[place, :middle, :], shifted)
            parts = ((0, 9 * CH, side), (9 * CH, HALF, inner))
        else:
            inner = dot_lanes(stacked_ref[place, middle:, :], shifted)
            side = dot_lanes(stacked_ref[place, :, 128:], grad)
            parts = ((0, middle, inner), (middle, HALF, side))
        for low, high, value in parts:
            if slot == 0:
                total_ref[low:high] = value
            else:
                total_ref[low:high] += value


def other_half_kernel(first_slope, second_slope, first_stacked, second_stacked, rows_ref, total_ref, grads_ref, bias_ref):
    order = onehot(
        (64 * SLOTS, 16 * BLOCK),
        lambda r, c: c == 16 * ((r & 63) >> 1) + 2 * (r >> 6) + (r & 1),
    )
    dense = bf16(dot(order, rows_ref[...]))
    table = pool_table(False)
    even = onehot((OUT, 64), lambda r, c: r == 2 * c)
    odd = onehot((OUT, 64), lambda r, c: r == 2 * c + 1)
    bias = jnp.zeros((OUT, 1), jnp.float32)
    for slot in range(SLOTS):
        row = dense[64 * slot : 64 * (slot + 1)]
        cells = dot(even, row[:, :64]) + dot(odd, row[:, 64:])
        slope = first_slope[slot] if slot < FIRST else second_slope[slot - FIRST]
        grad = dot(bf16(cells), table) * slope
        bias += jnp.sum(grad, axis=1, keepdims=True)
        grads_ref[slot] = bf16(grad)
    rows, columns = grid_of((OUT, OUT))
    bias_ref[...] = jnp.sum(jnp.where(rows == columns, bias, 0.0), axis=0, keepdims=True)
    core = lax.axis_index("c")
    for half in range(2):

        @pl.when(core == 1 - half)
        def _():
            add_half(half, total_ref, grads_ref, (first_stacked, second_stacked))


def own_half_kernel(grads_ref, first_stacked, second_stacked, total_ref):
    core = lax.axis_index("c")
    for half in range(2):

        @pl.when(core == half)
        def _():
            add_half(half, total_ref, grads_ref, (first_stacked, second_stacked))


def share_kernel(tags_ref, mine_ref, got_ref, bias_ref, pooled_ref, message_ref):
    total = mine_ref[...] + got_ref[...]
    tags = tags_ref[...].astype(jnp.float32)
    lines = dot_lanes(onehot((8, 128), lambda r, c: c == r), bf16(tags))
    lines = dot(bf16(lines), onehot((BLOCK, 16 * BLOCK), lambda r, c: (c >> 4) == r)).astype(jnp.int32)
    rows, columns = grid_of((8, 16 * BLOCK))
    lines = jnp.where(rows == ((columns >> 1) & 7) - SLOTS, lines, 0).astype(jnp.float32)
    line = jnp.sum(lines, axis=0, keepdims=True).astype(jnp.int32)
    columns = lax.broadcasted_iota(jnp.int32, (1, 16 * BLOCK), 1)
    target = 8 * ((line - 1) >> 1) + EXTRA + 2 * ((line - 1) & 1) + (columns & 1)
    target = jnp.where(line > 0, target, -1)
    rows = lax.broadcasted_iota(jnp.int32, (8 * BLOCK, 16 * BLOCK), 0)
    tail = dot(bf16(jnp.where(rows == target, 1.0, 0.0)), pooled_ref[...])
    extra = onehot(
        (8 * BLOCK, EXTRA * BLOCK), lambda r, c: ((r & 7) < EXTRA) & (c == (r & 7) * BLOCK + (r >> 3))
    )
    tail += dot(extra, bf16(total[MAIN * BLOCK : HALF]))
    bias = bias_ref[...]
    high = bf16(bias).astype(jnp.float32)
    rows = lax.broadcasted_iota(jnp.int32, (8 * BLOCK, 128), 0)
    tail = jnp.where((rows & 7) == 7, jnp.where((rows & 8) == 0, high, bias - high), tail)
    main = total[: MAIN * BLOCK].reshape(BLOCK, MAIN, 128)
    message_ref[...] = bf16(jnp.concatenate([main, tail.reshape(BLOCK, 8, 128)], axis=1))


def over_block_kernel(tags_ref, pieces_ref, message_ref):
    total = jnp.zeros((32, 128), jnp.float32)
    for device in range(BLOCK):
        total += pieces_ref[device].astype(jnp.float32)
    order = onehot(
        (128, 32 * BLOCK),
        lambda r, c: c == 32 * ((r & 63) >> 1) + SHARE + 2 * (r >> 6) + (r & 1),
    )
    pooled = bf16(dot(order, pieces_ref[...].reshape(32 * BLOCK, 128)))
    rows, lanes = grid_of((32, 128))
    total = jnp.where((rows < SHARE) | (rows == 31), total, 0.0)
    high = bf16(total).astype(jnp.float32)
    low = total - high
    owners = [place_of(tags_ref, row)[1] for row in range(2)]
    for z in range(8):
        tag = jnp.zeros((32, 128), jnp.float32)
        for core in range(2):
            for row in range(2):
                here = (rows == 28) & (lanes == core) & (owners[row] == 2 * z + core)
                tag = jnp.where(here, row + 1.0, tag)
        message_ref[3 * z] = bf16(jnp.concatenate([high + tag, low], axis=0))
        message_ref[3 * z + 1] = jnp.zeros((64, 128), jnp.bfloat16)
        message_ref[3 * z + 2] = jnp.zeros((64, 128), jnp.bfloat16)
    for row in range(2):
        message_ref[3 * (owners[row] >> 1) + 1 + (owners[row] & 1)] = pooled[64 * row : 64 * (row + 1)]


def over_z_kernel(pieces_ref, message_ref):
    total = jnp.zeros((32, 128), jnp.float32)
    for z in range(8):
        parts = pieces_ref[3 * z].astype(jnp.float32)
        total += parts[:32] + parts[32:]
    rows = lax.broadcasted_iota(jnp.int32, (32, 128), 0)
    bias = total[31:32]
    high = bf16(bias).astype(jnp.float32)
    part = jnp.where((lax.axis_index("b") & 2) == 0, high, bias - high)
    tile = jnp.where(rows < SHARE, total, part)[:ROWS]
    four = bf16(jnp.concatenate([tile] * 4, axis=0))
    for index in range(BLOCK // 4):
        message_ref[4 * ROWS * index : 4 * ROWS * (index + 1), :] = four


def pick_kernel(pieces_ref, mine_ref, other_ref):
    pooled = [[jnp.zeros((64, 128), jnp.float32) for _ in range(2)] for _ in range(2)]
    for z in range(8):
        tags = pieces_ref[3 * z, 16:32, :].astype(jnp.float32)
        for core in range(2):
            tag = tags[12:13, core : core + 1]
            value = pieces_ref[3 * z + 1 + core].astype(jnp.float32)
            for row in range(2):
                pooled[core][row] += jnp.where(tag == row + 1.0, value, 0.0)
    core = lax.axis_index("c")
    for row in range(2):
        mine_ref[row] = bf16(jnp.where(core == 0, pooled[0][row], pooled[1][row]))
        other_ref[row] = bf16(jnp.where(core == 0, pooled[1][row], pooled[0][row]))


def finish_kernel(pieces_ref, weight_ref, bias_ref):
    order = onehot((EXTRA * BLOCK, ROWS * BLOCK), lambda r, c: c == ROWS * (r & 31) + MAIN + (r >> 5))
    bias = []
    for half in range(2):
        pieces = pieces_ref[half * ROWS * BLOCK : (half + 1) * ROWS * BLOCK, :]
        values = pieces.astype(jnp.float32)
        for device in range(BLOCK):
            start = half * HALF + device * MAIN
            weight_ref[start : start + MAIN, :] = values[ROWS * device : ROWS * device + MAIN]
        start = half * HALF + MAIN * BLOCK
        weight_ref[start : start + EXTRA * BLOCK, :] = dot(order, pieces)
        parts = [values[ROWS * device + SHARE : ROWS * device + SHARE + 1] for device in range(4)]
        bias.append(parts[0] + parts[2] + (parts[1] + parts[3]))
    bias_ref[...] = bias[0] + bias[1]


def hbm(array):
    return pltpu.with_memory_space_constraint(array, HBM)


def vmem(array):
    return pltpu.with_memory_space_constraint(array, pltpu.VMEM)


def call(kernel, name, outs, operands, in_hbm=0, scratch=(), limit=12, flops=1_000_000):
    specs = [pl.BlockSpec(memory_space=HBM) for _ in range(in_hbm)]
    specs += [pl.BlockSpec(memory_space=pltpu.VMEM) for _ in operands[in_hbm:]]
    operands = [hbm(operand) for operand in operands[:in_hbm]] + list(operands[in_hbm:])
    return pl.pallas_call(
        kernel,
        out_shape=[
            pltpu.VMEM(shape, dtype) if kept else jax.ShapeDtypeStruct(shape, dtype) for shape, dtype, kept in outs
        ],
        in_specs=specs,
        out_specs=[pl.BlockSpec(memory_space=pltpu.VMEM) for _ in outs],
        scratch_shapes=list(scratch),
        compiler_params=pltpu.CompilerParams(vmem_limit_bytes=limit * 1024 * 1024),
        cost_estimate=pl.CostEstimate(flops=flops, bytes_accessed=1_000_000, transcendentals=0),
        name=name,
    )(*operands)


def begin(counts, rebalance, owner, features, adjoint):
    return call(
        begin_kernel,
        "begin",
        [
            ((SLOTS, CH, 128), jnp.bfloat16, False),
            ((8 * BLOCK, 128), jnp.bfloat16, False),
        ],
        (counts, rebalance, owner, features, adjoint),
        in_hbm=5,
        scratch=[
            pltpu.SMEM((SLOTS,), jnp.int32),
            pltpu.SMEM((SLOTS,), jnp.int32),
            pltpu.SMEM((SLOTS,), jnp.int32),
            pltpu.VMEM((SLOTS, CH, VOX), jnp.bfloat16),
            pltpu.VMEM((2, CH * 128), jnp.bfloat16),
            pltpu.VMEM((128, 128), jnp.float32),
            pltpu.SemaphoreType.DMA((5,)),
        ],
    )


def forward(start, *operands):
    in_hbm, in_vmem = pl.BlockSpec(memory_space=HBM), pl.BlockSpec(memory_space=pltpu.VMEM)
    count = FIRST if start == 0 else SLOTS - FIRST
    if start == 0:
        pooled, pooled_spec = HBM((FIRST, 64, 128), jnp.float32), in_hbm
    else:
        pooled, pooled_spec = jax.ShapeDtypeStruct((8 * BLOCK, 128), jnp.bfloat16), in_vmem
    return pl.pallas_call(
        functools.partial(forward_kernel, start),
        out_shape=[
            pooled,
            pltpu.VMEM((count, 9 * CH, FRAME), jnp.bfloat16),
            HBM((count, OUT, VOX), jnp.float32),
        ],
        in_specs=[in_vmem if i in (4, 5) else in_hbm for i in range(len(operands))],
        out_specs=[pooled_spec, in_vmem, in_hbm],
        scratch_shapes=[
            pltpu.VMEM((SLOTS, CH, VOX), jnp.bfloat16),
            pltpu.VMEM((SLOTS + 1, CH, VOX), jnp.float32),
            pltpu.VMEM((3 * SLOTS + 1, CH, 128), jnp.bfloat16),
            pltpu.VMEM((count, OUT, VOX), jnp.float32),
            pltpu.VMEM((SLOTS, 64, 128), jnp.float32),
            pltpu.SMEM((SLOTS,), jnp.int32),
            pltpu.SMEM((SLOTS, 26), jnp.int32),
            pltpu.VMEM((1, OUT), jnp.float32),
            pltpu.VMEM((TAP_ROWS, OUT), jnp.bfloat16),
            pltpu.VMEM((3 * OUT, 9 * CH), jnp.bfloat16),
            pltpu.SemaphoreType.DMA((8,)),
            pltpu.SemaphoreType.DMA((count + 1,)),
        ],
        compiler_params=pltpu.CompilerParams(vmem_limit_bytes=16 * 1024 * 1024),
        cost_estimate=pl.CostEstimate(flops=4_000_000_000, bytes_accessed=4_000_000, transcendentals=150_000),
        name="forward",
    )(*[operand if i in (4, 5) else hbm(operand) for i, operand in enumerate(operands)])


def exchange(message, axis):
    return lax.all_to_all(message, axis, 0, 0, tiled=True)


def per_device(
    features,
    counts,
    rebalance,
    neighbors,
    coarse_owner,
    conv_weight,
    convolution_bias_vector,
    merged_adjoint,
):
    narrow, wide = jnp.bfloat16, jnp.float32
    layers, offer = begin(counts, rebalance, coarse_owner, features, merged_adjoint)
    before = lax.ppermute(layers, "b", [(i, i + 1) for i in range(BLOCK - 1)])
    after = lax.ppermute(layers, "b", [(i + 1, i) for i in range(BLOCK - 1)])
    offers = exchange(offer.reshape(BLOCK, 8, 128), "b")
    weight = conv_weight.reshape(TAP_ROWS, OUT)
    bias = convolution_bias_vector.reshape(1, OUT)
    first = forward(0, counts, neighbors, bias, features, before, after, weight)
    offers, first_dense = lax.optimization_barrier((offers.reshape(8 * BLOCK, 128), first[0]))
    (message,) = call(spread_kernel, "spread", [((8, 4 * BLOCK, 128), narrow, False)], (offers,))
    message, bias = lax.optimization_barrier((message, bias))
    adjoint = exchange(message, "z")
    adjoint = lax.all_gather(adjoint, "c", tiled=True).reshape(64 * BLOCK, 128)
    (tags,) = call(tags_kernel, "tags", [((BLOCK, 128), jnp.int32, False)], (offers,))
    second = forward(FIRST, counts, neighbors, bias, features, before, after, weight, first_dense)
    (message,) = call(
        choose_kernel,
        "choose",
        [((BLOCK, 16, 128), narrow, False)],
        (tags, adjoint, second[0]),
    )
    rows = exchange(message, "b").reshape(16 * BLOCK, 128)
    stacked = (vmem(first[1]), vmem(second[1]))
    other, grads, bias_part = call(
        other_half_kernel,
        "other_half",
        [((HALF, OUT), wide, False), ((SLOTS, OUT, VOX), narrow, True), ((1, OUT), wide, True)],
        (vmem(first[2]), vmem(second[2])) + stacked + (rows,),
    )
    got = lax.ppermute(other, "c", [(0, 1), (1, 0)])
    (mine,) = call(
        own_half_kernel,
        "own_half",
        [((HALF, OUT), wide, False)],
        (vmem(grads),) + stacked,
        flops=2_000_000_000,
    )
    (message,) = call(
        share_kernel, "share", [((BLOCK, 32, 128), narrow, False)], (tags, mine, got, vmem(bias_part), rows)
    )
    pieces = exchange(message, "b")
    (message,) = call(over_block_kernel, "over_block", [((24, 64, 128), narrow, False)], (tags, pieces))
    pieces = exchange(message.reshape(8, 192, 128), "z").reshape(24, 64, 128)
    (message,) = call(over_z_kernel, "over_z", [((ROWS * BLOCK, 128), narrow, False)], (pieces,))
    totals = exchange(message.reshape(BLOCK, ROWS // 2, 2, 128), "b")
    pooled_mine, pooled_other = call(
        pick_kernel, "pick", [((2, CH, 128), narrow, False), ((2, CH, 128), narrow, False)], (pieces,)
    )
    pooled = pooled_mine + lax.ppermute(pooled_other, "c", [(0, 1), (1, 0)])
    pieces = lax.all_gather(totals, "c", tiled=True).reshape(2 * ROWS * BLOCK, 128)
    weight_total, bias_total = call(
        finish_kernel, "finish", [((TAP_ROWS, OUT), wide, False), ((1, OUT), wide, False)], (pieces,)
    )
    return pooled.reshape(2, CH * 128), weight_total.reshape(27, CH, OUT), bias_total.reshape(OUT)


def solution(mesh):
    chips = Mesh(mesh.devices.reshape(-1, 2, BLOCK), ("z", "c", "b"))
    whole = ("z", "c", "b")
    in_specs = (
        P(whole, None, None),
        P(whole),
        P(whole),
        P(whole, None),
        P(whole),
        P(),
        P(),
        P(whole, None),
    )
    out_specs = (P(whole, None), P(), P())
    return jax.shard_map(
        per_device, mesh=chips, in_specs=in_specs, out_specs=out_specs, check_vma=False
    )
```

```python
import functools

import jax
import jax.numpy as jnp
from jax import lax
from jax.experimental import pallas as pl
from jax.experimental.pallas import tpu as pltpu
from jax.sharding import Mesh
from jax.sharding import PartitionSpec as P

SLOTS = 4
FIRST = 1
CH = 64
OUT = 128
VOX = 512
FRAME = 640
TAP_ROWS = 1728
BLOCK = 32
HALF = TAP_ROWS // 2
MAIN = 24
EXTRA = 3
SHARE = MAIN + EXTRA
ROWS = SHARE + 1
HBM = pltpu.HBM
EDGES = ((-1, -1), (-1, 0), (-1, 1), (0, -1), (0, 0), (0, 1), (1, -1), (1, 0), (1, 1))
SMEM = pltpu.SMEM


def voxel_mask(count):
    lanes = lax.broadcasted_iota(jnp.int32, (1, VOX), 1)
    return ((lanes * 167) & 511) < count


def layer_pair(block):
    lanes = lax.broadcasted_iota(jnp.int32, (CH, 128), 1)
    return pltpu.roll(jnp.where(lanes < 64, block[:, :128], block[:, VOX - 128 :]), 64, 1)


def column_of(ea, eb, ec):
    tap = 9 * (ea + 1) + 3 * (eb + 1) + (ec + 1)
    return tap if tap < 13 else tap - 1


def dot(a, b):
    return jnp.dot(a, b, preferred_element_type=jnp.float32)


def dot_lanes(a, b):
    return lax.dot_general(a, b, (((1,), (1,)), ((), ())), preferred_element_type=jnp.float32)


def grid_of(shape):
    return lax.broadcasted_iota(jnp.int32, shape, 0), lax.broadcasted_iota(jnp.int32, shape, 1)


def onehot(shape, chosen):
    return jnp.where(chosen(*grid_of(shape)), 1.0, 0.0).astype(jnp.bfloat16)


def bf16(array):
    return array.astype(jnp.bfloat16)


def pool_table(voxels_first):
    shape = (VOX, 64) if voxels_first else (64, VOX)
    rows, columns = grid_of(shape)
    voxel, cell = (rows, columns) if voxels_first else (columns, rows)
    index = ((voxel >> 7) << 4) | (((voxel >> 4) & 3) << 2) | ((voxel & 7) >> 1)
    return bf16(jnp.where(index == cell, 0.125, 0.0))


def fetch(pairs, sems):
    copies = [pltpu.make_async_copy(source, target, sems.at[i]) for i, (source, target) in enumerate(pairs)]
    for copy in copies:
        copy.start()
    for copy in copies:
        copy.wait()


def begin_kernel(
    counts_hbm, rebalance_hbm, owner_hbm, features_hbm, adjoint_hbm,
    layers_ref, offer_ref,
    counts_ref, rebalance_ref, owner_ref, features_ref, adjoint_ref, dense_ref, sems,
):
    fetch(
        [
            (counts_hbm, counts_ref),
            (rebalance_hbm, rebalance_ref),
            (owner_hbm, owner_ref),
            (features_hbm, features_ref),
            (adjoint_hbm, adjoint_ref),
        ],
        sems,
    )
    lanes = lax.broadcasted_iota(jnp.int32, (1, 128), 1)
    tags = jnp.zeros((1, 128), jnp.float32)
    for slot in range(SLOTS):
        block = jnp.where(voxel_mask(counts_ref[slot]), features_ref[slot].astype(jnp.float32), 0.0)
        layers_ref[slot] = bf16(layer_pair(block))
        row = rebalance_ref[slot]
        line = jnp.where(row >= 0, (row & (2 * BLOCK - 1)) + 1, 0).astype(jnp.float32)
        owner = jnp.maximum(owner_ref[slot], 0).astype(jnp.float32)
        tags = jnp.where(lanes == slot, line, tags)
        tags = jnp.where(lanes == SLOTS + slot, owner, tags)
    for part in range(64):
        dense_ref[2 * part : 2 * part + 2, :] = adjoint_ref[:, 128 * part : 128 * (part + 1)].astype(jnp.float32)
    order = onehot(
        (8 * BLOCK, 128),
        lambda r, c: ((r & 7) < 4) & (c == 2 * (2 * (r >> 3) + (r & 1)) + ((r >> 1) & 1)),
    )
    rows = lax.broadcasted_iota(jnp.int32, (8 * BLOCK, 128), 0)
    offer_ref[...] = bf16(jnp.where((rows & 7) == 4, tags, dot(order, bf16(dense_ref[...]))))


def spread_kernel(offers_ref, message_ref):
    order = onehot((4 * BLOCK, 8 * BLOCK), lambda r, c: c == 8 * (r >> 2) + (r & 3))
    message_ref[...] = jnp.broadcast_to(bf16(dot(order, offers_ref[...]))[None], message_ref.shape)


def tags_kernel(offers_ref, tags_ref):
    order = onehot((BLOCK, 8 * BLOCK), lambda r, c: c == 8 * r + 4)
    tags_ref[...] = dot(order, offers_ref[...]).astype(jnp.int32)


def place_of(tags_ref, row):
    tags = tags_ref[...]
    rows, lanes = grid_of((BLOCK, 128))
    hit = (tags == 2 * lax.axis_index("b") + row + 1) & (lanes < SLOTS)
    owner = jnp.where(hit, pltpu.roll(tags, 128 - SLOTS, 1), 0).astype(jnp.float32)
    home = jnp.where(hit, rows, 0).astype(jnp.float32)
    return [
        jnp.sum(jnp.sum(value, axis=1, keepdims=True), axis=0, keepdims=True).astype(jnp.int32)[0, 0]
        for value in (home, owner)
    ]


def forward_kernel(start, *refs):
    given, count = (7, FIRST) if start == 0 else (8, SLOTS - FIRST)
    operands, refs = refs[:given], refs[given:]
    pooled_out, stacked_out, slope_hbm, features_ref, blocks_ref, rims_ref, slope_ref, dense_ref = refs[:8]
    counts_ref, neighbors_ref, bias_ref, taps_ref, weight_ref, sems, out_sems = refs[8:15]
    stacked_ref = refs[15] if start == 0 else stacked_out
    targets = [
        counts_ref,
        neighbors_ref,
        bias_ref,
        features_ref,
        rims_ref.at[pl.ds(0, SLOTS)],
        rims_ref.at[pl.ds(2 * SLOTS, SLOTS)],
        taps_ref,
        dense_ref.at[pl.ds(0, FIRST)],
    ]
    fetch(list(zip(operands, targets)), sems)
    for index in range(SLOTS):
        block = jnp.where(voxel_mask(counts_ref[index]), features_ref[index].astype(jnp.float32), 0.0)
        block = pltpu.roll(block, 64, 1)
        blocks_ref[index] = block
        rims_ref[SLOTS + index] = bf16(block[:, :128])
    blocks_ref[SLOTS] = jnp.zeros((CH, VOX), jnp.float32)
    rims_ref[3 * SLOTS] = jnp.zeros((CH, 128), jnp.bfloat16)
    same = onehot((OUT, OUT), lambda r, c: r == c)
    for part in range(3):
        turned = dot_lanes(same, taps_ref[part * 9 * CH : (part + 1) * 9 * CH, :])
        weight_ref[part * OUT : (part + 1) * OUT, :] = bf16(turned)
    first = ((lax.axis_index("z") * 2 + lax.axis_index("c")) * BLOCK + lax.axis_index("b")) * SLOTS
    rows, columns = grid_of((OUT, OUT))
    bias = jnp.sum(jnp.where(rows == columns, bias_ref[...], 0.0), axis=1, keepdims=True)
    lanes = lax.broadcasted_iota(jnp.int32, (CH, FRAME), 1)
    at_c = lanes & 7
    at_b = (lanes >> 3) & 7

    def moved(array, steps):
        return pltpu.roll(array, (-steps) % FRAME, 1)

    @pl.loop(0, count)
    def _(place):
        slot = start + place

        def rim(ea, eb, ec):
            target = neighbors_ref[slot, column_of(ea, eb, ec)]
            at = jnp.clip(target - (first - SLOTS), 0, 3 * SLOTS - 1)
            return rims_ref[jnp.where(target >= 0, at, 3 * SLOTS)].astype(jnp.float32)

        def inner(eb, ec):
            if eb == 0 and ec == 0:
                return blocks_ref[slot]
            target = neighbors_ref[slot, column_of(0, eb, ec)]
            at = jnp.clip(target - first, 0, SLOTS - 1)
            return blocks_ref[jnp.where(target >= 0, at, SLOTS)]

        def frame(eb, ec):
            low = lax.broadcasted_iota(jnp.int32, (CH, 128), 1) < 64
            block = inner(eb, ec)
            ends = block[:, :128]
            left = jnp.where(low, rim(-1, eb, ec), ends)
            right = jnp.where(low, ends, rim(1, eb, ec))
            return jnp.concatenate([left, block[:, 128:], right], axis=1)

        along_c = {}
        for eb in (-1, 0, 1):
            middle = frame(eb, 0)
            along_c[eb, 0] = middle
            along_c[eb, -1] = jnp.where(at_c == 0, moved(frame(eb, -1), 7), moved(middle, -1))
            along_c[eb, 1] = jnp.where(at_c == 7, moved(frame(eb, 1), -7), moved(middle, 1))
        for index, (eb, ec) in enumerate(EDGES):
            if eb == 0:
                value = along_c[0, ec]
            elif eb < 0:
                value = jnp.where(at_b == 0, moved(along_c[-1, ec], 56), moved(along_c[0, ec], -8))
            else:
                value = jnp.where(at_b == 7, moved(along_c[1, ec], -56), moved(along_c[0, ec], 8))
            stacked_ref[place, index * CH : (index + 1) * CH, :] = value.astype(jnp.bfloat16)

        if start == 0:
            pltpu.make_async_copy(stacked_ref.at[place], stacked_out.at[place], out_sems.at[count + 1 + place]).start()
        product = dot(weight_ref[...], stacked_ref[place])
        middle = pltpu.roll(product[OUT : 2 * OUT], FRAME - 64, 1)[:, :VOX]
        preact = product[:OUT, :VOX] + middle + product[2 * OUT :, 128:] + bias
        mask = voxel_mask(counts_ref[slot])
        sigmoid = jax.nn.sigmoid(preact)
        slope = sigmoid * (1.0 + preact * (1.0 - sigmoid))
        slope_ref[place] = jnp.where(mask, slope, 0.0)
        pltpu.make_async_copy(slope_ref.at[place], slope_hbm.at[place], out_sems.at[place]).start()
        activation = jnp.where(mask, preact * sigmoid, 0.0)
        high = activation.astype(jnp.bfloat16)
        low = (activation - high.astype(jnp.float32)).astype(jnp.bfloat16)
        table = pool_table(True)
        cells = bf16(dot(high, table) + dot(low, table))
        even = dot(onehot((64, OUT), lambda r, c: c == 2 * r), cells)
        odd = dot(onehot((64, OUT), lambda r, c: c == 2 * r + 1), cells)
        dense_ref[start + place] = jnp.concatenate([even, odd], axis=1)

    copies = [pltpu.make_async_copy(slope_ref.at[place], slope_hbm.at[place], out_sems.at[place]) for place in range(count)]
    if start == 0:
        copies.append(pltpu.make_async_copy(dense_ref.at[pl.ds(0, FIRST)], pooled_out, out_sems.at[count]))
        copies[count].start()
        copies += [
            pltpu.make_async_copy(stacked_ref.at[place], stacked_out.at[place], out_sems.at[count + 1 + place])
            for place in range(count)
        ]
    else:
        order = onehot((8 * BLOCK, 64 * SLOTS), lambda r, c: c == 64 * ((r & 7) >> 1) + 2 * (r >> 3) + (r & 1))
        pooled_out[...] = bf16(dot(order, bf16(dense_ref[...].reshape(64 * SLOTS, 128))))
    for copy in copies:
        copy.wait()


def choose_kernel(tags_ref, adjoint_ref, pooled_ref, message_ref):
    tags = bf16(tags_ref[...].astype(jnp.float32))
    tags = dot(onehot((8 * BLOCK, BLOCK), lambda r, c: (r >> 3) == c), tags)
    rows, lanes = grid_of((8 * BLOCK, 128))
    slot = (rows & 7) >> 1
    line = jnp.sum(jnp.where(lanes == slot, tags, 0.0), axis=1, keepdims=True).astype(jnp.int32)
    owner = jnp.sum(jnp.where(lanes == slot + SLOTS, tags, 0.0), axis=1, keepdims=True).astype(jnp.int32)
    source = ((owner & 1) * 8 + (owner >> 1)) * (4 * BLOCK) + 2 * (line - 1) + (rows[:, :1] & 1)
    source = jnp.where(line > 0, source, -1)
    lanes = lax.broadcasted_iota(jnp.int32, (8 * BLOCK, 64 * BLOCK), 1)
    cotangent = dot(bf16(jnp.where(lanes == source, 1.0, 0.0)), adjoint_ref[...])
    pooled = pooled_ref[...].astype(jnp.float32)
    message_ref[...] = bf16(
        jnp.concatenate([cotangent.reshape(BLOCK, 8, 128), pooled.reshape(BLOCK, 8, 128)], axis=1)
    )


def add_half(half, total_ref, grads_ref, stacked_refs):
    middle = HALF - 9 * CH
    for slot in range(SLOTS):
        stacked_ref, place = (stacked_refs[0], slot) if slot < FIRST else (stacked_refs[1], slot - FIRST)
        grad = grads_ref[slot]
        wide = jnp.concatenate([grad.astype(jnp.float32), jnp.zeros((OUT, 128), jnp.float32)], axis=1)
        shifted = bf16(pltpu.roll(wide, 64, 1))
        if half == 0:
            side = dot_lanes(stacked_ref[place, :, :VOX], grad)
            inner = dot_lanes(stacked_ref[place, :middle, :], shifted)
            parts = ((0, 9 * CH, side), (9 * CH, HALF, inner))
        else:
            inner = dot_lanes(stacked_ref[place, middle:, :], shifted)
            side = dot_lanes(stacked_ref[place, :, 128:], grad)
            parts = ((0, middle, inner), (middle, HALF, side))
        for low, high, value in parts:
            if slot == 0:
                total_ref[low:high] = value
            else:
                total_ref[low:high] += value


def other_half_kernel(first_slope, second_slope, first_stacked, second_stacked, rows_ref, total_ref, grads_ref, bias_ref):
    order = onehot(
        (64 * SLOTS, 16 * BLOCK),
        lambda r, c: c == 16 * ((r & 63) >> 1) + 2 * (r >> 6) + (r & 1),
    )
    dense = bf16(dot(order, rows_ref[...]))
    table = pool_table(False)
    even = onehot((OUT, 64), lambda r, c: r == 2 * c)
    odd = onehot((OUT, 64), lambda r, c: r == 2 * c + 1)
    bias = jnp.zeros((OUT, 1), jnp.float32)
    for slot in range(SLOTS):
        row = dense[64 * slot : 64 * (slot + 1)]
        cells = dot(even, row[:, :64]) + dot(odd, row[:, 64:])
        slope = first_slope[slot] if slot < FIRST else second_slope[slot - FIRST]
        grad = dot(bf16(cells), table) * slope
        bias += jnp.sum(grad, axis=1, keepdims=True)
        grads_ref[slot] = bf16(grad)
    rows, columns = grid_of((OUT, OUT))
    bias_ref[...] = jnp.sum(jnp.where(rows == columns, bias, 0.0), axis=0, keepdims=True)
    core = lax.axis_index("c")
    for half in range(2):

        @pl.when(core == 1 - half)
        def _():
            add_half(half, total_ref, grads_ref, (first_stacked, second_stacked))


def own_half_kernel(grads_ref, first_stacked, second_stacked, total_ref):
    core = lax.axis_index("c")
    for half in range(2):

        @pl.when(core == half)
        def _():
            add_half(half, total_ref, grads_ref, (first_stacked, second_stacked))


def share_kernel(tags_ref, mine_ref, got_ref, bias_ref, pooled_ref, message_ref):
    total = mine_ref[...] + got_ref[...]
    tags = tags_ref[...].astype(jnp.float32)
    lines = dot_lanes(onehot((8, 128), lambda r, c: c == r), bf16(tags))
    lines = dot(bf16(lines), onehot((BLOCK, 16 * BLOCK), lambda r, c: (c >> 4) == r)).astype(jnp.int32)
    rows, columns = grid_of((8, 16 * BLOCK))
    lines = jnp.where(rows == ((columns >> 1) & 7) - SLOTS, lines, 0).astype(jnp.float32)
    line = jnp.sum(lines, axis=0, keepdims=True).astype(jnp.int32)
    columns = lax.broadcasted_iota(jnp.int32, (1, 16 * BLOCK), 1)
    target = 8 * ((line - 1) >> 1) + EXTRA + 2 * ((line - 1) & 1) + (columns & 1)
    target = jnp.where(line > 0, target, -1)
    rows = lax.broadcasted_iota(jnp.int32, (8 * BLOCK, 16 * BLOCK), 0)
    tail = dot(bf16(jnp.where(rows == target, 1.0, 0.0)), pooled_ref[...])
    extra = onehot(
        (8 * BLOCK, EXTRA * BLOCK), lambda r, c: ((r & 7) < EXTRA) & (c == (r & 7) * BLOCK + (r >> 3))
    )
    tail += dot(extra, bf16(total[MAIN * BLOCK : HALF]))
    bias = bias_ref[...]
    high = bf16(bias).astype(jnp.float32)
    rows = lax.broadcasted_iota(jnp.int32, (8 * BLOCK, 128), 0)
    tail = jnp.where((rows & 7) == 7, jnp.where((rows & 8) == 0, high, bias - high), tail)
    main = total[: MAIN * BLOCK].reshape(BLOCK, MAIN, 128)
    message_ref[...] = bf16(jnp.concatenate([main, tail.reshape(BLOCK, 8, 128)], axis=1))


def over_block_kernel(tags_ref, pieces_ref, message_ref):
    total = jnp.zeros((32, 128), jnp.float32)
    for device in range(BLOCK):
        total += pieces_ref[device].astype(jnp.float32)
    order = onehot(
        (128, 32 * BLOCK),
        lambda r, c: c == 32 * ((r & 63) >> 1) + SHARE + 2 * (r >> 6) + (r & 1),
    )
    pooled = bf16(dot(order, pieces_ref[...].reshape(32 * BLOCK, 128)))
    rows, lanes = grid_of((32, 128))
    total = jnp.where((rows < SHARE) | (rows == 31), total, 0.0)
    high = bf16(total).astype(jnp.float32)
    low = total - high
    owners = [place_of(tags_ref, row)[1] for row in range(2)]
    for z in range(8):
        tag = jnp.zeros((32, 128), jnp.float32)
        for core in range(2):
            for row in range(2):
                here = (rows == 28) & (lanes == core) & (owners[row] == 2 * z + core)
                tag = jnp.where(here, row + 1.0, tag)
        message_ref[3 * z] = bf16(jnp.concatenate([high + tag, low], axis=0))
        message_ref[3 * z + 1] = jnp.zeros((64, 128), jnp.bfloat16)
        message_ref[3 * z + 2] = jnp.zeros((64, 128), jnp.bfloat16)
    for row in range(2):
        message_ref[3 * (owners[row] >> 1) + 1 + (owners[row] & 1)] = pooled[64 * row : 64 * (row + 1)]


def over_z_kernel(pieces_ref, message_ref):
    total = jnp.zeros((32, 128), jnp.float32)
    for z in range(8):
        parts = pieces_ref[3 * z].astype(jnp.float32)
        total += parts[:32] + parts[32:]
    rows = lax.broadcasted_iota(jnp.int32, (32, 128), 0)
    bias = total[31:32]
    high = bf16(bias).astype(jnp.float32)
    part = jnp.where((lax.axis_index("b") & 2) == 0, high, bias - high)
    tile = jnp.where(rows < SHARE, total, part)[:ROWS]
    four = bf16(jnp.concatenate([tile] * 4, axis=0))
    for index in range(BLOCK // 4):
        message_ref[4 * ROWS * index : 4 * ROWS * (index + 1), :] = four


def pick_kernel(pieces_ref, mine_ref, other_ref):
    pooled = [[jnp.zeros((64, 128), jnp.float32) for _ in range(2)] for _ in range(2)]
    for z in range(8):
        tags = pieces_ref[3 * z, 16:32, :].astype(jnp.float32)
        for core in range(2):
            tag = tags[12:13, core : core + 1]
            value = pieces_ref[3 * z + 1 + core].astype(jnp.float32)
            for row in range(2):
                pooled[core][row] += jnp.where(tag == row + 1.0, value, 0.0)
    core = lax.axis_index("c")
    for row in range(2):
        mine_ref[row] = bf16(jnp.where(core == 0, pooled[0][row], pooled[1][row]))
        other_ref[row] = bf16(jnp.where(core == 0, pooled[1][row], pooled[0][row]))


def finish_kernel(pieces_ref, weight_ref, bias_ref):
    order = onehot((EXTRA * BLOCK, ROWS * BLOCK), lambda r, c: c == ROWS * (r & 31) + MAIN + (r >> 5))
    bias = []
    for half in range(2):
        pieces = pieces_ref[half * ROWS * BLOCK : (half + 1) * ROWS * BLOCK, :]
        values = pieces.astype(jnp.float32)
        for device in range(BLOCK):
            start = half * HALF + device * MAIN
            weight_ref[start : start + MAIN, :] = values[ROWS * device : ROWS * device + MAIN]
        start = half * HALF + MAIN * BLOCK
        weight_ref[start : start + EXTRA * BLOCK, :] = dot(order, pieces)
        parts = [values[ROWS * device + SHARE : ROWS * device + SHARE + 1] for device in range(4)]
        bias.append(parts[0] + parts[2] + (parts[1] + parts[3]))
    bias_ref[...] = bias[0] + bias[1]


def hbm(array):
    return pltpu.with_memory_space_constraint(array, HBM)


def vmem(array):
    return pltpu.with_memory_space_constraint(array, pltpu.VMEM)


def call(kernel, name, outs, operands, in_hbm=0, scratch=(), limit=12, flops=1_000_000):
    specs = [pl.BlockSpec(memory_space=HBM) for _ in range(in_hbm)]
    specs += [pl.BlockSpec(memory_space=pltpu.VMEM) for _ in operands[in_hbm:]]
    operands = [hbm(operand) for operand in operands[:in_hbm]] + list(operands[in_hbm:])
    return pl.pallas_call(
        kernel,
        out_shape=[
            pltpu.VMEM(shape, dtype) if kept else jax.ShapeDtypeStruct(shape, dtype) for shape, dtype, kept in outs
        ],
        in_specs=specs,
        out_specs=[pl.BlockSpec(memory_space=pltpu.VMEM) for _ in outs],
        scratch_shapes=list(scratch),
        compiler_params=pltpu.CompilerParams(vmem_limit_bytes=limit * 1024 * 1024),
        cost_estimate=pl.CostEstimate(flops=flops, bytes_accessed=1_000_000, transcendentals=0),
        name=name,
    )(*operands)


def begin(counts, rebalance, owner, features, adjoint):
    return call(
        begin_kernel,
        "begin",
        [
            ((SLOTS, CH, 128), jnp.bfloat16, False),
            ((8 * BLOCK, 128), jnp.bfloat16, False),
        ],
        (counts, rebalance, owner, features, adjoint),
        in_hbm=5,
        scratch=[
            pltpu.SMEM((SLOTS,), jnp.int32),
            pltpu.SMEM((SLOTS,), jnp.int32),
            pltpu.SMEM((SLOTS,), jnp.int32),
            pltpu.VMEM((SLOTS, CH, VOX), jnp.bfloat16),
            pltpu.VMEM((2, CH * 128), jnp.bfloat16),
            pltpu.VMEM((128, 128), jnp.float32),
            pltpu.SemaphoreType.DMA((5,)),
        ],
    )


def forward(start, *operands):
    in_hbm, in_vmem = pl.BlockSpec(memory_space=HBM), pl.BlockSpec(memory_space=pltpu.VMEM)
    count = FIRST if start == 0 else SLOTS - FIRST
    if start == 0:
        pooled, pooled_spec = HBM((FIRST, 64, 128), jnp.float32), in_hbm
    else:
        pooled, pooled_spec = jax.ShapeDtypeStruct((8 * BLOCK, 128), jnp.bfloat16), in_vmem
    return pl.pallas_call(
        functools.partial(forward_kernel, start),
        out_shape=[
            pooled,
            (HBM if start == 0 else pltpu.VMEM)((count, 9 * CH, FRAME), jnp.bfloat16),
            HBM((count, OUT, VOX), jnp.float32),
        ],
        in_specs=[in_vmem if i in (4, 5) else in_hbm for i in range(len(operands))],
        out_specs=[pooled_spec, in_hbm if start == 0 else in_vmem, in_hbm],
        scratch_shapes=[
            pltpu.VMEM((SLOTS, CH, VOX), jnp.bfloat16),
            pltpu.VMEM((SLOTS + 1, CH, VOX), jnp.float32),
            pltpu.VMEM((3 * SLOTS + 1, CH, 128), jnp.bfloat16),
            pltpu.VMEM((count, OUT, VOX), jnp.float32),
            pltpu.VMEM((SLOTS, 64, 128), jnp.float32),
            pltpu.SMEM((SLOTS,), jnp.int32),
            pltpu.SMEM((SLOTS, 26), jnp.int32),
            pltpu.VMEM((1, OUT), jnp.float32),
            pltpu.VMEM((TAP_ROWS, OUT), jnp.bfloat16),
            pltpu.VMEM((3 * OUT, 9 * CH), jnp.bfloat16),
            pltpu.SemaphoreType.DMA((8,)),
            pltpu.SemaphoreType.DMA((2 * count + 1,)),
        ]
        + [pltpu.VMEM((count, 9 * CH, FRAME), jnp.bfloat16) for _ in range(start == 0)],
        compiler_params=pltpu.CompilerParams(vmem_limit_bytes=16 * 1024 * 1024),
        cost_estimate=pl.CostEstimate(flops=4_000_000_000, bytes_accessed=4_000_000, transcendentals=150_000),
        name="forward",
    )(*[operand if i in (4, 5) else hbm(operand) for i, operand in enumerate(operands)])


def exchange(message, axis):
    return lax.all_to_all(message, axis, 0, 0, tiled=True)


def per_device(
    features,
    counts,
    rebalance,
    neighbors,
    coarse_owner,
    conv_weight,
    convolution_bias_vector,
    merged_adjoint,
):
    narrow, wide = jnp.bfloat16, jnp.float32
    layers, offer = begin(counts, rebalance, coarse_owner, features, merged_adjoint)
    before = lax.ppermute(layers, "b", [(i, i + 1) for i in range(BLOCK - 1)])
    after = lax.ppermute(layers, "b", [(i + 1, i) for i in range(BLOCK - 1)])
    offers = exchange(offer.reshape(BLOCK, 8, 128), "b")
    weight = conv_weight.reshape(TAP_ROWS, OUT)
    bias = convolution_bias_vector.reshape(1, OUT)
    first = forward(0, counts, neighbors, bias, features, before, after, weight)
    offers, first_dense = lax.optimization_barrier((offers.reshape(8 * BLOCK, 128), first[0]))
    (message,) = call(spread_kernel, "spread", [((8, 4 * BLOCK, 128), narrow, False)], (offers,))
    message, bias = lax.optimization_barrier((message, bias))
    adjoint = exchange(message, "z")
    adjoint = lax.all_gather(adjoint, "c", tiled=True).reshape(64 * BLOCK, 128)
    (tags,) = call(tags_kernel, "tags", [((BLOCK, 128), jnp.int32, False)], (offers,))
    second = forward(FIRST, counts, neighbors, bias, features, before, after, weight, first_dense)
    (message,) = call(
        choose_kernel,
        "choose",
        [((BLOCK, 16, 128), narrow, False)],
        (tags, adjoint, second[0]),
    )
    rows = exchange(message, "b").reshape(16 * BLOCK, 128)
    stacked = (vmem(first[1]), vmem(second[1]))
    other, grads, bias_part = call(
        other_half_kernel,
        "other_half",
        [((HALF, OUT), wide, False), ((SLOTS, OUT, VOX), narrow, True), ((1, OUT), wide, True)],
        (vmem(first[2]), vmem(second[2])) + stacked + (rows,),
    )
    got = lax.ppermute(other, "c", [(0, 1), (1, 0)])
    (mine,) = call(
        own_half_kernel,
        "own_half",
        [((HALF, OUT), wide, False)],
        (vmem(grads),) + stacked,
        flops=2_000_000_000,
    )
    (message,) = call(
        share_kernel, "share", [((BLOCK, 32, 128), narrow, False)], (tags, mine, got, vmem(bias_part), rows)
    )
    pieces = exchange(message, "b")
    (message,) = call(over_block_kernel, "over_block", [((24, 64, 128), narrow, False)], (tags, pieces))
    pieces = exchange(message.reshape(8, 192, 128), "z").reshape(24, 64, 128)
    (message,) = call(over_z_kernel, "over_z", [((ROWS * BLOCK, 128), narrow, False)], (pieces,))
    totals = exchange(message.reshape(BLOCK, ROWS // 2, 2, 128), "b")
    pooled_mine, pooled_other = call(
        pick_kernel, "pick", [((2, CH, 128), narrow, False), ((2, CH, 128), narrow, False)], (pieces,)
    )
    pooled = pooled_mine + lax.ppermute(pooled_other, "c", [(0, 1), (1, 0)])
    pieces = lax.all_gather(totals, "c", tiled=True).reshape(2 * ROWS * BLOCK, 128)
    weight_total, bias_total = call(
        finish_kernel, "finish", [((TAP_ROWS, OUT), wide, False), ((1, OUT), wide, False)], (pieces,)
    )
    return pooled.reshape(2, CH * 128), weight_total.reshape(27, CH, OUT), bias_total.reshape(OUT)


def solution(mesh):
    chips = Mesh(mesh.devices.reshape(-1, 2, BLOCK), ("z", "c", "b"))
    whole = ("z", "c", "b")
    in_specs = (
        P(whole, None, None),
        P(whole),
        P(whole),
        P(whole, None),
        P(whole),
        P(),
        P(),
        P(whole, None),
    )
    out_specs = (P(whole, None), P(), P())
    return jax.shard_map(
        per_device, mesh=chips, in_specs=in_specs, out_specs=out_specs, check_vma=False
    )
```

```python
import jax
import jax.numpy as jnp
from jax import lax
from jax.experimental import pallas as pl
from jax.experimental.pallas import tpu as pltpu
from jax.sharding import Mesh
from jax.sharding import PartitionSpec as P

SLOTS = 4
CH = 64
OUT = 128
VOX = 512
FRAME = 640
TAP_ROWS = 1728
BLOCK = 32
HALF = TAP_ROWS // 2
MAIN = 24
EXTRA = 3
SHARE = MAIN + EXTRA
ROWS = SHARE + 1
HBM = pltpu.HBM
EDGES = ((-1, -1), (-1, 0), (-1, 1), (0, -1), (0, 0), (0, 1), (1, -1), (1, 0), (1, 1))
SMEM = pltpu.SMEM


def voxel_mask(count):
    lanes = lax.broadcasted_iota(jnp.int32, (1, VOX), 1)
    return ((lanes * 167) & 511) < count


def layer_pair(block):
    lanes = lax.broadcasted_iota(jnp.int32, (CH, 128), 1)
    return pltpu.roll(jnp.where(lanes < 64, block[:, :128], block[:, VOX - 128 :]), 64, 1)


def column_of(ea, eb, ec):
    tap = 9 * (ea + 1) + 3 * (eb + 1) + (ec + 1)
    return tap if tap < 13 else tap - 1


def dot(a, b):
    return jnp.dot(a, b, preferred_element_type=jnp.float32)


def dot_lanes(a, b):
    return lax.dot_general(a, b, (((1,), (1,)), ((), ())), preferred_element_type=jnp.float32)


def grid_of(shape):
    return lax.broadcasted_iota(jnp.int32, shape, 0), lax.broadcasted_iota(jnp.int32, shape, 1)


def onehot(shape, chosen):
    return jnp.where(chosen(*grid_of(shape)), 1.0, 0.0).astype(jnp.bfloat16)


def bf16(array):
    return array.astype(jnp.bfloat16)


def pool_table(voxels_first):
    shape = (VOX, 64) if voxels_first else (64, VOX)
    rows, columns = grid_of(shape)
    voxel, cell = (rows, columns) if voxels_first else (columns, rows)
    index = ((voxel >> 7) << 4) | (((voxel >> 4) & 3) << 2) | ((voxel & 7) >> 1)
    return bf16(jnp.where(index == cell, 0.125, 0.0))


def fetch(pairs, sems):
    copies = [pltpu.make_async_copy(source, target, sems.at[i]) for i, (source, target) in enumerate(pairs)]
    for copy in copies:
        copy.start()
    for copy in copies:
        copy.wait()


def begin_kernel(
    counts_hbm, rebalance_hbm, owner_hbm, features_hbm, adjoint_hbm,
    layers_ref, offer_ref,
    counts_ref, rebalance_ref, owner_ref, features_ref, adjoint_ref, dense_ref, sems,
):
    fetch(
        [
            (counts_hbm, counts_ref),
            (rebalance_hbm, rebalance_ref),
            (owner_hbm, owner_ref),
            (features_hbm, features_ref),
            (adjoint_hbm, adjoint_ref),
        ],
        sems,
    )
    lanes = lax.broadcasted_iota(jnp.int32, (1, 128), 1)
    tags = jnp.zeros((1, 128), jnp.float32)
    for slot in range(SLOTS):
        block = jnp.where(voxel_mask(counts_ref[slot]), features_ref[slot].astype(jnp.float32), 0.0)
        layers_ref[slot] = bf16(layer_pair(block))
        row = rebalance_ref[slot]
        line = jnp.where(row >= 0, (row & (2 * BLOCK - 1)) + 1, 0).astype(jnp.float32)
        owner = jnp.maximum(owner_ref[slot], 0).astype(jnp.float32)
        tags = jnp.where(lanes == slot, line, tags)
        tags = jnp.where(lanes == SLOTS + slot, owner, tags)
    for part in range(64):
        dense_ref[2 * part : 2 * part + 2, :] = adjoint_ref[:, 128 * part : 128 * (part + 1)].astype(jnp.float32)
    order = onehot(
        (8 * BLOCK, 128),
        lambda r, c: ((r & 7) < 4) & (c == 2 * (2 * (r >> 3) + (r & 1)) + ((r >> 1) & 1)),
    )
    rows = lax.broadcasted_iota(jnp.int32, (8 * BLOCK, 128), 0)
    offer_ref[...] = bf16(jnp.where((rows & 7) == 4, tags, dot(order, bf16(dense_ref[...]))))


def spread_kernel(offers_ref, message_ref):
    order = onehot((4 * BLOCK, 8 * BLOCK), lambda r, c: c == 8 * (r >> 2) + (r & 3))
    message_ref[...] = jnp.broadcast_to(bf16(dot(order, offers_ref[...]))[None], message_ref.shape)


def tags_kernel(offers_ref, tags_ref):
    order = onehot((BLOCK, 8 * BLOCK), lambda r, c: c == 8 * r + 4)
    tags_ref[...] = dot(order, offers_ref[...]).astype(jnp.int32)


def place_of(tags_ref, row):
    tags = tags_ref[...]
    rows, lanes = grid_of((BLOCK, 128))
    hit = (tags == 2 * lax.axis_index("b") + row + 1) & (lanes < SLOTS)
    owner = jnp.where(hit, pltpu.roll(tags, 128 - SLOTS, 1), 0).astype(jnp.float32)
    home = jnp.where(hit, rows, 0).astype(jnp.float32)
    return [
        jnp.sum(jnp.sum(value, axis=1, keepdims=True), axis=0, keepdims=True).astype(jnp.int32)[0, 0]
        for value in (home, owner)
    ]


def forward_kernel(*refs):
    operands, refs = refs[:7], refs[7:]
    pooled_ref, stacked_ref, first_slope, second_slope, features_ref, blocks_ref, rims_ref, slope_ref, dense_ref = refs[:9]
    counts_ref, neighbors_ref, bias_ref, taps_ref, weight_ref, sems, out_sems = refs[9:]
    targets = [
        counts_ref,
        neighbors_ref,
        bias_ref,
        features_ref,
        rims_ref.at[pl.ds(0, SLOTS)],
        rims_ref.at[pl.ds(2 * SLOTS, SLOTS)],
        taps_ref,
    ]
    fetch(list(zip(operands, targets)), sems)
    for index in range(SLOTS):
        block = jnp.where(voxel_mask(counts_ref[index]), features_ref[index].astype(jnp.float32), 0.0)
        block = pltpu.roll(block, 64, 1)
        blocks_ref[index] = block
        rims_ref[SLOTS + index] = bf16(block[:, :128])
    blocks_ref[SLOTS] = jnp.zeros((CH, VOX), jnp.float32)
    rims_ref[3 * SLOTS] = jnp.zeros((CH, 128), jnp.bfloat16)
    same = onehot((OUT, OUT), lambda r, c: r == c)
    for part in range(3):
        turned = dot_lanes(same, taps_ref[part * 9 * CH : (part + 1) * 9 * CH, :])
        weight_ref[part * OUT : (part + 1) * OUT, :] = bf16(turned)
    first = ((lax.axis_index("z") * 2 + lax.axis_index("c")) * BLOCK + lax.axis_index("b")) * SLOTS
    rows, columns = grid_of((OUT, OUT))
    bias = jnp.sum(jnp.where(rows == columns, bias_ref[...], 0.0), axis=1, keepdims=True)
    lanes = lax.broadcasted_iota(jnp.int32, (CH, FRAME), 1)
    at_c = lanes & 7
    at_b = (lanes >> 3) & 7

    def moved(array, steps):
        return pltpu.roll(array, (-steps) % FRAME, 1)

    @pl.loop(0, SLOTS)
    def _(slot):
        def rim(ea, eb, ec):
            target = neighbors_ref[slot, column_of(ea, eb, ec)]
            at = jnp.clip(target - (first - SLOTS), 0, 3 * SLOTS - 1)
            return rims_ref[jnp.where(target >= 0, at, 3 * SLOTS)].astype(jnp.float32)

        def inner(eb, ec):
            if eb == 0 and ec == 0:
                return blocks_ref[slot]
            target = neighbors_ref[slot, column_of(0, eb, ec)]
            at = jnp.clip(target - first, 0, SLOTS - 1)
            return blocks_ref[jnp.where(target >= 0, at, SLOTS)]

        def frame(eb, ec):
            low = lax.broadcasted_iota(jnp.int32, (CH, 128), 1) < 64
            block = inner(eb, ec)
            ends = block[:, :128]
            left = jnp.where(low, rim(-1, eb, ec), ends)
            right = jnp.where(low, ends, rim(1, eb, ec))
            return jnp.concatenate([left, block[:, 128:], right], axis=1)

        along_c = {}
        for eb in (-1, 0, 1):
            middle = frame(eb, 0)
            along_c[eb, 0] = middle
            along_c[eb, -1] = jnp.where(at_c == 0, moved(frame(eb, -1), 7), moved(middle, -1))
            along_c[eb, 1] = jnp.where(at_c == 7, moved(frame(eb, 1), -7), moved(middle, 1))
        for index, (eb, ec) in enumerate(EDGES):
            if eb == 0:
                value = along_c[0, ec]
            elif eb < 0:
                value = jnp.where(at_b == 0, moved(along_c[-1, ec], 56), moved(along_c[0, ec], -8))
            else:
                value = jnp.where(at_b == 7, moved(along_c[1, ec], -56), moved(along_c[0, ec], 8))
            stacked_ref[slot, index * CH : (index + 1) * CH, :] = value.astype(jnp.bfloat16)

        product = dot(weight_ref[...], stacked_ref[slot])
        middle = pltpu.roll(product[OUT : 2 * OUT], FRAME - 64, 1)[:, :VOX]
        preact = product[:OUT, :VOX] + middle + product[2 * OUT :, 128:] + bias
        mask = voxel_mask(counts_ref[slot])
        sigmoid = jax.nn.sigmoid(preact)
        slope = sigmoid * (1.0 + preact * (1.0 - sigmoid))
        slope_ref[slot] = jnp.where(mask, slope, 0.0)

        @pl.when(slot < 1)
        def _():
            pltpu.make_async_copy(slope_ref.at[slot], first_slope.at[slot], out_sems.at[slot]).start()

        @pl.when(slot >= 1)
        def _():
            pltpu.make_async_copy(slope_ref.at[slot], second_slope.at[slot - 1], out_sems.at[slot]).start()

        activation = jnp.where(mask, preact * sigmoid, 0.0)
        high = activation.astype(jnp.bfloat16)
        low = (activation - high.astype(jnp.float32)).astype(jnp.bfloat16)
        table = pool_table(True)
        cells = bf16(dot(high, table) + dot(low, table))
        even = dot(onehot((64, OUT), lambda r, c: c == 2 * r), cells)
        odd = dot(onehot((64, OUT), lambda r, c: c == 2 * r + 1), cells)
        dense_ref[slot] = jnp.concatenate([even, odd], axis=1)

    order = onehot((8 * BLOCK, 64 * SLOTS), lambda r, c: c == 64 * ((r & 7) >> 1) + 2 * (r >> 3) + (r & 1))
    pooled_ref[...] = bf16(dot(order, bf16(dense_ref[...].reshape(64 * SLOTS, 128))))
    for slot in range(SLOTS):
        target = first_slope.at[slot] if slot < 1 else second_slope.at[slot - 1]
        pltpu.make_async_copy(slope_ref.at[slot], target, out_sems.at[slot]).wait()


def choose_kernel(
    first_hbm, second_hbm, tags_ref, adjoint_ref, pooled_ref, message_ref, slope_ref, sems
):
    copies = [
        pltpu.make_async_copy(first_hbm, slope_ref.at[pl.ds(0, 1)], sems.at[0]),
        pltpu.make_async_copy(second_hbm, slope_ref.at[pl.ds(1, SLOTS - 1)], sems.at[1]),
    ]
    for copy in copies:
        copy.start()
    tags = bf16(tags_ref[...].astype(jnp.float32))
    tags = dot(onehot((8 * BLOCK, BLOCK), lambda r, c: (r >> 3) == c), tags)
    rows, lanes = grid_of((8 * BLOCK, 128))
    slot = (rows & 7) >> 1
    line = jnp.sum(jnp.where(lanes == slot, tags, 0.0), axis=1, keepdims=True).astype(jnp.int32)
    owner = jnp.sum(jnp.where(lanes == slot + SLOTS, tags, 0.0), axis=1, keepdims=True).astype(jnp.int32)
    source = ((owner & 1) * 8 + (owner >> 1)) * (4 * BLOCK) + 2 * (line - 1) + (rows[:, :1] & 1)
    source = jnp.where(line > 0, source, -1)
    lanes = lax.broadcasted_iota(jnp.int32, (8 * BLOCK, 64 * BLOCK), 1)
    cotangent = dot(bf16(jnp.where(lanes == source, 1.0, 0.0)), adjoint_ref[...])
    pooled = pooled_ref[...].astype(jnp.float32)
    message_ref[...] = bf16(
        jnp.concatenate([cotangent.reshape(BLOCK, 8, 128), pooled.reshape(BLOCK, 8, 128)], axis=1)
    )
    for copy in copies:
        copy.wait()


def add_half(half, total_ref, grads_ref, stacked_ref):
    middle = HALF - 9 * CH
    for slot in range(SLOTS):
        grad = grads_ref[slot]
        wide = jnp.concatenate([grad.astype(jnp.float32), jnp.zeros((OUT, 128), jnp.float32)], axis=1)
        shifted = bf16(pltpu.roll(wide, 64, 1))
        if half == 0:
            side = dot_lanes(stacked_ref[slot, :, :VOX], grad)
            inner = dot_lanes(stacked_ref[slot, :middle, :], shifted)
            parts = ((0, 9 * CH, side), (9 * CH, HALF, inner))
        else:
            inner = dot_lanes(stacked_ref[slot, middle:, :], shifted)
            side = dot_lanes(stacked_ref[slot, :, 128:], grad)
            parts = ((0, middle, inner), (middle, HALF, side))
        for low, high, value in parts:
            if slot == 0:
                total_ref[low:high] = value
            else:
                total_ref[low:high] += value


def other_half_kernel(slope_ref, stacked_ref, rows_ref, total_ref, grads_ref, bias_ref):
    order = onehot(
        (64 * SLOTS, 16 * BLOCK),
        lambda r, c: c == 16 * ((r & 63) >> 1) + 2 * (r >> 6) + (r & 1),
    )
    dense = bf16(dot(order, rows_ref[...]))
    table = pool_table(False)
    even = onehot((OUT, 64), lambda r, c: r == 2 * c)
    odd = onehot((OUT, 64), lambda r, c: r == 2 * c + 1)
    bias = jnp.zeros((OUT, 1), jnp.float32)
    for slot in range(SLOTS):
        row = dense[64 * slot : 64 * (slot + 1)]
        cells = dot(even, row[:, :64]) + dot(odd, row[:, 64:])
        grad = dot(bf16(cells), table) * slope_ref[slot]
        bias += jnp.sum(grad, axis=1, keepdims=True)
        grads_ref[slot] = bf16(grad)
    rows, columns = grid_of((OUT, OUT))
    bias_ref[...] = jnp.sum(jnp.where(rows == columns, bias, 0.0), axis=0, keepdims=True)
    core = lax.axis_index("c")
    for half in range(2):

        @pl.when(core == 1 - half)
        def _():
            add_half(half, total_ref, grads_ref, stacked_ref)


def own_half_kernel(grads_ref, stacked_ref, total_ref):
    core = lax.axis_index("c")
    for half in range(2):

        @pl.when(core == half)
        def _():
            add_half(half, total_ref, grads_ref, stacked_ref)


def share_kernel(tags_ref, mine_ref, got_ref, bias_ref, pooled_ref, message_ref):
    total = mine_ref[...] + got_ref[...]
    tags = tags_ref[...].astype(jnp.float32)
    lines = dot_lanes(onehot((8, 128), lambda r, c: c == r), bf16(tags))
    lines = dot(bf16(lines), onehot((BLOCK, 16 * BLOCK), lambda r, c: (c >> 4) == r)).astype(jnp.int32)
    rows, columns = grid_of((8, 16 * BLOCK))
    lines = jnp.where(rows == ((columns >> 1) & 7) - SLOTS, lines, 0).astype(jnp.float32)
    line = jnp.sum(lines, axis=0, keepdims=True).astype(jnp.int32)
    columns = lax.broadcasted_iota(jnp.int32, (1, 16 * BLOCK), 1)
    target = 8 * ((line - 1) >> 1) + EXTRA + 2 * ((line - 1) & 1) + (columns & 1)
    target = jnp.where(line > 0, target, -1)
    rows = lax.broadcasted_iota(jnp.int32, (8 * BLOCK, 16 * BLOCK), 0)
    tail = dot(bf16(jnp.where(rows == target, 1.0, 0.0)), pooled_ref[...])
    extra = onehot(
        (8 * BLOCK, EXTRA * BLOCK), lambda r, c: ((r & 7) < EXTRA) & (c == (r & 7) * BLOCK + (r >> 3))
    )
    tail += dot(extra, bf16(total[MAIN * BLOCK : HALF]))
    bias = bias_ref[...]
    high = bf16(bias).astype(jnp.float32)
    rows = lax.broadcasted_iota(jnp.int32, (8 * BLOCK, 128), 0)
    tail = jnp.where((rows & 7) == 7, jnp.where((rows & 8) == 0, high, bias - high), tail)
    main = total[: MAIN * BLOCK].reshape(BLOCK, MAIN, 128)
    message_ref[...] = bf16(jnp.concatenate([main, tail.reshape(BLOCK, 8, 128)], axis=1))


def over_block_kernel(tags_ref, pieces_ref, message_ref):
    total = jnp.zeros((32, 128), jnp.float32)
    for device in range(BLOCK):
        total += pieces_ref[device].astype(jnp.float32)
    order = onehot(
        (128, 32 * BLOCK),
        lambda r, c: c == 32 * ((r & 63) >> 1) + SHARE + 2 * (r >> 6) + (r & 1),
    )
    pooled = bf16(dot(order, pieces_ref[...].reshape(32 * BLOCK, 128)))
    rows, lanes = grid_of((32, 128))
    total = jnp.where((rows < SHARE) | (rows == 31), total, 0.0)
    high = bf16(total).astype(jnp.float32)
    low = total - high
    owners = [place_of(tags_ref, row)[1] for row in range(2)]
    for z in range(8):
        tag = jnp.zeros((32, 128), jnp.float32)
        for core in range(2):
            for row in range(2):
                here = (rows == 28) & (lanes == core) & (owners[row] == 2 * z + core)
                tag = jnp.where(here, row + 1.0, tag)
        message_ref[3 * z] = bf16(jnp.concatenate([high + tag, low], axis=0))
        message_ref[3 * z + 1] = jnp.zeros((64, 128), jnp.bfloat16)
        message_ref[3 * z + 2] = jnp.zeros((64, 128), jnp.bfloat16)
    for row in range(2):
        message_ref[3 * (owners[row] >> 1) + 1 + (owners[row] & 1)] = pooled[64 * row : 64 * (row + 1)]


def over_z_kernel(pieces_ref, message_ref):
    total = jnp.zeros((32, 128), jnp.float32)
    for z in range(8):
        parts = pieces_ref[3 * z].astype(jnp.float32)
        total += parts[:32] + parts[32:]
    rows = lax.broadcasted_iota(jnp.int32, (32, 128), 0)
    bias = total[31:32]
    high = bf16(bias).astype(jnp.float32)
    part = jnp.where((lax.axis_index("b") & 2) == 0, high, bias - high)
    tile = jnp.where(rows < SHARE, total, part)[:ROWS]
    four = bf16(jnp.concatenate([tile] * 4, axis=0))
    for index in range(BLOCK // 4):
        message_ref[4 * ROWS * index : 4 * ROWS * (index + 1), :] = four


def pick_kernel(pieces_ref, mine_ref, other_ref):
    pooled = [[jnp.zeros((64, 128), jnp.float32) for _ in range(2)] for _ in range(2)]
    for z in range(8):
        tags = pieces_ref[3 * z, 16:32, :].astype(jnp.float32)
        for core in range(2):
            tag = tags[12:13, core : core + 1]
            value = pieces_ref[3 * z + 1 + core].astype(jnp.float32)
            for row in range(2):
                pooled[core][row] += jnp.where(tag == row + 1.0, value, 0.0)
    core = lax.axis_index("c")
    for row in range(2):
        mine_ref[row] = bf16(jnp.where(core == 0, pooled[0][row], pooled[1][row]))
        other_ref[row] = bf16(jnp.where(core == 0, pooled[1][row], pooled[0][row]))


def finish_kernel(pieces_ref, weight_ref, bias_ref):
    order = onehot((EXTRA * BLOCK, ROWS * BLOCK), lambda r, c: c == ROWS * (r & 31) + MAIN + (r >> 5))
    bias = []
    for half in range(2):
        pieces = pieces_ref[half * ROWS * BLOCK : (half + 1) * ROWS * BLOCK, :]
        values = pieces.astype(jnp.float32)
        for device in range(BLOCK):
            start = half * HALF + device * MAIN
            weight_ref[start : start + MAIN, :] = values[ROWS * device : ROWS * device + MAIN]
        start = half * HALF + MAIN * BLOCK
        weight_ref[start : start + EXTRA * BLOCK, :] = dot(order, pieces)
        parts = [values[ROWS * device + SHARE : ROWS * device + SHARE + 1] for device in range(4)]
        bias.append(parts[0] + parts[2] + (parts[1] + parts[3]))
    bias_ref[...] = bias[0] + bias[1]


def hbm(array):
    return pltpu.with_memory_space_constraint(array, HBM)


def vmem(array):
    return pltpu.with_memory_space_constraint(array, pltpu.VMEM)


def call(kernel, name, outs, operands, in_hbm=0, scratch=(), limit=12, flops=1_000_000):
    specs = [pl.BlockSpec(memory_space=HBM) for _ in range(in_hbm)]
    specs += [pl.BlockSpec(memory_space=pltpu.VMEM) for _ in operands[in_hbm:]]
    operands = [hbm(operand) for operand in operands[:in_hbm]] + list(operands[in_hbm:])
    return pl.pallas_call(
        kernel,
        out_shape=[
            pltpu.VMEM(shape, dtype) if kept else jax.ShapeDtypeStruct(shape, dtype) for shape, dtype, kept in outs
        ],
        in_specs=specs,
        out_specs=[pl.BlockSpec(memory_space=pltpu.VMEM) for _ in outs],
        scratch_shapes=list(scratch),
        compiler_params=pltpu.CompilerParams(vmem_limit_bytes=limit * 1024 * 1024),
        cost_estimate=pl.CostEstimate(flops=flops, bytes_accessed=1_000_000, transcendentals=0),
        name=name,
    )(*operands)


def begin(counts, rebalance, owner, features, adjoint):
    return call(
        begin_kernel,
        "begin",
        [
            ((SLOTS, CH, 128), jnp.bfloat16, False),
            ((8 * BLOCK, 128), jnp.bfloat16, False),
        ],
        (counts, rebalance, owner, features, adjoint),
        in_hbm=5,
        scratch=[
            pltpu.SMEM((SLOTS,), jnp.int32),
            pltpu.SMEM((SLOTS,), jnp.int32),
            pltpu.SMEM((SLOTS,), jnp.int32),
            pltpu.VMEM((SLOTS, CH, VOX), jnp.bfloat16),
            pltpu.VMEM((2, CH * 128), jnp.bfloat16),
            pltpu.VMEM((128, 128), jnp.float32),
            pltpu.SemaphoreType.DMA((5,)),
        ],
    )


def forward(*operands):
    in_hbm, in_vmem = pl.BlockSpec(memory_space=HBM), pl.BlockSpec(memory_space=pltpu.VMEM)
    return pl.pallas_call(
        forward_kernel,
        out_shape=[
            jax.ShapeDtypeStruct((8 * BLOCK, 128), jnp.bfloat16),
            pltpu.VMEM((SLOTS, 9 * CH, FRAME), jnp.bfloat16),
            HBM((1, OUT, VOX), jnp.float32),
            HBM((SLOTS - 1, OUT, VOX), jnp.float32),
        ],
        in_specs=[in_vmem if i in (4, 5) else in_hbm for i in range(len(operands))],
        out_specs=[in_vmem, in_vmem, in_hbm, in_hbm],
        scratch_shapes=[
            pltpu.VMEM((SLOTS, CH, VOX), jnp.bfloat16),
            pltpu.VMEM((SLOTS + 1, CH, VOX), jnp.float32),
            pltpu.VMEM((3 * SLOTS + 1, CH, 128), jnp.bfloat16),
            pltpu.VMEM((SLOTS, OUT, VOX), jnp.float32),
            pltpu.VMEM((SLOTS, 64, 128), jnp.float32),
            pltpu.SMEM((SLOTS,), jnp.int32),
            pltpu.SMEM((SLOTS, 26), jnp.int32),
            pltpu.VMEM((1, OUT), jnp.float32),
            pltpu.VMEM((TAP_ROWS, OUT), jnp.bfloat16),
            pltpu.VMEM((3 * OUT, 9 * CH), jnp.bfloat16),
            pltpu.SemaphoreType.DMA((7,)),
            pltpu.SemaphoreType.DMA((SLOTS,)),
        ],
        compiler_params=pltpu.CompilerParams(vmem_limit_bytes=16 * 1024 * 1024),
        cost_estimate=pl.CostEstimate(flops=40_000_000_000, bytes_accessed=4_000_000, transcendentals=300_000),
        name="forward",
    )(*[operand if i in (4, 5) else hbm(operand) for i, operand in enumerate(operands)])


def exchange(message, axis):
    return lax.all_to_all(message, axis, 0, 0, tiled=True)


def per_device(
    features,
    counts,
    rebalance,
    neighbors,
    coarse_owner,
    conv_weight,
    convolution_bias_vector,
    merged_adjoint,
):
    narrow, wide = jnp.bfloat16, jnp.float32
    layers, offer = begin(counts, rebalance, coarse_owner, features, merged_adjoint)
    offers = exchange(offer.reshape(BLOCK, 8, 128), "b")
    before = lax.ppermute(layers, "b", [(i, i + 1) for i in range(BLOCK - 1)])
    after = lax.ppermute(layers, "b", [(i + 1, i) for i in range(BLOCK - 1)])
    offers = offers.reshape(8 * BLOCK, 128)
    (message,) = call(spread_kernel, "spread", [((8, 4 * BLOCK, 128), narrow, False)], (offers,))
    bias = convolution_bias_vector.reshape(1, OUT)
    message, bias = lax.optimization_barrier((message, bias))
    adjoint = exchange(message, "z")
    adjoint = lax.all_gather(adjoint, "c", tiled=True).reshape(64 * BLOCK, 128)
    (tags,) = call(tags_kernel, "tags", [((BLOCK, 128), jnp.int32, False)], (offers,))
    weight = conv_weight.reshape(TAP_ROWS, OUT)
    pooled, stacked, *slopes = forward(counts, neighbors, bias, features, before, after, weight)
    message, slope = call(
        choose_kernel,
        "choose",
        [((BLOCK, 16, 128), narrow, False), ((SLOTS, OUT, VOX), wide, True)],
        (slopes[0], slopes[1], tags, adjoint, pooled),
        in_hbm=2,
        scratch=[pltpu.SemaphoreType.DMA((2,))],
    )
    rows = exchange(message, "b").reshape(16 * BLOCK, 128)
    other, grads, bias_part = call(
        other_half_kernel,
        "other_half",
        [((HALF, OUT), wide, False), ((SLOTS, OUT, VOX), narrow, True), ((1, OUT), wide, True)],
        (vmem(slope), vmem(stacked), rows),
    )
    got = lax.ppermute(other, "c", [(0, 1), (1, 0)])
    (mine,) = call(
        own_half_kernel,
        "own_half",
        [((HALF, OUT), wide, False)],
        (vmem(grads), vmem(stacked)),
        flops=2_000_000_000,
    )
    (message,) = call(
        share_kernel, "share", [((BLOCK, 32, 128), narrow, False)], (tags, mine, got, vmem(bias_part), rows)
    )
    pieces = exchange(message, "b")
    (message,) = call(over_block_kernel, "over_block", [((24, 64, 128), narrow, False)], (tags, pieces))
    pieces = exchange(message.reshape(8, 192, 128), "z").reshape(24, 64, 128)
    (message,) = call(over_z_kernel, "over_z", [((ROWS * BLOCK, 128), narrow, False)], (pieces,))
    totals = exchange(message.reshape(BLOCK, ROWS // 2, 2, 128), "b")
    pooled_mine, pooled_other = call(
        pick_kernel, "pick", [((2, CH, 128), narrow, False), ((2, CH, 128), narrow, False)], (pieces,)
    )
    pooled = pooled_mine + lax.ppermute(pooled_other, "c", [(0, 1), (1, 0)])
    pieces = lax.all_gather(totals, "c", tiled=True).reshape(2 * ROWS * BLOCK, 128)
    weight_total, bias_total = call(
        finish_kernel, "finish", [((TAP_ROWS, OUT), wide, False), ((1, OUT), wide, False)], (pieces,)
    )
    return pooled.reshape(2, CH * 128), weight_total.reshape(27, CH, OUT), bias_total.reshape(OUT)


def solution(mesh):
    chips = Mesh(mesh.devices.reshape(-1, 2, BLOCK), ("z", "c", "b"))
    whole = ("z", "c", "b")
    in_specs = (
        P(whole, None, None),
        P(whole),
        P(whole),
        P(whole, None),
        P(whole),
        P(),
        P(),
        P(whole, None),
    )
    out_specs = (P(whole, None), P(), P())
    return jax.shard_map(
        per_device, mesh=chips, in_specs=in_specs, out_specs=out_specs, check_vma=False
    )
```

```python
import jax
import jax.numpy as jnp
from jax import lax
from jax.experimental import pallas as pl
from jax.experimental.pallas import tpu as pltpu
from jax.sharding import Mesh
from jax.sharding import PartitionSpec as P

SLOTS = 4
CH = 64
OUT = 128
VOX = 512
FRAME = 640
TAP_ROWS = 1728
BLOCK = 32
HALF = TAP_ROWS // 2
MAIN = 24
EXTRA = 3
SHARE = MAIN + EXTRA
ROWS = SHARE + 1
HBM = pltpu.HBM
EDGES = ((-1, -1), (-1, 0), (-1, 1), (0, -1), (0, 0), (0, 1), (1, -1), (1, 0), (1, 1))
SMEM = pltpu.SMEM


def voxel_mask(count):
    lanes = lax.broadcasted_iota(jnp.int32, (1, VOX), 1)
    return ((lanes * 167) & 511) < count


def layer_pair(block):
    lanes = lax.broadcasted_iota(jnp.int32, (CH, 128), 1)
    return pltpu.roll(jnp.where(lanes < 64, block[:, :128], block[:, VOX - 128 :]), 64, 1)


def column_of(ea, eb, ec):
    tap = 9 * (ea + 1) + 3 * (eb + 1) + (ec + 1)
    return tap if tap < 13 else tap - 1


def dot(a, b):
    return jnp.dot(a, b, preferred_element_type=jnp.float32)


def dot_lanes(a, b):
    return lax.dot_general(a, b, (((1,), (1,)), ((), ())), preferred_element_type=jnp.float32)


def grid_of(shape):
    return lax.broadcasted_iota(jnp.int32, shape, 0), lax.broadcasted_iota(jnp.int32, shape, 1)


def onehot(shape, chosen):
    return jnp.where(chosen(*grid_of(shape)), 1.0, 0.0).astype(jnp.bfloat16)


def bf16(array):
    return array.astype(jnp.bfloat16)


def pool_table(voxels_first):
    shape = (VOX, 64) if voxels_first else (64, VOX)
    rows, columns = grid_of(shape)
    voxel, cell = (rows, columns) if voxels_first else (columns, rows)
    index = ((voxel >> 7) << 4) | (((voxel >> 4) & 3) << 2) | ((voxel & 7) >> 1)
    return bf16(jnp.where(index == cell, 0.125, 0.0))


def fetch(pairs, sems):
    copies = [pltpu.make_async_copy(source, target, sems.at[i]) for i, (source, target) in enumerate(pairs)]
    for copy in copies:
        copy.start()
    for copy in copies:
        copy.wait()


def begin_kernel(
    counts_hbm, rebalance_hbm, owner_hbm, features_hbm, adjoint_hbm,
    layers_ref, offer_ref,
    counts_ref, rebalance_ref, owner_ref, features_ref, adjoint_ref, dense_ref, sems,
):
    fetch(
        [
            (counts_hbm, counts_ref),
            (rebalance_hbm, rebalance_ref),
            (owner_hbm, owner_ref),
            (features_hbm, features_ref),
            (adjoint_hbm, adjoint_ref),
        ],
        sems,
    )
    lanes = lax.broadcasted_iota(jnp.int32, (1, 128), 1)
    tags = jnp.zeros((1, 128), jnp.float32)
    for slot in range(SLOTS):
        block = jnp.where(voxel_mask(counts_ref[slot]), features_ref[slot].astype(jnp.float32), 0.0)
        layers_ref[slot] = bf16(layer_pair(block))
        row = rebalance_ref[slot]
        line = jnp.where(row >= 0, (row & (2 * BLOCK - 1)) + 1, 0).astype(jnp.float32)
        owner = jnp.maximum(owner_ref[slot], 0).astype(jnp.float32)
        tags = jnp.where(lanes == slot, line, tags)
        tags = jnp.where(lanes == SLOTS + slot, owner, tags)
    for part in range(64):
        dense_ref[2 * part : 2 * part + 2, :] = adjoint_ref[:, 128 * part : 128 * (part + 1)].astype(jnp.float32)
    order = onehot(
        (8 * BLOCK, 128),
        lambda r, c: ((r & 7) < 4) & (c == 2 * (2 * (r >> 3) + (r & 1)) + ((r >> 1) & 1)),
    )
    rows = lax.broadcasted_iota(jnp.int32, (8 * BLOCK, 128), 0)
    offer_ref[...] = bf16(jnp.where((rows & 7) == 4, tags, dot(order, bf16(dense_ref[...]))))


def spread_kernel(offers_ref, message_ref):
    order = onehot((4 * BLOCK, 8 * BLOCK), lambda r, c: c == 8 * (r >> 2) + (r & 3))
    message_ref[...] = jnp.broadcast_to(bf16(dot(order, offers_ref[...]))[None], message_ref.shape)


def tags_kernel(offers_ref, tags_ref):
    order = onehot((BLOCK, 8 * BLOCK), lambda r, c: c == 8 * r + 4)
    tags_ref[...] = dot(order, offers_ref[...]).astype(jnp.int32)


def place_of(tags_ref, row):
    tags = tags_ref[...]
    rows, lanes = grid_of((BLOCK, 128))
    hit = (tags == 2 * lax.axis_index("b") + row + 1) & (lanes < SLOTS)
    owner = jnp.where(hit, pltpu.roll(tags, 128 - SLOTS, 1), 0).astype(jnp.float32)
    home = jnp.where(hit, rows, 0).astype(jnp.float32)
    return [
        jnp.sum(jnp.sum(value, axis=1, keepdims=True), axis=0, keepdims=True).astype(jnp.int32)[0, 0]
        for value in (home, owner)
    ]


def forward_kernel(*refs):
    operands, refs = refs[:7], refs[7:]
    pooled_ref, first_stacked, second_stacked, slope_hbm, features_ref, blocks_ref, rims_ref, slope_ref = refs[:8]
    dense_ref, first_ref, counts_ref, neighbors_ref, bias_ref, taps_ref, weight_ref, sems, out_sems = refs[8:]
    targets = [
        counts_ref,
        neighbors_ref,
        bias_ref,
        features_ref,
        rims_ref.at[pl.ds(0, SLOTS)],
        rims_ref.at[pl.ds(2 * SLOTS, SLOTS)],
        taps_ref,
    ]
    fetch(list(zip(operands, targets)), sems)
    for index in range(SLOTS):
        block = jnp.where(voxel_mask(counts_ref[index]), features_ref[index].astype(jnp.float32), 0.0)
        block = pltpu.roll(block, 64, 1)
        blocks_ref[index] = block
        rims_ref[SLOTS + index] = bf16(block[:, :128])
    blocks_ref[SLOTS] = jnp.zeros((CH, VOX), jnp.float32)
    rims_ref[3 * SLOTS] = jnp.zeros((CH, 128), jnp.bfloat16)
    same = onehot((OUT, OUT), lambda r, c: r == c)
    for part in range(3):
        turned = dot_lanes(same, taps_ref[part * 9 * CH : (part + 1) * 9 * CH, :])
        weight_ref[part * OUT : (part + 1) * OUT, :] = bf16(turned)
    first = ((lax.axis_index("z") * 2 + lax.axis_index("c")) * BLOCK + lax.axis_index("b")) * SLOTS
    rows, columns = grid_of((OUT, OUT))
    bias = jnp.sum(jnp.where(rows == columns, bias_ref[...], 0.0), axis=1, keepdims=True)
    lanes = lax.broadcasted_iota(jnp.int32, (CH, FRAME), 1)
    at_c = lanes & 7
    at_b = (lanes >> 3) & 7

    def moved(array, steps):
        return pltpu.roll(array, (-steps) % FRAME, 1)

    def one(slot, stacked_ref, place):
        def rim(ea, eb, ec):
            target = neighbors_ref[slot, column_of(ea, eb, ec)]
            at = jnp.clip(target - (first - SLOTS), 0, 3 * SLOTS - 1)
            return rims_ref[jnp.where(target >= 0, at, 3 * SLOTS)].astype(jnp.float32)

        def inner(eb, ec):
            if eb == 0 and ec == 0:
                return blocks_ref[slot]
            target = neighbors_ref[slot, column_of(0, eb, ec)]
            at = jnp.clip(target - first, 0, SLOTS - 1)
            return blocks_ref[jnp.where(target >= 0, at, SLOTS)]

        def frame(eb, ec):
            low = lax.broadcasted_iota(jnp.int32, (CH, 128), 1) < 64
            block = inner(eb, ec)
            ends = block[:, :128]
            left = jnp.where(low, rim(-1, eb, ec), ends)
            right = jnp.where(low, ends, rim(1, eb, ec))
            return jnp.concatenate([left, block[:, 128:], right], axis=1)

        along_c = {}
        for eb in (-1, 0, 1):
            middle = frame(eb, 0)
            along_c[eb, 0] = middle
            along_c[eb, -1] = jnp.where(at_c == 0, moved(frame(eb, -1), 7), moved(middle, -1))
            along_c[eb, 1] = jnp.where(at_c == 7, moved(frame(eb, 1), -7), moved(middle, 1))
        for index, (eb, ec) in enumerate(EDGES):
            if eb == 0:
                value = along_c[0, ec]
            elif eb < 0:
                value = jnp.where(at_b == 0, moved(along_c[-1, ec], 56), moved(along_c[0, ec], -8))
            else:
                value = jnp.where(at_b == 7, moved(along_c[1, ec], -56), moved(along_c[0, ec], 8))
            stacked_ref[place, index * CH : (index + 1) * CH, :] = value.astype(jnp.bfloat16)

        product = dot(weight_ref[...], stacked_ref[place])
        middle = pltpu.roll(product[OUT : 2 * OUT], FRAME - 64, 1)[:, :VOX]
        preact = product[:OUT, :VOX] + middle + product[2 * OUT :, 128:] + bias
        mask = voxel_mask(counts_ref[slot])
        sigmoid = jax.nn.sigmoid(preact)
        slope = sigmoid * (1.0 + preact * (1.0 - sigmoid))
        slope_ref[slot] = jnp.where(mask, slope, 0.0)

        pltpu.make_async_copy(slope_ref.at[slot], slope_hbm.at[slot], out_sems.at[slot]).start()
        activation = jnp.where(mask, preact * sigmoid, 0.0)
        high = activation.astype(jnp.bfloat16)
        low = (activation - high.astype(jnp.float32)).astype(jnp.bfloat16)
        table = pool_table(True)
        cells = bf16(dot(high, table) + dot(low, table))
        even = dot(onehot((64, OUT), lambda r, c: c == 2 * r), cells)
        odd = dot(onehot((64, OUT), lambda r, c: c == 2 * r + 1), cells)
        dense_ref[slot] = jnp.concatenate([even, odd], axis=1)

    one(0, first_ref, 0)
    frames = pltpu.make_async_copy(first_ref, first_stacked, out_sems.at[SLOTS])
    frames.start()

    @pl.loop(1, SLOTS)
    def _(slot):
        one(slot, second_stacked, slot - 1)

    order = onehot((8 * BLOCK, 64 * SLOTS), lambda r, c: c == 64 * ((r & 7) >> 1) + 2 * (r >> 3) + (r & 1))
    pooled_ref[...] = bf16(dot(order, bf16(dense_ref[...].reshape(64 * SLOTS, 128))))
    for slot in range(SLOTS):
        pltpu.make_async_copy(slope_ref.at[slot], slope_hbm.at[slot], out_sems.at[slot]).wait()
    frames.wait()


def choose_kernel(tags_ref, adjoint_ref, pooled_ref, message_ref):
    tags = bf16(tags_ref[...].astype(jnp.float32))
    tags = dot(onehot((8 * BLOCK, BLOCK), lambda r, c: (r >> 3) == c), tags)
    rows, lanes = grid_of((8 * BLOCK, 128))
    slot = (rows & 7) >> 1
    line = jnp.sum(jnp.where(lanes == slot, tags, 0.0), axis=1, keepdims=True).astype(jnp.int32)
    owner = jnp.sum(jnp.where(lanes == slot + SLOTS, tags, 0.0), axis=1, keepdims=True).astype(jnp.int32)
    source = ((owner & 1) * 8 + (owner >> 1)) * (4 * BLOCK) + 2 * (line - 1) + (rows[:, :1] & 1)
    source = jnp.where(line > 0, source, -1)
    lanes = lax.broadcasted_iota(jnp.int32, (8 * BLOCK, 64 * BLOCK), 1)
    cotangent = dot(bf16(jnp.where(lanes == source, 1.0, 0.0)), adjoint_ref[...])
    pooled = pooled_ref[...].astype(jnp.float32)
    message_ref[...] = bf16(
        jnp.concatenate([cotangent.reshape(BLOCK, 8, 128), pooled.reshape(BLOCK, 8, 128)], axis=1)
    )


def add_half(half, total_ref, grads_ref, stacked_refs):
    middle = HALF - 9 * CH
    for slot in range(SLOTS):
        stacked_ref, place = (stacked_refs[0], 0) if slot == 0 else (stacked_refs[1], slot - 1)
        grad = grads_ref[slot]
        wide = jnp.concatenate([grad.astype(jnp.float32), jnp.zeros((OUT, 128), jnp.float32)], axis=1)
        shifted = bf16(pltpu.roll(wide, 64, 1))
        if half == 0:
            side = dot_lanes(stacked_ref[place, :, :VOX], grad)
            inner = dot_lanes(stacked_ref[place, :middle, :], shifted)
            parts = ((0, 9 * CH, side), (9 * CH, HALF, inner))
        else:
            inner = dot_lanes(stacked_ref[place, middle:, :], shifted)
            side = dot_lanes(stacked_ref[place, :, 128:], grad)
            parts = ((0, middle, inner), (middle, HALF, side))
        for low, high, value in parts:
            if slot == 0:
                total_ref[low:high] = value
            else:
                total_ref[low:high] += value


def other_half_kernel(slope_ref, first_stacked, second_stacked, rows_ref, total_ref, grads_ref, bias_ref):
    order = onehot(
        (64 * SLOTS, 16 * BLOCK),
        lambda r, c: c == 16 * ((r & 63) >> 1) + 2 * (r >> 6) + (r & 1),
    )
    dense = bf16(dot(order, rows_ref[...]))
    table = pool_table(False)
    even = onehot((OUT, 64), lambda r, c: r == 2 * c)
    odd = onehot((OUT, 64), lambda r, c: r == 2 * c + 1)
    bias = jnp.zeros((OUT, 1), jnp.float32)
    for slot in range(SLOTS):
        row = dense[64 * slot : 64 * (slot + 1)]
        cells = dot(even, row[:, :64]) + dot(odd, row[:, 64:])
        grad = dot(bf16(cells), table) * slope_ref[slot]
        bias += jnp.sum(grad, axis=1, keepdims=True)
        grads_ref[slot] = bf16(grad)
    rows, columns = grid_of((OUT, OUT))
    bias_ref[...] = jnp.sum(jnp.where(rows == columns, bias, 0.0), axis=0, keepdims=True)
    core = lax.axis_index("c")
    for half in range(2):

        @pl.when(core == 1 - half)
        def _():
            add_half(half, total_ref, grads_ref, (first_stacked, second_stacked))


def own_half_kernel(grads_ref, first_stacked, second_stacked, total_ref):
    core = lax.axis_index("c")
    for half in range(2):

        @pl.when(core == half)
        def _():
            add_half(half, total_ref, grads_ref, (first_stacked, second_stacked))


def share_kernel(tags_ref, mine_ref, got_ref, bias_ref, pooled_ref, message_ref):
    total = mine_ref[...] + got_ref[...]
    tags = tags_ref[...].astype(jnp.float32)
    lines = dot_lanes(onehot((8, 128), lambda r, c: c == r), bf16(tags))
    lines = dot(bf16(lines), onehot((BLOCK, 16 * BLOCK), lambda r, c: (c >> 4) == r)).astype(jnp.int32)
    rows, columns = grid_of((8, 16 * BLOCK))
    lines = jnp.where(rows == ((columns >> 1) & 7) - SLOTS, lines, 0).astype(jnp.float32)
    line = jnp.sum(lines, axis=0, keepdims=True).astype(jnp.int32)
    columns = lax.broadcasted_iota(jnp.int32, (1, 16 * BLOCK), 1)
    target = 8 * ((line - 1) >> 1) + EXTRA + 2 * ((line - 1) & 1) + (columns & 1)
    target = jnp.where(line > 0, target, -1)
    rows = lax.broadcasted_iota(jnp.int32, (8 * BLOCK, 16 * BLOCK), 0)
    tail = dot(bf16(jnp.where(rows == target, 1.0, 0.0)), pooled_ref[...])
    extra = onehot(
        (8 * BLOCK, EXTRA * BLOCK), lambda r, c: ((r & 7) < EXTRA) & (c == (r & 7) * BLOCK + (r >> 3))
    )
    tail += dot(extra, bf16(total[MAIN * BLOCK : HALF]))
    bias = bias_ref[...]
    high = bf16(bias).astype(jnp.float32)
    rows = lax.broadcasted_iota(jnp.int32, (8 * BLOCK, 128), 0)
    tail = jnp.where((rows & 7) == 7, jnp.where((rows & 8) == 0, high, bias - high), tail)
    main = total[: MAIN * BLOCK].reshape(BLOCK, MAIN, 128)
    message_ref[...] = bf16(jnp.concatenate([main, tail.reshape(BLOCK, 8, 128)], axis=1))


def over_block_kernel(tags_ref, pieces_ref, message_ref):
    total = jnp.zeros((32, 128), jnp.float32)
    for device in range(BLOCK):
        total += pieces_ref[device].astype(jnp.float32)
    order = onehot(
        (128, 32 * BLOCK),
        lambda r, c: c == 32 * ((r & 63) >> 1) + SHARE + 2 * (r >> 6) + (r & 1),
    )
    pooled = bf16(dot(order, pieces_ref[...].reshape(32 * BLOCK, 128)))
    rows, lanes = grid_of((32, 128))
    total = jnp.where((rows < SHARE) | (rows == 31), total, 0.0)
    high = bf16(total).astype(jnp.float32)
    low = total - high
    owners = [place_of(tags_ref, row)[1] for row in range(2)]
    for z in range(8):
        tag = jnp.zeros((32, 128), jnp.float32)
        for core in range(2):
            for row in range(2):
                here = (rows == 28) & (lanes == core) & (owners[row] == 2 * z + core)
                tag = jnp.where(here, row + 1.0, tag)
        message_ref[3 * z] = bf16(jnp.concatenate([high + tag, low], axis=0))
        message_ref[3 * z + 1] = jnp.zeros((64, 128), jnp.bfloat16)
        message_ref[3 * z + 2] = jnp.zeros((64, 128), jnp.bfloat16)
    for row in range(2):
        message_ref[3 * (owners[row] >> 1) + 1 + (owners[row] & 1)] = pooled[64 * row : 64 * (row + 1)]


def over_z_kernel(pieces_ref, message_ref):
    total = jnp.zeros((32, 128), jnp.float32)
    for z in range(8):
        parts = pieces_ref[3 * z].astype(jnp.float32)
        total += parts[:32] + parts[32:]
    rows = lax.broadcasted_iota(jnp.int32, (32, 128), 0)
    bias = total[31:32]
    high = bf16(bias).astype(jnp.float32)
    part = jnp.where((lax.axis_index("b") & 2) == 0, high, bias - high)
    tile = jnp.where(rows < SHARE, total, part)[:ROWS]
    four = bf16(jnp.concatenate([tile] * 4, axis=0))
    for index in range(BLOCK // 4):
        message_ref[4 * ROWS * index : 4 * ROWS * (index + 1), :] = four


def pick_kernel(pieces_ref, mine_ref, other_ref):
    pooled = [[jnp.zeros((64, 128), jnp.float32) for _ in range(2)] for _ in range(2)]
    for z in range(8):
        tags = pieces_ref[3 * z, 16:32, :].astype(jnp.float32)
        for core in range(2):
            tag = tags[12:13, core : core + 1]
            value = pieces_ref[3 * z + 1 + core].astype(jnp.float32)
            for row in range(2):
                pooled[core][row] += jnp.where(tag == row + 1.0, value, 0.0)
    core = lax.axis_index("c")
    for row in range(2):
        mine_ref[row] = bf16(jnp.where(core == 0, pooled[0][row], pooled[1][row]))
        other_ref[row] = bf16(jnp.where(core == 0, pooled[1][row], pooled[0][row]))


def finish_kernel(pieces_ref, weight_ref, bias_ref):
    order = onehot((EXTRA * BLOCK, ROWS * BLOCK), lambda r, c: c == ROWS * (r & 31) + MAIN + (r >> 5))
    bias = []
    for half in range(2):
        pieces = pieces_ref[half * ROWS * BLOCK : (half + 1) * ROWS * BLOCK, :]
        values = pieces.astype(jnp.float32)
        for device in range(BLOCK):
            start = half * HALF + device * MAIN
            weight_ref[start : start + MAIN, :] = values[ROWS * device : ROWS * device + MAIN]
        start = half * HALF + MAIN * BLOCK
        weight_ref[start : start + EXTRA * BLOCK, :] = dot(order, pieces)
        parts = [values[ROWS * device + SHARE : ROWS * device + SHARE + 1] for device in range(4)]
        bias.append(parts[0] + parts[2] + (parts[1] + parts[3]))
    bias_ref[...] = bias[0] + bias[1]


def hbm(array):
    return pltpu.with_memory_space_constraint(array, HBM)


def vmem(array):
    return pltpu.with_memory_space_constraint(array, pltpu.VMEM)


def call(kernel, name, outs, operands, in_hbm=0, scratch=(), limit=12, flops=1_000_000):
    specs = [pl.BlockSpec(memory_space=HBM) for _ in range(in_hbm)]
    specs += [pl.BlockSpec(memory_space=pltpu.VMEM) for _ in operands[in_hbm:]]
    operands = [hbm(operand) for operand in operands[:in_hbm]] + list(operands[in_hbm:])
    return pl.pallas_call(
        kernel,
        out_shape=[
            pltpu.VMEM(shape, dtype) if kept else jax.ShapeDtypeStruct(shape, dtype) for shape, dtype, kept in outs
        ],
        in_specs=specs,
        out_specs=[pl.BlockSpec(memory_space=pltpu.VMEM) for _ in outs],
        scratch_shapes=list(scratch),
        compiler_params=pltpu.CompilerParams(vmem_limit_bytes=limit * 1024 * 1024),
        cost_estimate=pl.CostEstimate(flops=flops, bytes_accessed=1_000_000, transcendentals=0),
        name=name,
    )(*operands)


def begin(counts, rebalance, owner, features, adjoint):
    return call(
        begin_kernel,
        "begin",
        [
            ((SLOTS, CH, 128), jnp.bfloat16, False),
            ((8 * BLOCK, 128), jnp.bfloat16, False),
        ],
        (counts, rebalance, owner, features, adjoint),
        in_hbm=5,
        scratch=[
            pltpu.SMEM((SLOTS,), jnp.int32),
            pltpu.SMEM((SLOTS,), jnp.int32),
            pltpu.SMEM((SLOTS,), jnp.int32),
            pltpu.VMEM((SLOTS, CH, VOX), jnp.bfloat16),
            pltpu.VMEM((2, CH * 128), jnp.bfloat16),
            pltpu.VMEM((128, 128), jnp.float32),
            pltpu.SemaphoreType.DMA((5,)),
        ],
    )


def forward(*operands):
    in_hbm, in_vmem = pl.BlockSpec(memory_space=HBM), pl.BlockSpec(memory_space=pltpu.VMEM)
    return pl.pallas_call(
        forward_kernel,
        out_shape=[
            jax.ShapeDtypeStruct((8 * BLOCK, 128), jnp.bfloat16),
            HBM((1, 9 * CH, FRAME), jnp.bfloat16),
            pltpu.VMEM((SLOTS - 1, 9 * CH, FRAME), jnp.bfloat16),
            HBM((SLOTS, OUT, VOX), jnp.float32),
        ],
        in_specs=[in_vmem if i in (4, 5) else in_hbm for i in range(len(operands))],
        out_specs=[in_vmem, in_hbm, in_vmem, in_hbm],
        scratch_shapes=[
            pltpu.VMEM((SLOTS, CH, VOX), jnp.bfloat16),
            pltpu.VMEM((SLOTS + 1, CH, VOX), jnp.float32),
            pltpu.VMEM((3 * SLOTS + 1, CH, 128), jnp.bfloat16),
            pltpu.VMEM((SLOTS, OUT, VOX), jnp.float32),
            pltpu.VMEM((SLOTS, 64, 128), jnp.float32),
            pltpu.VMEM((1, 9 * CH, FRAME), jnp.bfloat16),
            pltpu.SMEM((SLOTS,), jnp.int32),
            pltpu.SMEM((SLOTS, 26), jnp.int32),
            pltpu.VMEM((1, OUT), jnp.float32),
            pltpu.VMEM((TAP_ROWS, OUT), jnp.bfloat16),
            pltpu.VMEM((3 * OUT, 9 * CH), jnp.bfloat16),
            pltpu.SemaphoreType.DMA((7,)),
            pltpu.SemaphoreType.DMA((SLOTS + 1,)),
        ],
        compiler_params=pltpu.CompilerParams(vmem_limit_bytes=16 * 1024 * 1024),
        cost_estimate=pl.CostEstimate(flops=40_000_000_000, bytes_accessed=4_000_000, transcendentals=300_000),
        name="forward",
    )(*[operand if i in (4, 5) else hbm(operand) for i, operand in enumerate(operands)])


def exchange(message, axis):
    return lax.all_to_all(message, axis, 0, 0, tiled=True)


def per_device(
    features,
    counts,
    rebalance,
    neighbors,
    coarse_owner,
    conv_weight,
    convolution_bias_vector,
    merged_adjoint,
):
    narrow, wide = jnp.bfloat16, jnp.float32
    layers, offer = begin(counts, rebalance, coarse_owner, features, merged_adjoint)
    offers = exchange(offer.reshape(BLOCK, 8, 128), "b")
    before = lax.ppermute(layers, "b", [(i, i + 1) for i in range(BLOCK - 1)])
    after = lax.ppermute(layers, "b", [(i + 1, i) for i in range(BLOCK - 1)])
    offers = offers.reshape(8 * BLOCK, 128)
    (message,) = call(spread_kernel, "spread", [((8, 4 * BLOCK, 128), narrow, False)], (offers,))
    bias = convolution_bias_vector.reshape(1, OUT)
    message, bias = lax.optimization_barrier((message, bias))
    adjoint = exchange(message, "z")
    adjoint = lax.all_gather(adjoint, "c", tiled=True).reshape(64 * BLOCK, 128)
    (tags,) = call(tags_kernel, "tags", [((BLOCK, 128), jnp.int32, False)], (offers,))
    weight = conv_weight.reshape(TAP_ROWS, OUT)
    pooled, *kept = forward(counts, neighbors, bias, features, before, after, weight)
    (message,) = call(choose_kernel, "choose", [((BLOCK, 16, 128), narrow, False)], (tags, adjoint, pooled))
    rows = exchange(message, "b").reshape(16 * BLOCK, 128)
    stacked = (vmem(kept[0]), vmem(kept[1]))
    other, grads, bias_part = call(
        other_half_kernel,
        "other_half",
        [((HALF, OUT), wide, False), ((SLOTS, OUT, VOX), narrow, True), ((1, OUT), wide, True)],
        (vmem(kept[2]),) + stacked + (rows,),
    )
    got = lax.ppermute(other, "c", [(0, 1), (1, 0)])
    (mine,) = call(
        own_half_kernel,
        "own_half",
        [((HALF, OUT), wide, False)],
        (vmem(grads),) + stacked,
        flops=2_000_000_000,
    )
    (message,) = call(
        share_kernel, "share", [((BLOCK, 32, 128), narrow, False)], (tags, mine, got, vmem(bias_part), rows)
    )
    pieces = exchange(message, "b")
    (message,) = call(over_block_kernel, "over_block", [((24, 64, 128), narrow, False)], (tags, pieces))
    pieces = exchange(message.reshape(8, 192, 128), "z").reshape(24, 64, 128)
    (message,) = call(over_z_kernel, "over_z", [((ROWS * BLOCK, 128), narrow, False)], (pieces,))
    totals = exchange(message.reshape(BLOCK, ROWS // 2, 2, 128), "b")
    pooled_mine, pooled_other = call(
        pick_kernel, "pick", [((2, CH, 128), narrow, False), ((2, CH, 128), narrow, False)], (pieces,)
    )
    pooled = pooled_mine + lax.ppermute(pooled_other, "c", [(0, 1), (1, 0)])
    pieces = lax.all_gather(totals, "c", tiled=True).reshape(2 * ROWS * BLOCK, 128)
    weight_total, bias_total = call(
        finish_kernel, "finish", [((TAP_ROWS, OUT), wide, False), ((1, OUT), wide, False)], (pieces,)
    )
    return pooled.reshape(2, CH * 128), weight_total.reshape(27, CH, OUT), bias_total.reshape(OUT)


def solution(mesh):
    chips = Mesh(mesh.devices.reshape(-1, 2, BLOCK), ("z", "c", "b"))
    whole = ("z", "c", "b")
    in_specs = (
        P(whole, None, None),
        P(whole),
        P(whole),
        P(whole, None),
        P(whole),
        P(),
        P(),
        P(whole, None),
    )
    out_specs = (P(whole, None), P(), P())
    return jax.shard_map(
        per_device, mesh=chips, in_specs=in_specs, out_specs=out_specs, check_vma=False
    )
```

```python
import jax
import jax.numpy as jnp
from jax import lax
from jax.experimental import pallas as pl
from jax.experimental.pallas import tpu as pltpu
from jax.sharding import Mesh
from jax.sharding import PartitionSpec as P

SLOTS = 4
CH = 64
OUT = 128
VOX = 512
FRAME = 640
TAP_ROWS = 1728
BLOCK = 32
HALF = TAP_ROWS // 2
MAIN = 24
EXTRA = 3
SHARE = MAIN + EXTRA
ROWS = SHARE + 1
HBM = pltpu.HBM
EDGES = ((-1, -1), (-1, 0), (-1, 1), (0, -1), (0, 0), (0, 1), (1, -1), (1, 0), (1, 1))
SMEM = pltpu.SMEM


def voxel_mask(count):
    lanes = lax.broadcasted_iota(jnp.int32, (1, VOX), 1)
    return ((lanes * 167) & 511) < count


def layer_pair(block):
    lanes = lax.broadcasted_iota(jnp.int32, (CH, 128), 1)
    return pltpu.roll(jnp.where(lanes < 64, block[:, :128], block[:, VOX - 128 :]), 64, 1)


def column_of(ea, eb, ec):
    tap = 9 * (ea + 1) + 3 * (eb + 1) + (ec + 1)
    return tap if tap < 13 else tap - 1


def dot(a, b):
    return jnp.dot(a, b, preferred_element_type=jnp.float32)


def dot_lanes(a, b):
    return lax.dot_general(a, b, (((1,), (1,)), ((), ())), preferred_element_type=jnp.float32)


def grid_of(shape):
    return lax.broadcasted_iota(jnp.int32, shape, 0), lax.broadcasted_iota(jnp.int32, shape, 1)


def onehot(shape, chosen):
    return jnp.where(chosen(*grid_of(shape)), 1.0, 0.0).astype(jnp.bfloat16)


def bf16(array):
    return array.astype(jnp.bfloat16)


def pool_table(voxels_first):
    shape = (VOX, 64) if voxels_first else (64, VOX)
    rows, columns = grid_of(shape)
    voxel, cell = (rows, columns) if voxels_first else (columns, rows)
    index = ((voxel >> 7) << 4) | (((voxel >> 4) & 3) << 2) | ((voxel & 7) >> 1)
    return bf16(jnp.where(index == cell, 0.125, 0.0))


def fetch(pairs, sems):
    copies = [pltpu.make_async_copy(source, target, sems.at[i]) for i, (source, target) in enumerate(pairs)]
    for copy in copies:
        copy.start()
    for copy in copies:
        copy.wait()


def begin_kernel(
    counts_hbm, rebalance_hbm, owner_hbm, features_hbm, adjoint_hbm,
    layers_ref, offer_ref,
    counts_ref, rebalance_ref, owner_ref, features_ref, adjoint_ref, dense_ref, sems,
):
    fetch(
        [
            (counts_hbm, counts_ref),
            (rebalance_hbm, rebalance_ref),
            (owner_hbm, owner_ref),
            (features_hbm, features_ref),
            (adjoint_hbm, adjoint_ref),
        ],
        sems,
    )
    lanes = lax.broadcasted_iota(jnp.int32, (1, 128), 1)
    tags = jnp.zeros((1, 128), jnp.float32)
    for slot in range(SLOTS):
        block = jnp.where(voxel_mask(counts_ref[slot]), features_ref[slot].astype(jnp.float32), 0.0)
        layers_ref[slot] = bf16(layer_pair(block))
        row = rebalance_ref[slot]
        line = jnp.where(row >= 0, (row & (2 * BLOCK - 1)) + 1, 0).astype(jnp.float32)
        owner = jnp.maximum(owner_ref[slot], 0).astype(jnp.float32)
        tags = jnp.where(lanes == slot, line, tags)
        tags = jnp.where(lanes == SLOTS + slot, owner, tags)
    for part in range(64):
        dense_ref[2 * part : 2 * part + 2, :] = adjoint_ref[:, 128 * part : 128 * (part + 1)].astype(jnp.float32)
    order = onehot(
        (8 * BLOCK, 128),
        lambda r, c: ((r & 7) < 4) & (c == 2 * (2 * (r >> 3) + (r & 1)) + ((r >> 1) & 1)),
    )
    rows = lax.broadcasted_iota(jnp.int32, (8 * BLOCK, 128), 0)
    offer_ref[...] = bf16(jnp.where((rows & 7) == 4, tags, dot(order, bf16(dense_ref[...]))))


def spread_kernel(offers_ref, message_ref):
    order = onehot((4 * BLOCK, 8 * BLOCK), lambda r, c: c == 8 * (r >> 2) + (r & 3))
    message_ref[...] = jnp.broadcast_to(bf16(dot(order, offers_ref[...]))[None], message_ref.shape)


def tags_kernel(offers_ref, tags_ref):
    order = onehot((BLOCK, 8 * BLOCK), lambda r, c: c == 8 * r + 4)
    tags_ref[...] = dot(order, offers_ref[...]).astype(jnp.int32)


def place_of(tags_ref, row):
    tags = tags_ref[...]
    rows, lanes = grid_of((BLOCK, 128))
    hit = (tags == 2 * lax.axis_index("b") + row + 1) & (lanes < SLOTS)
    owner = jnp.where(hit, pltpu.roll(tags, 128 - SLOTS, 1), 0).astype(jnp.float32)
    home = jnp.where(hit, rows, 0).astype(jnp.float32)
    return [
        jnp.sum(jnp.sum(value, axis=1, keepdims=True), axis=0, keepdims=True).astype(jnp.int32)[0, 0]
        for value in (home, owner)
    ]


def forward_kernel(*refs):
    operands, refs = refs[:7], refs[7:]
    pooled_ref, first_stacked, second_stacked, slope_hbm, features_ref, blocks_ref, rims_ref, slope_ref = refs[:8]
    dense_ref, first_ref, counts_ref, neighbors_ref, bias_ref, taps_ref, weight_ref, sems, out_sems = refs[8:]
    targets = [
        counts_ref,
        neighbors_ref,
        bias_ref,
        features_ref,
        rims_ref.at[pl.ds(0, SLOTS)],
        rims_ref.at[pl.ds(2 * SLOTS, SLOTS)],
        taps_ref,
    ]
    fetch(list(zip(operands, targets)), sems)
    for index in range(SLOTS):
        block = jnp.where(voxel_mask(counts_ref[index]), features_ref[index].astype(jnp.float32), 0.0)
        block = pltpu.roll(block, 64, 1)
        blocks_ref[index] = block
        rims_ref[SLOTS + index] = bf16(block[:, :128])
    blocks_ref[SLOTS] = jnp.zeros((CH, VOX), jnp.float32)
    rims_ref[3 * SLOTS] = jnp.zeros((CH, 128), jnp.bfloat16)
    same = onehot((OUT, OUT), lambda r, c: r == c)
    for part in range(3):
        turned = dot_lanes(same, taps_ref[part * 9 * CH : (part + 1) * 9 * CH, :])
        weight_ref[part * OUT : (part + 1) * OUT, :] = bf16(turned)
    first = ((lax.axis_index("z") * 2 + lax.axis_index("c")) * BLOCK + lax.axis_index("b")) * SLOTS
    rows, columns = grid_of((OUT, OUT))
    bias = jnp.sum(jnp.where(rows == columns, bias_ref[...], 0.0), axis=1, keepdims=True)
    lanes = lax.broadcasted_iota(jnp.int32, (CH, FRAME), 1)
    at_c = lanes & 7
    at_b = (lanes >> 3) & 7

    def moved(array, steps):
        return pltpu.roll(array, (-steps) % FRAME, 1)

    def one(slot, stacked_ref, place):
        def rim(ea, eb, ec):
            target = neighbors_ref[slot, column_of(ea, eb, ec)]
            at = jnp.clip(target - (first - SLOTS), 0, 3 * SLOTS - 1)
            return rims_ref[jnp.where(target >= 0, at, 3 * SLOTS)].astype(jnp.float32)

        def inner(eb, ec):
            if eb == 0 and ec == 0:
                return blocks_ref[slot]
            target = neighbors_ref[slot, column_of(0, eb, ec)]
            at = jnp.clip(target - first, 0, SLOTS - 1)
            return blocks_ref[jnp.where(target >= 0, at, SLOTS)]

        def frame(eb, ec):
            low = lax.broadcasted_iota(jnp.int32, (CH, 128), 1) < 64
            block = inner(eb, ec)
            ends = block[:, :128]
            left = jnp.where(low, rim(-1, eb, ec), ends)
            right = jnp.where(low, ends, rim(1, eb, ec))
            return jnp.concatenate([left, block[:, 128:], right], axis=1)

        along_c = {}
        for eb in (-1, 0, 1):
            middle = frame(eb, 0)
            along_c[eb, 0] = middle
            along_c[eb, -1] = jnp.where(at_c == 0, moved(frame(eb, -1), 7), moved(middle, -1))
            along_c[eb, 1] = jnp.where(at_c == 7, moved(frame(eb, 1), -7), moved(middle, 1))
        for index, (eb, ec) in enumerate(EDGES):
            if eb == 0:
                value = along_c[0, ec]
            elif eb < 0:
                value = jnp.where(at_b == 0, moved(along_c[-1, ec], 56), moved(along_c[0, ec], -8))
            else:
                value = jnp.where(at_b == 7, moved(along_c[1, ec], -56), moved(along_c[0, ec], 8))
            stacked_ref[place, index * CH : (index + 1) * CH, :] = value.astype(jnp.bfloat16)

        product = dot(weight_ref[...], stacked_ref[place])
        middle = pltpu.roll(product[OUT : 2 * OUT], FRAME - 64, 1)[:, :VOX]
        preact = product[:OUT, :VOX] + middle + product[2 * OUT :, 128:] + bias
        mask = voxel_mask(counts_ref[slot])
        sigmoid = jax.nn.sigmoid(preact)
        slope = sigmoid * (1.0 + preact * (1.0 - sigmoid))
        slope_ref[slot] = jnp.where(mask, slope, 0.0)

        pltpu.make_async_copy(slope_ref.at[slot], slope_hbm.at[slot], out_sems.at[slot]).start()
        activation = jnp.where(mask, preact * sigmoid, 0.0)
        high = activation.astype(jnp.bfloat16)
        low = (activation - high.astype(jnp.float32)).astype(jnp.bfloat16)
        table = pool_table(True)
        cells = bf16(dot(high, table) + dot(low, table))
        even = dot(onehot((64, OUT), lambda r, c: c == 2 * r), cells)
        odd = dot(onehot((64, OUT), lambda r, c: c == 2 * r + 1), cells)
        dense_ref[slot] = jnp.concatenate([even, odd], axis=1)

    one(0, first_ref, 0)
    frames = pltpu.make_async_copy(first_ref, first_stacked, out_sems.at[SLOTS])
    frames.start()

    @pl.loop(1, SLOTS, unroll=True)
    def _(slot):
        one(slot, second_stacked, slot - 1)

    order = onehot((8 * BLOCK, 64 * SLOTS), lambda r, c: c == 64 * ((r & 7) >> 1) + 2 * (r >> 3) + (r & 1))
    pooled_ref[...] = bf16(dot(order, bf16(dense_ref[...].reshape(64 * SLOTS, 128))))
    for slot in range(SLOTS):
        pltpu.make_async_copy(slope_ref.at[slot], slope_hbm.at[slot], out_sems.at[slot]).wait()
    frames.wait()


def choose_kernel(tags_ref, adjoint_ref, pooled_ref, message_ref):
    tags = bf16(tags_ref[...].astype(jnp.float32))
    tags = dot(onehot((8 * BLOCK, BLOCK), lambda r, c: (r >> 3) == c), tags)
    rows, lanes = grid_of((8 * BLOCK, 128))
    slot = (rows & 7) >> 1
    line = jnp.sum(jnp.where(lanes == slot, tags, 0.0), axis=1, keepdims=True).astype(jnp.int32)
    owner = jnp.sum(jnp.where(lanes == slot + SLOTS, tags, 0.0), axis=1, keepdims=True).astype(jnp.int32)
    source = ((owner & 1) * 8 + (owner >> 1)) * (4 * BLOCK) + 2 * (line - 1) + (rows[:, :1] & 1)
    source = jnp.where(line > 0, source, -1)
    lanes = lax.broadcasted_iota(jnp.int32, (8 * BLOCK, 64 * BLOCK), 1)
    cotangent = dot(bf16(jnp.where(lanes == source, 1.0, 0.0)), adjoint_ref[...])
    pooled = pooled_ref[...].astype(jnp.float32)
    message_ref[...] = bf16(
        jnp.concatenate([cotangent.reshape(BLOCK, 8, 128), pooled.reshape(BLOCK, 8, 128)], axis=1)
    )


def add_half(half, total_ref, grads_ref, stacked_refs):
    middle = HALF - 9 * CH
    for slot in range(SLOTS):
        stacked_ref, place = (stacked_refs[0], 0) if slot == 0 else (stacked_refs[1], slot - 1)
        grad = grads_ref[slot]
        wide = jnp.concatenate([grad.astype(jnp.float32), jnp.zeros((OUT, 128), jnp.float32)], axis=1)
        shifted = bf16(pltpu.roll(wide, 64, 1))
        if half == 0:
            side = dot_lanes(stacked_ref[place, :, :VOX], grad)
            inner = dot_lanes(stacked_ref[place, :middle, :], shifted)
            parts = ((0, 9 * CH, side), (9 * CH, HALF, inner))
        else:
            inner = dot_lanes(stacked_ref[place, middle:, :], shifted)
            side = dot_lanes(stacked_ref[place, :, 128:], grad)
            parts = ((0, middle, inner), (middle, HALF, side))
        for low, high, value in parts:
            if slot == 0:
                total_ref[low:high] = value
            else:
                total_ref[low:high] += value


def other_half_kernel(slope_ref, first_stacked, second_stacked, rows_ref, total_ref, grads_ref, bias_ref):
    order = onehot(
        (64 * SLOTS, 16 * BLOCK),
        lambda r, c: c == 16 * ((r & 63) >> 1) + 2 * (r >> 6) + (r & 1),
    )
    dense = bf16(dot(order, rows_ref[...]))
    table = pool_table(False)
    even = onehot((OUT, 64), lambda r, c: r == 2 * c)
    odd = onehot((OUT, 64), lambda r, c: r == 2 * c + 1)
    bias = jnp.zeros((OUT, 1), jnp.float32)
    for slot in range(SLOTS):
        row = dense[64 * slot : 64 * (slot + 1)]
        cells = dot(even, row[:, :64]) + dot(odd, row[:, 64:])
        grad = dot(bf16(cells), table) * slope_ref[slot]
        bias += jnp.sum(grad, axis=1, keepdims=True)
        grads_ref[slot] = bf16(grad)
    rows, columns = grid_of((OUT, OUT))
    bias_ref[...] = jnp.sum(jnp.where(rows == columns, bias, 0.0), axis=0, keepdims=True)
    core = lax.axis_index("c")
    for half in range(2):

        @pl.when(core == 1 - half)
        def _():
            add_half(half, total_ref, grads_ref, (first_stacked, second_stacked))


def own_half_kernel(grads_ref, first_stacked, second_stacked, total_ref):
    core = lax.axis_index("c")
    for half in range(2):

        @pl.when(core == half)
        def _():
            add_half(half, total_ref, grads_ref, (first_stacked, second_stacked))


def share_kernel(tags_ref, mine_ref, got_ref, bias_ref, pooled_ref, message_ref):
    total = mine_ref[...] + got_ref[...]
    tags = tags_ref[...].astype(jnp.float32)
    lines = dot_lanes(onehot((8, 128), lambda r, c: c == r), bf16(tags))
    lines = dot(bf16(lines), onehot((BLOCK, 16 * BLOCK), lambda r, c: (c >> 4) == r)).astype(jnp.int32)
    rows, columns = grid_of((8, 16 * BLOCK))
    lines = jnp.where(rows == ((columns >> 1) & 7) - SLOTS, lines, 0).astype(jnp.float32)
    line = jnp.sum(lines, axis=0, keepdims=True).astype(jnp.int32)
    columns = lax.broadcasted_iota(jnp.int32, (1, 16 * BLOCK), 1)
    target = 8 * ((line - 1) >> 1) + EXTRA + 2 * ((line - 1) & 1) + (columns & 1)
    target = jnp.where(line > 0, target, -1)
    rows = lax.broadcasted_iota(jnp.int32, (8 * BLOCK, 16 * BLOCK), 0)
    tail = dot(bf16(jnp.where(rows == target, 1.0, 0.0)), pooled_ref[...])
    extra = onehot(
        (8 * BLOCK, EXTRA * BLOCK), lambda r, c: ((r & 7) < EXTRA) & (c == (r & 7) * BLOCK + (r >> 3))
    )
    tail += dot(extra, bf16(total[MAIN * BLOCK : HALF]))
    bias = bias_ref[...]
    high = bf16(bias).astype(jnp.float32)
    rows = lax.broadcasted_iota(jnp.int32, (8 * BLOCK, 128), 0)
    tail = jnp.where((rows & 7) == 7, jnp.where((rows & 8) == 0, high, bias - high), tail)
    main = total[: MAIN * BLOCK].reshape(BLOCK, MAIN, 128)
    message_ref[...] = bf16(jnp.concatenate([main, tail.reshape(BLOCK, 8, 128)], axis=1))


def over_block_kernel(tags_ref, pieces_ref, message_ref):
    total = jnp.zeros((32, 128), jnp.float32)
    for device in range(BLOCK):
        total += pieces_ref[device].astype(jnp.float32)
    order = onehot(
        (128, 32 * BLOCK),
        lambda r, c: c == 32 * ((r & 63) >> 1) + SHARE + 2 * (r >> 6) + (r & 1),
    )
    pooled = bf16(dot(order, pieces_ref[...].reshape(32 * BLOCK, 128)))
    rows, lanes = grid_of((32, 128))
    total = jnp.where((rows < SHARE) | (rows == 31), total, 0.0)
    high = bf16(total).astype(jnp.float32)
    low = total - high
    owners = [place_of(tags_ref, row)[1] for row in range(2)]
    for z in range(8):
        tag = jnp.zeros((32, 128), jnp.float32)
        for core in range(2):
            for row in range(2):
                here = (rows == 28) & (lanes == core) & (owners[row] == 2 * z + core)
                tag = jnp.where(here, row + 1.0, tag)
        message_ref[3 * z] = bf16(jnp.concatenate([high + tag, low], axis=0))
        message_ref[3 * z + 1] = jnp.zeros((64, 128), jnp.bfloat16)
        message_ref[3 * z + 2] = jnp.zeros((64, 128), jnp.bfloat16)
    for row in range(2):
        message_ref[3 * (owners[row] >> 1) + 1 + (owners[row] & 1)] = pooled[64 * row : 64 * (row + 1)]


def over_z_kernel(pieces_ref, message_ref):
    total = jnp.zeros((32, 128), jnp.float32)
    for z in range(8):
        parts = pieces_ref[3 * z].astype(jnp.float32)
        total += parts[:32] + parts[32:]
    rows = lax.broadcasted_iota(jnp.int32, (32, 128), 0)
    bias = total[31:32]
    high = bf16(bias).astype(jnp.float32)
    part = jnp.where((lax.axis_index("b") & 2) == 0, high, bias - high)
    tile = jnp.where(rows < SHARE, total, part)[:ROWS]
    four = bf16(jnp.concatenate([tile] * 4, axis=0))
    for index in range(BLOCK // 4):
        message_ref[4 * ROWS * index : 4 * ROWS * (index + 1), :] = four


def pick_kernel(pieces_ref, mine_ref, other_ref):
    pooled = [[jnp.zeros((64, 128), jnp.float32) for _ in range(2)] for _ in range(2)]
    for z in range(8):
        tags = pieces_ref[3 * z, 16:32, :].astype(jnp.float32)
        for core in range(2):
            tag = tags[12:13, core : core + 1]
            value = pieces_ref[3 * z + 1 + core].astype(jnp.float32)
            for row in range(2):
                pooled[core][row] += jnp.where(tag == row + 1.0, value, 0.0)
    core = lax.axis_index("c")
    for row in range(2):
        mine_ref[row] = bf16(jnp.where(core == 0, pooled[0][row], pooled[1][row]))
        other_ref[row] = bf16(jnp.where(core == 0, pooled[1][row], pooled[0][row]))


def finish_kernel(pieces_ref, weight_ref, bias_ref):
    order = onehot((EXTRA * BLOCK, ROWS * BLOCK), lambda r, c: c == ROWS * (r & 31) + MAIN + (r >> 5))
    bias = []
    for half in range(2):
        pieces = pieces_ref[half * ROWS * BLOCK : (half + 1) * ROWS * BLOCK, :]
        values = pieces.astype(jnp.float32)
        for device in range(BLOCK):
            start = half * HALF + device * MAIN
            weight_ref[start : start + MAIN, :] = values[ROWS * device : ROWS * device + MAIN]
        start = half * HALF + MAIN * BLOCK
        weight_ref[start : start + EXTRA * BLOCK, :] = dot(order, pieces)
        parts = [values[ROWS * device + SHARE : ROWS * device + SHARE + 1] for device in range(4)]
        bias.append(parts[0] + parts[2] + (parts[1] + parts[3]))
    bias_ref[...] = bias[0] + bias[1]


def hbm(array):
    return pltpu.with_memory_space_constraint(array, HBM)


def vmem(array):
    return pltpu.with_memory_space_constraint(array, pltpu.VMEM)


def call(kernel, name, outs, operands, in_hbm=0, scratch=(), limit=12, flops=1_000_000):
    specs = [pl.BlockSpec(memory_space=HBM) for _ in range(in_hbm)]
    specs += [pl.BlockSpec(memory_space=pltpu.VMEM) for _ in operands[in_hbm:]]
    operands = [hbm(operand) for operand in operands[:in_hbm]] + list(operands[in_hbm:])
    return pl.pallas_call(
        kernel,
        out_shape=[
            pltpu.VMEM(shape, dtype) if kept else jax.ShapeDtypeStruct(shape, dtype) for shape, dtype, kept in outs
        ],
        in_specs=specs,
        out_specs=[pl.BlockSpec(memory_space=pltpu.VMEM) for _ in outs],
        scratch_shapes=list(scratch),
        compiler_params=pltpu.CompilerParams(vmem_limit_bytes=limit * 1024 * 1024),
        cost_estimate=pl.CostEstimate(flops=flops, bytes_accessed=1_000_000, transcendentals=0),
        name=name,
    )(*operands)


def begin(counts, rebalance, owner, features, adjoint):
    return call(
        begin_kernel,
        "begin",
        [
            ((SLOTS, CH, 128), jnp.bfloat16, False),
            ((8 * BLOCK, 128), jnp.bfloat16, False),
        ],
        (counts, rebalance, owner, features, adjoint),
        in_hbm=5,
        scratch=[
            pltpu.SMEM((SLOTS,), jnp.int32),
            pltpu.SMEM((SLOTS,), jnp.int32),
            pltpu.SMEM((SLOTS,), jnp.int32),
            pltpu.VMEM((SLOTS, CH, VOX), jnp.bfloat16),
            pltpu.VMEM((2, CH * 128), jnp.bfloat16),
            pltpu.VMEM((128, 128), jnp.float32),
            pltpu.SemaphoreType.DMA((5,)),
        ],
    )


def forward(*operands):
    in_hbm, in_vmem = pl.BlockSpec(memory_space=HBM), pl.BlockSpec(memory_space=pltpu.VMEM)
    return pl.pallas_call(
        forward_kernel,
        out_shape=[
            jax.ShapeDtypeStruct((8 * BLOCK, 128), jnp.bfloat16),
            HBM((1, 9 * CH, FRAME), jnp.bfloat16),
            pltpu.VMEM((SLOTS - 1, 9 * CH, FRAME), jnp.bfloat16),
            HBM((SLOTS, OUT, VOX), jnp.float32),
        ],
        in_specs=[in_vmem if i in (4, 5) else in_hbm for i in range(len(operands))],
        out_specs=[in_vmem, in_hbm, in_vmem, in_hbm],
        scratch_shapes=[
            pltpu.VMEM((SLOTS, CH, VOX), jnp.bfloat16),
            pltpu.VMEM((SLOTS + 1, CH, VOX), jnp.float32),
            pltpu.VMEM((3 * SLOTS + 1, CH, 128), jnp.bfloat16),
            pltpu.VMEM((SLOTS, OUT, VOX), jnp.float32),
            pltpu.VMEM((SLOTS, 64, 128), jnp.float32),
            pltpu.VMEM((1, 9 * CH, FRAME), jnp.bfloat16),
            pltpu.SMEM((SLOTS,), jnp.int32),
            pltpu.SMEM((SLOTS, 26), jnp.int32),
            pltpu.VMEM((1, OUT), jnp.float32),
            pltpu.VMEM((TAP_ROWS, OUT), jnp.bfloat16),
            pltpu.VMEM((3 * OUT, 9 * CH), jnp.bfloat16),
            pltpu.SemaphoreType.DMA((7,)),
            pltpu.SemaphoreType.DMA((SLOTS + 1,)),
        ],
        compiler_params=pltpu.CompilerParams(vmem_limit_bytes=16 * 1024 * 1024),
        cost_estimate=pl.CostEstimate(flops=40_000_000_000, bytes_accessed=4_000_000, transcendentals=300_000),
        name="forward",
    )(*[operand if i in (4, 5) else hbm(operand) for i, operand in enumerate(operands)])


def exchange(message, axis):
    return lax.all_to_all(message, axis, 0, 0, tiled=True)


def per_device(
    features,
    counts,
    rebalance,
    neighbors,
    coarse_owner,
    conv_weight,
    convolution_bias_vector,
    merged_adjoint,
):
    narrow, wide = jnp.bfloat16, jnp.float32
    layers, offer = begin(counts, rebalance, coarse_owner, features, merged_adjoint)
    offers = exchange(offer.reshape(BLOCK, 8, 128), "b")
    before = lax.ppermute(layers, "b", [(i, i + 1) for i in range(BLOCK - 1)])
    after = lax.ppermute(layers, "b", [(i + 1, i) for i in range(BLOCK - 1)])
    offers = offers.reshape(8 * BLOCK, 128)
    (message,) = call(spread_kernel, "spread", [((8, 4 * BLOCK, 128), narrow, False)], (offers,))
    bias = convolution_bias_vector.reshape(1, OUT)
    message, bias = lax.optimization_barrier((message, bias))
    adjoint = exchange(message, "z")
    adjoint = lax.all_gather(adjoint, "c", tiled=True).reshape(64 * BLOCK, 128)
    (tags,) = call(tags_kernel, "tags", [((BLOCK, 128), jnp.int32, False)], (offers,))
    weight = conv_weight.reshape(TAP_ROWS, OUT)
    pooled, *kept = forward(counts, neighbors, bias, features, before, after, weight)
    (message,) = call(choose_kernel, "choose", [((BLOCK, 16, 128), narrow, False)], (tags, adjoint, pooled))
    rows = exchange(message, "b").reshape(16 * BLOCK, 128)
    stacked = (vmem(kept[0]), vmem(kept[1]))
    other, grads, bias_part = call(
        other_half_kernel,
        "other_half",
        [((HALF, OUT), wide, False), ((SLOTS, OUT, VOX), narrow, True), ((1, OUT), wide, True)],
        (vmem(kept[2]),) + stacked + (rows,),
    )
    got = lax.ppermute(other, "c", [(0, 1), (1, 0)])
    (mine,) = call(
        own_half_kernel,
        "own_half",
        [((HALF, OUT), wide, False)],
        (vmem(grads),) + stacked,
        flops=2_000_000_000,
    )
    (message,) = call(
        share_kernel, "share", [((BLOCK, 32, 128), narrow, False)], (tags, mine, got, vmem(bias_part), rows)
    )
    pieces = exchange(message, "b")
    (message,) = call(over_block_kernel, "over_block", [((24, 64, 128), narrow, False)], (tags, pieces))
    pieces = exchange(message.reshape(8, 192, 128), "z").reshape(24, 64, 128)
    (message,) = call(over_z_kernel, "over_z", [((ROWS * BLOCK, 128), narrow, False)], (pieces,))
    totals = exchange(message.reshape(BLOCK, ROWS // 2, 2, 128), "b")
    pooled_mine, pooled_other = call(
        pick_kernel, "pick", [((2, CH, 128), narrow, False), ((2, CH, 128), narrow, False)], (pieces,)
    )
    pooled = pooled_mine + lax.ppermute(pooled_other, "c", [(0, 1), (1, 0)])
    pieces = lax.all_gather(totals, "c", tiled=True).reshape(2 * ROWS * BLOCK, 128)
    weight_total, bias_total = call(
        finish_kernel, "finish", [((TAP_ROWS, OUT), wide, False), ((1, OUT), wide, False)], (pieces,)
    )
    return pooled.reshape(2, CH * 128), weight_total.reshape(27, CH, OUT), bias_total.reshape(OUT)


def solution(mesh):
    chips = Mesh(mesh.devices.reshape(-1, 2, BLOCK), ("z", "c", "b"))
    whole = ("z", "c", "b")
    in_specs = (
        P(whole, None, None),
        P(whole),
        P(whole),
        P(whole, None),
        P(whole),
        P(),
        P(),
        P(whole, None),
    )
    out_specs = (P(whole, None), P(), P())
    return jax.shard_map(
        per_device, mesh=chips, in_specs=in_specs, out_specs=out_specs, check_vma=False
    )
```
